32 devices in a mesh: groups: 2 (over y), tp: 4 (over z), batch: 4 (over x, core).
Axes of the slice: x: 2, y: 2, z: 4, core: 2. Of those that a mesh axis runs over, the one named last changes fastest.
Arguments:
- gate_input: bfloat16 [1024, 53248], P(('groups', 'batch'), 'tp'), parts along dimension 0, may hold values from -6 to 6
- up_input: bfloat16 [1024, 53248], P(('groups', 'batch'), 'tp'), parts along dimension 0, may hold values from -6 to 6
- down_weight: bfloat16 [53248, 8192], P('tp', 'batch'), may hold values from -0.02734375 to 0.02734375
Outputs:
- mixed_codes: bfloat16 [1024, 8192], P(('groups', 'batch')), parts along dimension 0
- mixed_scales: bfloat16 [1024, 64], P(('groups', 'batch')), parts along dimension 0
The draws below stay inside these ranges and needn't reach their ends.
There are 2 independent parts, one for each index of `groups`. The reference program is written for one: setup_inputs(seed, part) draws one part's arguments, and reference() takes and returns one part's arrays. A program takes and returns all parts, laid end to end along the dimension named above; an argument that names none is the same for every part. Nothing has to cross between parts.
All inputs are finite; a program needn't handle non-finite values.
Results may differ from the reference program's by a relative error of at most 0.011.
Values may be sent and summed in bfloat16 or wider, within the bound.
No kernel may reach another device: no remote copies, remote signals or barrier semaphores. Data moves between devices by JAX's collectives and lax.ppermute only.
A program may use at most 192 MiB of HBM per device.

```python
import jax
import jax.numpy as jnp
from jax import lax

D = 8192
FF = 53248
BLOCK = 128
TOKENS = 512
N_TP = 4


def raised(result, own_key, source, target, shards_of, factor):
    owner, partner = [(jnp.arange(result.shape[dim]) // (result.shape[dim] // shards_of)).reshape([-1 if axis == dim else 1 for axis in range(result.ndim)]) for dim in (source, target)]
    chosen = jax.random.permutation(own_key, shards_of)[partner]
    strong = (owner == chosen) | (owner == (partner + shards_of // 2) % shards_of)
    return jnp.where(strong, factor * result, result)


def steps_of(own_key, extent, split, low, high):
    level, own = 1.0, jax.random.fold_in(own_key, 6)
    for dim, parts in split:
        steps = jnp.exp(jax.random.uniform(jax.random.fold_in(own, dim), (parts,), jnp.float32, low / len(split), high / len(split)))
        level = level * jnp.repeat(steps, extent[dim] // parts).reshape([-1 if axis == dim else 1 for axis in range(len(extent))])
    return level


def normal_values(own_key, dims, spread, bound, pieces=(), dtype=jnp.bfloat16):
    factor_of = steps_of(own_key, dims, pieces, -0.22, 0.18) if pieces else 1.0
    drawn = jax.random.normal(own_key, dims, jnp.float32) * spread * factor_of
    return jnp.minimum(jnp.maximum(drawn, -bound), bound).astype(dtype)


def bell_draw_with(rng, shape, deviation, reach, cuts, heavy, kind=jnp.bfloat16):
    entries = deviation * jax.random.normal(rng, shape, jnp.float32)
    if cuts:
        entries = entries * steps_of(rng, shape, cuts, -0.22, 0.18)
    return jnp.clip(raised(entries, jax.random.fold_in(rng, 3), *heavy), -reach, reach).astype(kind)


def setup_inputs(seed: int = 0, part: int = 0) -> dict:
    arg_keys = jax.random.split(jax.random.key(seed), 4)
    own_keys = jax.random.split(jax.random.fold_in(arg_keys[3], part), 4)
    gate_input = normal_values(own_keys[0], (TOKENS, FF), 1.0, 6.0, ((0, 4), (1, 4)))
    up_input = bell_draw_with(own_keys[1], (TOKENS, FF), 1.0, 6.0, ((0, 4), (1, 4)), (1, 0, 4, 2.0))
    down_weight = normal_values(arg_keys[2], (FF, D), FF ** -0.5, 0.02734375, ((0, 4), (1, 4)))
    return {"gate_input": gate_input, "up_input": up_input, "down_weight": down_weight}


EPSILON = 1e-6


def encode(values):
    leading = values.shape[:-1]
    blocks = values.reshape(leading + (values.shape[-1] // BLOCK, BLOCK))
    scales = (jnp.max(jnp.abs(blocks), axis=-1) + EPSILON).astype(jnp.bfloat16)
    widened = lax.optimization_barrier(scales).astype(jnp.float32)
    encoded = (blocks / widened[..., None]).astype(jnp.bfloat16)
    return encoded.reshape(values.shape), scales


def decode(encoded, scales):
    blocks = encoded.reshape(scales.shape + (BLOCK,)).astype(jnp.float32)
    return (blocks * scales.astype(jnp.float32)[..., None]).reshape(encoded.shape)


def reference(gate_input, up_input, down_weight):
    hidden = (jax.nn.silu(gate_input.astype(jnp.float32)) * up_input.astype(jnp.float32)).astype(jnp.bfloat16)
    shard_width = FF // N_TP
    hidden_shards = hidden.reshape(TOKENS, N_TP, shard_width).transpose(1, 0, 2)
    weight_shards = down_weight.reshape(N_TP, shard_width, D)

    def add_shard(summed, shard_pair):
        shard_rows, shard_weight = shard_pair
        partial_value = jnp.dot(shard_rows, shard_weight, preferred_element_type=jnp.float32)
        part_codes, part_scales = encode(partial_value)
        return summed + decode(part_codes, part_scales), None

    summed, ignored = lax.scan(add_shard, jnp.zeros((TOKENS, D), jnp.float32), (hidden_shards, weight_shards))
    mixed_codes, mixed_scales = encode(summed)
    return mixed_codes, mixed_scales
```

```python
import functools

import jax
import jax.numpy as jnp
from jax import lax
from jax.experimental import pallas as pl
from jax.experimental.pallas import tpu as pltpu
from jax.sharding import PartitionSpec as P

BLOCK = 128
EPSILON = 1e-06

STEP = 512
CHUNKS = (7, 7, 6, 6)
VMEM = 40 * 2**20


def encode(values):
    leading = values.shape[:-1]
    blocks = values.reshape(leading + (values.shape[-1] // BLOCK, BLOCK))
    scales = (jnp.max(jnp.abs(blocks), axis=-1) + EPSILON).astype(jnp.bfloat16)
    widened = lax.optimization_barrier(scales).astype(jnp.float32)
    encoded = (blocks / widened[..., None]).astype(jnp.bfloat16)
    return (encoded.reshape(values.shape), scales)


def decode(encoded, scales):
    blocks = encoded.reshape(scales.shape + (BLOCK,)).astype(jnp.float32)
    return (blocks * scales.astype(jnp.float32)[..., None]).reshape(encoded.shape)


def general_shards(gate_input, up_input, down_weight):
    hidden = (jax.nn.silu(gate_input.astype(jnp.float32)) * up_input.astype(jnp.float32)).astype(
        jnp.bfloat16
    )
    partial_value = jnp.dot(
        lax.all_gather(hidden, "batch", axis=0, tiled=True),
        down_weight,
        preferred_element_type=jnp.float32,
    )
    part_codes, part_scales = encode(partial_value)
    tp_count = lax.axis_size("tp")
    batch_count = lax.axis_size("batch")
    row_count = hidden.shape[0]
    local_cols = partial_value.shape[1]
    local_blocks = part_scales.shape[1]
    row_share = row_count // tp_count
    got_codes, got_scales = (
        lax.all_to_all(
            part_codes.reshape(batch_count, tp_count, row_share, local_cols),
            "tp",
            split_axis=1,
            concat_axis=1,
            tiled=True,
        ),
        lax.all_to_all(
            part_scales.reshape(batch_count, tp_count, row_share, local_blocks),
            "tp",
            split_axis=1,
            concat_axis=1,
            tiled=True,
        ),
    )
    summed = jnp.sum(decode(got_codes, got_scales), axis=1)
    new_codes, new_scales = encode(summed)
    home_codes, home_scales = (
        lax.all_to_all(new_codes, "batch", split_axis=0, concat_axis=2, tiled=True),
        lax.all_to_all(new_scales, "batch", split_axis=0, concat_axis=2, tiled=True),
    )
    out_codes, out_scales = (
        lax.all_gather(home_codes, "tp", axis=1, tiled=True),
        lax.all_gather(home_scales, "tp", axis=1, tiled=True),
    )
    return (out_codes.reshape(row_count, -1), out_scales.reshape(row_count, -1))


def params(limit=VMEM):
    return pltpu.CompilerParams(vmem_limit_bytes=limit)


ANY = pl.BlockSpec(memory_space=pl.ANY)


def after(value, *earlier):
    def body(*refs):
        pass

    return pl.pallas_call(
        body,
        out_shape=jax.ShapeDtypeStruct(value.shape, value.dtype),
        in_specs=[ANY] * (1 + len(earlier)),
        out_specs=ANY,
        input_output_aliases={0: 0},
        name="after",
    )(value, *earlier)


def activate(gate, up, first, steps, cut):
    rows = gate.shape[0]

    def body(gate_ref, up_ref, all_ref, low_ref, high_ref):
        value = gate_ref[...].astype(jnp.float32)
        value = value / (1.0 + jnp.exp(-value)) * up_ref[...].astype(jnp.float32)
        value = value.astype(jnp.bfloat16)
        all_ref[...] = value
        low_ref[...] = value[:cut]
        high_ref[...] = value[cut:]

    width = steps * STEP
    return pl.pallas_call(
        body,
        grid=(steps,),
        in_specs=[pl.BlockSpec((rows, STEP), lambda k: (0, first + k))] * 2,
        out_specs=[pl.BlockSpec((n, STEP), lambda k: (0, k)) for n in (rows, cut, rows - cut)],
        out_shape=[jax.ShapeDtypeStruct((n, width), jnp.bfloat16) for n in (rows, cut, rows - cut)],
        compiler_params=params(),
        cost_estimate=pl.CostEstimate(
            flops=8 * rows * width, bytes_accessed=8 * rows * width, transcendentals=rows * width
        ),
        name="activate",
    )(gate, up)


def multiply(pieces, weight, first, total, split, final, earlier=()):
    steps = pieces[0].shape[1] // STEP
    counts = [piece.shape[0] for piece in pieces]
    rows, cols = sum(counts), weight.shape[1]
    tile = min(512, cols)
    part = cols // split
    n_pieces, has_total, n_earlier = len(pieces), total is not None, len(earlier)

    def body(*refs):
        piece_refs = refs[:n_pieces]
        weight_ref = refs[n_pieces]
        total_ref = refs[n_pieces + 1] if has_total else None
        out_ref, sums = refs[-2:]
        k = pl.program_id(0)
        left = jnp.concatenate([ref[...] for ref in piece_refs], axis=0)
        for n in range(cols // tile):
            at = pl.ds(n * tile, tile)
            value = jnp.dot(left, weight_ref[:, at], preferred_element_type=jnp.float32)

            @pl.when(k == 0)
            def _():
                sums[:, at] = value + total_ref[:, at] if has_total else value

            @pl.when(k > 0)
            def _():
                sums[:, at] += value

        @pl.when(k == steps - 1)
        def _():
            if not final:
                out_ref[...] = sums[...]
            elif split == 1:
                out_ref[...] = sums[...].astype(jnp.bfloat16)
            else:
                for s in range(split):
                    out_ref[s] = sums[:, s * part : (s + 1) * part].astype(jnp.bfloat16)

    if not final:
        out = jax.ShapeDtypeStruct((rows, cols), jnp.float32)
    elif split == 1:
        out = jax.ShapeDtypeStruct((rows, cols), jnp.bfloat16)
    else:
        out = jax.ShapeDtypeStruct((split, rows, part), jnp.bfloat16)
    whole = pl.BlockSpec((rows, cols), lambda k: (0, 0))
    return pl.pallas_call(
        body,
        grid=(steps,),
        in_specs=[pl.BlockSpec((n, STEP), lambda k: (0, k)) for n in counts]
        + [pl.BlockSpec((STEP, cols), lambda k: (first + k, 0))]
        + ([whole] if has_total else [])
        + [ANY] * n_earlier,
        out_specs=pl.BlockSpec(out.shape, lambda k: (0,) * len(out.shape)),
        out_shape=out,
        scratch_shapes=[pltpu.VMEM((rows, cols), jnp.float32)],
        compiler_params=params(),
        cost_estimate=pl.CostEstimate(
            flops=2 * rows * cols * steps * STEP,
            bytes_accessed=2 * cols * steps * STEP,
            transcendentals=0,
        ),
        name="multiply",
    )(*pieces, weight, *([total] if has_total else []), *earlier)


def encode_blocks(value, code_ref, scale_ref):
    for n in range(value.shape[1] // BLOCK):
        block = value[:, n * BLOCK : (n + 1) * BLOCK]
        scale = (jnp.max(jnp.abs(block), axis=1, keepdims=True) + EPSILON).astype(jnp.bfloat16)
        code_ref[:, n * BLOCK : (n + 1) * BLOCK] = (block / scale.astype(jnp.float32)).astype(
            jnp.bfloat16
        )
        scale_ref[:, n : n + 1] = scale


def encode_near(own, beside, place, width):
    rows, cols = beside.shape
    blocks = cols // BLOCK

    def body(place_ref, own_ref, beside_ref, code_ref, scale_ref):
        @pl.when(pl.program_id(0) == 0)
        def _():
            encode_blocks(own_ref[...].astype(jnp.float32), code_ref, scale_ref)

        @pl.when(pl.program_id(0) == 1)
        def _():
            encode_blocks(beside_ref[...].astype(jnp.float32), code_ref, scale_ref)

    return pl.pallas_call(
        body,
        grid_spec=pltpu.PrefetchScalarGridSpec(
            num_scalar_prefetch=1,
            grid=(2,),
            in_specs=[pl.BlockSpec((rows, cols), lambda j, place: (0, 0))] * 2,
            out_specs=[
                pl.BlockSpec((rows, cols), lambda j, place: (0, place[0] ^ j)),
                pl.BlockSpec((None, rows, blocks), lambda j, place: (j, 0, 0)),
            ],
        ),
        out_shape=[
            jax.ShapeDtypeStruct((rows, width), jnp.bfloat16),
            jax.ShapeDtypeStruct((2, rows, blocks), jnp.bfloat16),
        ],
        compiler_params=params(),
        name="encode_near",
    )(place, own, beside)


def encode_far(codes, shares, place, start):
    tp, _, rows, part = shares.shape
    blocks = part // BLOCK

    def body(place_ref, codes_ref, share_ref, code_ref, scale_ref):
        encode_blocks(share_ref[...].astype(jnp.float32), code_ref, scale_ref)

    return pl.pallas_call(
        body,
        grid_spec=pltpu.PrefetchScalarGridSpec(
            num_scalar_prefetch=1,
            grid=(2, tp),
            in_specs=[
                ANY,
                pl.BlockSpec((None, None, rows, part), lambda j, t, place: (t, j, 0, 0)),
            ],
            out_specs=[
                pl.BlockSpec(
                    (rows, part),
                    lambda j, t, place: (start // rows, (place[0] ^ (j + 2)) * tp + t),
                ),
                pl.BlockSpec((None, None, rows, blocks), lambda j, t, place: (j, t, 0, 0)),
            ],
        ),
        out_shape=[
            jax.ShapeDtypeStruct(codes.shape, codes.dtype),
            jax.ShapeDtypeStruct((2, tp, rows, blocks), jnp.bfloat16),
        ],
        input_output_aliases={1: 0},
        compiler_params=params(),
        name="encode_far",
    )(place, codes, shares)


def swap(value, flip, count):
    return lax.ppermute(value, "batch", [(b, b ^ flip) for b in range(count)])


def paired_shards(gate_input, up_input, down_weight):
    rows, width = gate_input.shape
    cols = down_weight.shape[1]
    tp, batch = lax.axis_size("tp"), lax.axis_size("batch")
    cut = rows * 3 // 4
    place = lax.axis_index("batch").astype(jnp.int32).reshape(1)

    firsts = [sum(CHUNKS[:c]) for c in range(len(CHUNKS))]
    hidden, low, high = zip(
        *[activate(gate_input, up_input, f, n, cut) for f, n in zip(firsts, CHUNKS)]
    )

    got = []
    for piece in low + high:
        if len(got) >= 2:
            piece = after(piece, got[-2])
        got.append(swap(piece, 2, batch))
    beside = [swap(h, 1, batch) for h in hidden]
    got_beside = [swap(g, 1, batch) for g in got]

    near = None
    for c, f in enumerate(firsts):
        last = c == len(firsts) - 1
        near = multiply([hidden[c], beside[c]], down_weight, f, near, 1, last)
    near = lax.psum(near, "tp")
    codes, near_scales = encode_near(near[:rows], swap(near[rows:], 1, batch), place, cols * batch)

    far_scales = []
    for group, start in ((0, 0), (1, cut)):
        far = None
        for c, f in enumerate(firsts):
            last = c == len(firsts) - 1
            i = group * len(firsts) + c
            far = multiply([got[i], got_beside[i]], down_weight, f, far, tp, last)
        share = lax.psum_scatter(far, "tp", scatter_dimension=0)
        n = share.shape[0] // 2
        home = jnp.stack([swap(share[:n], 2, batch), swap(share[n:], 3, batch)])
        shares = lax.all_gather(home, "tp")
        codes, scales = encode_far(codes, shares, place, start)
        far_scales.append(scales.transpose(0, 2, 1, 3).reshape(2, n, -1))
    scales = jnp.concatenate([near_scales, jnp.concatenate(far_scales, axis=1)], axis=0)
    scales = jnp.take(scales, jnp.arange(batch) ^ place, axis=0)
    return codes, scales.transpose(1, 0, 2).reshape(rows, -1)


def solution(mesh):
    def shards(gate_input, up_input, down_weight):
        tp, batch = mesh.shape["tp"], mesh.shape["batch"]
        width, cols = down_weight.shape
        paired = batch == 4 and cols % (tp * BLOCK) == 0 and width == sum(CHUNKS) * STEP
        return (paired_shards if paired else general_shards)(gate_input, up_input, down_weight)

    in_specs = (P(("groups", "batch"), "tp"), P(("groups", "batch"), "tp"), P("tp", "batch"))
    out_specs = (P(("groups", "batch"), None), P(("groups", "batch"), None))
    return jax.shard_map(shards, mesh=mesh, in_specs=in_specs, out_specs=out_specs, check_vma=False)
```

```python
import functools

import jax
import jax.numpy as jnp
from jax import lax
from jax.experimental import pallas as pl
from jax.experimental.pallas import tpu as pltpu
from jax.sharding import PartitionSpec as P

BLOCK = 128
EPSILON = 1e-06

STEP = 1024
CHUNKS = (4, 3, 3, 3)
GROUPS = (3, 1)
TILE = 512
VMEM = 24 * 2**20


def encode(values):
    leading = values.shape[:-1]
    blocks = values.reshape(leading + (values.shape[-1] // BLOCK, BLOCK))
    scales = (jnp.max(jnp.abs(blocks), axis=-1) + EPSILON).astype(jnp.bfloat16)
    widened = lax.optimization_barrier(scales).astype(jnp.float32)
    encoded = (blocks / widened[..., None]).astype(jnp.bfloat16)
    return (encoded.reshape(values.shape), scales)


def decode(encoded, scales):
    blocks = encoded.reshape(scales.shape + (BLOCK,)).astype(jnp.float32)
    return (blocks * scales.astype(jnp.float32)[..., None]).reshape(encoded.shape)


def general_shards(gate_input, up_input, down_weight):
    hidden = (jax.nn.silu(gate_input.astype(jnp.float32)) * up_input.astype(jnp.float32)).astype(
        jnp.bfloat16
    )
    partial_value = jnp.dot(
        lax.all_gather(hidden, "batch", axis=0, tiled=True),
        down_weight,
        preferred_element_type=jnp.float32,
    )
    part_codes, part_scales = encode(partial_value)
    tp_count = lax.axis_size("tp")
    batch_count = lax.axis_size("batch")
    row_count = hidden.shape[0]
    local_cols = partial_value.shape[1]
    local_blocks = part_scales.shape[1]
    row_share = row_count // tp_count
    got_codes, got_scales = (
        lax.all_to_all(
            part_codes.reshape(batch_count, tp_count, row_share, local_cols),
            "tp",
            split_axis=1,
            concat_axis=1,
            tiled=True,
        ),
        lax.all_to_all(
            part_scales.reshape(batch_count, tp_count, row_share, local_blocks),
            "tp",
            split_axis=1,
            concat_axis=1,
            tiled=True,
        ),
    )
    summed = jnp.sum(decode(got_codes, got_scales), axis=1)
    new_codes, new_scales = encode(summed)
    home_codes, home_scales = (
        lax.all_to_all(new_codes, "batch", split_axis=0, concat_axis=2, tiled=True),
        lax.all_to_all(new_scales, "batch", split_axis=0, concat_axis=2, tiled=True),
    )
    out_codes, out_scales = (
        lax.all_gather(home_codes, "tp", axis=1, tiled=True),
        lax.all_gather(home_scales, "tp", axis=1, tiled=True),
    )
    return (out_codes.reshape(row_count, -1), out_scales.reshape(row_count, -1))


ANY = pl.BlockSpec(memory_space=pl.ANY)
SMALL = pl.CostEstimate(flops=1024, bytes_accessed=1024, transcendentals=0)


TOKEN = (8, 128)


def large(value):
    return value.size * value.dtype.itemsize > 3 * 2**20


class Chain:
    def __init__(self):
        self.tokens = []

    def call(self, body, operands, in_specs, out_specs, out_shape, name, grid=(), scratch=(), aliases=None):
        count, n_tokens, n_outs = len(operands), len(self.tokens), len(out_shape)

        def with_tokens(*refs):
            outs = count + n_tokens
            body(*refs[:count], *refs[outs : outs + n_outs], *refs[outs + n_outs + 1 :])

        operands = [
            pltpu.with_memory_space_constraint(value, pltpu.HBM) if large(value) else value
            for value in operands
        ]
        outs = pl.pallas_call(
            with_tokens,
            grid=grid,
            in_specs=list(in_specs) + [ANY] * n_tokens,
            out_specs=list(out_specs) + [ANY],
            out_shape=list(out_shape) + [jax.ShapeDtypeStruct(TOKEN, jnp.float32)],
            scratch_shapes=scratch,
            input_output_aliases=aliases or {},
            compiler_params=pltpu.CompilerParams(vmem_limit_bytes=VMEM),
            cost_estimate=SMALL,
            name=name,
        )(*operands, *self.tokens)
        self.tokens = [outs[-1]]
        return outs[:-1]

    def pin(self, value):
        pinned = self.call(
            lambda *refs: None,
            [value],
            [ANY],
            [ANY],
            [jax.ShapeDtypeStruct(value.shape, value.dtype)],
            "pin",
            aliases={0: 0},
        )
        return pinned[0]


def activate(chain, gate, up, first, steps, cuts):
    rows = gate.shape[0]
    counts = [rows] + [b - a for a, b in zip(cuts, cuts[1:])]

    def body(gate_ref, up_ref, all_ref, *group_refs):
        value = gate_ref[...].astype(jnp.float32)
        value = value / (1.0 + jnp.exp(-value)) * up_ref[...].astype(jnp.float32)
        value = value.astype(jnp.bfloat16)
        all_ref[...] = value
        for ref, a, b in zip(group_refs, cuts, cuts[1:]):
            ref[...] = value[a:b]

    return chain.call(
        body,
        [gate, up],
        [pl.BlockSpec((rows, STEP), lambda k: (0, first + k))] * 2,
        [pl.BlockSpec((n, STEP), lambda k: (0, k)) for n in counts],
        [jax.ShapeDtypeStruct((n, steps * STEP), jnp.bfloat16) for n in counts],
        "activate",
        grid=(steps,),
    )


def multiply(chain, chunks, weight, first, total, place, split):
    steps = [pieces[0].shape[1] // STEP for pieces in chunks]
    starts = [sum(steps[:c]) for c in range(len(steps))]
    counts = [piece.shape[0] for piece in chunks[0]]
    rows, cols = sum(counts), weight.shape[1]
    tiles, part = cols // TILE, cols // max(split, 1)
    flat = [piece for pieces in chunks for piece in pieces]
    n_total = 0 if total is None else 1

    def body(place_ref, *refs):
        piece_refs, refs = refs[: len(flat)], refs[len(flat) :]
        weight_refs, refs = refs[:tiles], refs[tiles:]
        total_refs, refs = refs[:n_total], refs[n_total:]
        outs, (left, *sums) = refs[: max(split, 1)], refs[max(split, 1) :]
        sums = sums[0] if sums else outs[0]
        k = pl.program_id(0)

        @pl.when(k == 0)
        def _():
            sums[...] = total_refs[0][...] if n_total else jnp.zeros(sums.shape, sums.dtype)

        for c, n in enumerate(steps):

            @pl.when((k >= starts[c]) & (k < starts[c] + n))
            def _():
                at = 0
                for ref in piece_refs[c * len(counts) : (c + 1) * len(counts)]:
                    left[at : at + ref.shape[0]] = ref[...]
                    at += ref.shape[0]

        for n in range(tiles):
            sums[:, n * TILE : (n + 1) * TILE] += jnp.dot(
                left[...], weight_refs[n][...], preferred_element_type=jnp.float32
            )

        if split:

            @pl.when(k == sum(steps) - 1)
            def _():
                for o in range(split):
                    at = lax.rem(place_ref[0] + o, split) * part
                    outs[o][...] = sums[:, pl.ds(pl.multiple_of(at, part), part)].astype(jnp.bfloat16)

    def piece_spec(c, n):
        return pl.BlockSpec((n, STEP), lambda k: (0, jnp.clip(k - starts[c], 0, steps[c] - 1)))

    def weight_spec(n):
        return pl.BlockSpec((STEP, TILE), lambda k: (first + k, n))

    whole = pl.BlockSpec((rows, cols), lambda k: (0, 0))
    return chain.call(
        body,
        [place] + flat + [weight] * tiles + ([total] if n_total else []),
        [pl.BlockSpec(memory_space=pltpu.SMEM)]
        + [piece_spec(c, n) for c in range(len(chunks)) for n in counts]
        + [weight_spec(n) for n in range(tiles)]
        + [whole] * n_total,
        [pl.BlockSpec((rows, part), lambda k: (0, 0))] * max(split, 1),
        [jax.ShapeDtypeStruct((rows, part), jnp.bfloat16 if split else jnp.float32)] * max(split, 1),
        "multiply",
        grid=(sum(steps),),
        scratch=[pltpu.VMEM((rows, STEP), jnp.bfloat16)]
        + ([pltpu.VMEM((rows, cols), jnp.float32)] if split else []),
    )


def add_parts(chain, parts):
    rows, cols = parts[0].shape
    half = rows // 2

    def body(*refs):
        value = sum(ref[...].astype(jnp.float32) for ref in refs[:-2]).astype(jnp.bfloat16)
        refs[-2][...] = value[:half]
        refs[-1][...] = value[half:]

    return chain.call(
        body,
        parts,
        [pl.BlockSpec((rows, cols), lambda k: (0, 0))] * len(parts),
        [pl.BlockSpec((half, cols), lambda k: (0, 0))] * 2,
        [jax.ShapeDtypeStruct((half, cols), jnp.bfloat16)] * 2,
        "add_parts",
        grid=(1,),
    )


def encode_blocks(value, store, scales, first):
    lanes = lax.broadcasted_iota(jnp.int32, scales.shape, 1)
    for n in range(value.shape[1] // BLOCK):
        block = value[:, n * BLOCK : (n + 1) * BLOCK].astype(jnp.float32)
        scale = (jnp.max(jnp.abs(block), axis=1, keepdims=True) + EPSILON).astype(jnp.bfloat16)
        scale = scale.astype(jnp.float32)
        store(n, (block / scale).astype(jnp.bfloat16))
        scales = jnp.where(lanes == first + n, scale, scales)
    return scales


def encode_near(chain, own, beside, place, rows, batch):
    cols = own.shape[1]
    blocks = cols // BLOCK

    def body(place_ref, own_ref, beside_ref, code_ref, scale_ref):
        j = pl.program_id(0)

        def store(n, codes):
            code_ref[:, n * BLOCK : (n + 1) * BLOCK] = codes

        first = (place_ref[0] ^ j) * blocks

        @pl.when(j == 0)
        def _():
            scales = jnp.zeros(scale_ref.shape, jnp.float32)
            scale_ref[...] = encode_blocks(own_ref[...], store, scales, first).astype(jnp.bfloat16)

        @pl.when(j == 1)
        def _():
            scales = scale_ref[...].astype(jnp.float32)
            scale_ref[...] = encode_blocks(beside_ref[...], store, scales, first).astype(jnp.bfloat16)

    return chain.call(
        body,
        [place, own, beside],
        [
            pl.BlockSpec(memory_space=pltpu.SMEM),
            pl.BlockSpec((rows, cols), lambda j: (0, 0)),
            pl.BlockSpec((rows, cols), lambda j: (1, 0)),
        ],
        [
            pl.BlockSpec((rows, cols), lambda j: (0, lax.axis_index("batch") ^ j)),
            pl.BlockSpec((rows, batch * blocks), lambda j: (0, 0)),
        ],
        [
            jax.ShapeDtypeStruct((rows, batch * cols), jnp.bfloat16),
            jax.ShapeDtypeStruct((rows, batch * blocks), jnp.bfloat16),
        ],
        "encode_near",
        grid=(2,),
    )


def encode_far(chain, codes, scales, shares, place, spot, start):
    _, rows, part = shares[0].shape
    tp = len(shares)
    blocks = part // BLOCK
    width = scales.shape[1]

    def body(place_ref, spot_ref, codes_in, scales_in, *refs):
        share_refs, (code_ref, scale_ref) = refs[:tp], refs[tp:]
        j = pl.program_id(0)

        @pl.when(j == 0)
        def _():
            scale_ref[...] = scales_in[...]

        total = scale_ref[...].astype(jnp.float32)
        for o in range(tp):
            t = lax.rem(spot_ref[0] + tp - o, tp)

            def store(n, value, t=t):
                code_ref[:, pl.ds(pl.multiple_of((t * blocks + n) * BLOCK, BLOCK), BLOCK)] = value

            first = ((place_ref[0] ^ (j + 2)) * tp + t) * blocks
            total = encode_blocks(share_refs[o][...], store, total, first)
        scale_ref[...] = total.astype(jnp.bfloat16)

    smem = pl.BlockSpec(memory_space=pltpu.SMEM)
    group = pl.BlockSpec((rows, width), lambda j: (start // rows, 0))
    return chain.call(
        body,
        [place, spot, codes, scales, *shares],
        [smem, smem, ANY, group] + [pl.BlockSpec((None, rows, part), lambda j: (j, 0, 0))] * tp,
        [
            pl.BlockSpec((rows, tp * part), lambda j: (start // rows, lax.axis_index("batch") ^ (j + 2))),
            group,
        ],
        [
            jax.ShapeDtypeStruct(codes.shape, codes.dtype),
            jax.ShapeDtypeStruct(scales.shape, scales.dtype),
        ],
        "encode_far",
        grid=(2,),
        aliases={2: 0, 3: 1},
    )


def paired_shards(gate_input, up_input, down_weight):
    rows = gate_input.shape[0]
    tp, batch = lax.axis_size("tp"), lax.axis_size("batch")
    place = lax.axis_index("batch").astype(jnp.int32).reshape(1)
    spot = lax.axis_index("tp").astype(jnp.int32).reshape(1)
    zero = jnp.zeros(1, jnp.int32)
    quarter = rows // sum(GROUPS)
    cuts = [sum(GROUPS[:g]) * quarter for g in range(len(GROUPS) + 1)]
    firsts = [sum(CHUNKS[:c]) for c in range(len(CHUNKS))]
    n_chunks = len(CHUNKS)
    chain = Chain()

    def swap(value, flip):
        return lax.ppermute(value, "batch", [(b, b ^ flip) for b in range(batch)])

    def shift(value, o):
        return lax.ppermute(value, "tp", [(t, (t + o) % tp) for t in range(tp)])

    hidden, beside, pieces, got = [], [], [[] for _ in GROUPS], []
    for first, steps in zip(firsts, CHUNKS):
        whole, *parts = activate(chain, gate_input, up_input, first, steps, cuts)
        for group, part in zip(pieces, parts):
            group.append(part)
        hidden.append(whole)
        beside.append(swap(whole, 1))
    queue = [piece for group in pieces for piece in group]
    for _ in range(3):
        got.append(swap(queue.pop(0), 2))

    def arrive(i):
        got[i] = chain.pin(got[i])
        if queue:
            got.append(swap(chain.pin(queue.pop(0)), 2))
        got[i] = [got[i], swap(got[i], 1)]

    def spread(parts):
        parts = [parts[0]] + [shift(parts[o], o) for o in range(1, tp)]

        def home():
            ahead, behind = add_parts(chain, parts)
            ahead, behind = swap(ahead, 2), swap(behind, 3)

            def everywhere():
                both = chain.pin(jnp.stack([ahead, behind]))
                return [both] + [shift(both, o) for o in range(1, tp)]

            return everywhere

        return home

    near = None
    for c in range(0, n_chunks, 2):
        last = c + 2 >= n_chunks
        near = multiply(
            chain,
            [[hidden[i], beside[i]] for i in (c, c + 1)],
            down_weight,
            firsts[c],
            near,
            zero,
            1 if last else 0,
        )[0]
        arrive(c // 2)
    near = lax.psum(near, "tp")

    def far_product(group, c, total):
        last = c == n_chunks - 1
        pieces = got[group * n_chunks + c]
        outs = multiply(
            chain, [pieces], down_weight, firsts[c], total, spot, tp if last else 0
        )
        return outs if last else outs[0]

    total = None
    for c in range(n_chunks):
        total = far_product(0, c, total)
        if c + 2 < len(got):
            arrive(c + 2)
    home_0 = spread(total)
    total = far_product(1, 0, None)
    arrive(n_chunks + 2)
    total = far_product(1, 1, total)
    all_0 = home_0()
    arrive(n_chunks + 3)
    total = far_product(1, 2, total)
    shares_0 = all_0()
    near = chain.pin(near)
    near_beside = swap(near, 1)
    total = far_product(1, 3, total)
    home_1 = spread(total)
    codes, scales = encode_near(chain, near, near_beside, place, rows, batch)
    all_1 = home_1()
    codes, scales = encode_far(chain, codes, scales, shares_0, place, spot, cuts[0])
    shares_1 = all_1()
    codes, scales = encode_far(chain, codes, scales, shares_1, place, spot, cuts[1])
    return codes, scales


def solution(mesh):
    def shards(gate_input, up_input, down_weight):
        tp, batch = mesh.shape["tp"], mesh.shape["batch"]
        width, cols = down_weight.shape
        paired = batch == 4 and cols % (tp * TILE) == 0 and width == sum(CHUNKS) * STEP
        return (paired_shards if paired else general_shards)(gate_input, up_input, down_weight)

    in_specs = (P(("groups", "batch"), "tp"), P(("groups", "batch"), "tp"), P("tp", "batch"))
    out_specs = (P(("groups", "batch"), None), P(("groups", "batch"), None))
    return jax.shard_map(shards, mesh=mesh, in_specs=in_specs, out_specs=out_specs, check_vma=False)
```

```python
import functools

import jax
import jax.numpy as jnp
from jax import lax
from jax.experimental import pallas as pl
from jax.experimental.pallas import tpu as pltpu
from jax.sharding import PartitionSpec as P

BLOCK = 128
EPSILON = 1e-06

STEP = 1024
FIRST = 1
PIECE = 4
DEPTH = 512
SLOTS = 6
TILE = 512
EARLY = 5
VMEM = 32 * 2**20


def encode(values):
    leading = values.shape[:-1]
    blocks = values.reshape(leading + (values.shape[-1] // BLOCK, BLOCK))
    scales = (jnp.max(jnp.abs(blocks), axis=-1) + EPSILON).astype(jnp.bfloat16)
    widened = lax.optimization_barrier(scales).astype(jnp.float32)
    encoded = (blocks / widened[..., None]).astype(jnp.bfloat16)
    return (encoded.reshape(values.shape), scales)


def decode(encoded, scales):
    blocks = encoded.reshape(scales.shape + (BLOCK,)).astype(jnp.float32)
    return (blocks * scales.astype(jnp.float32)[..., None]).reshape(encoded.shape)


def general_shards(gate_input, up_input, down_weight):
    hidden = (jax.nn.silu(gate_input.astype(jnp.float32)) * up_input.astype(jnp.float32)).astype(
        jnp.bfloat16
    )
    partial_value = jnp.dot(
        lax.all_gather(hidden, "batch", axis=0, tiled=True),
        down_weight,
        preferred_element_type=jnp.float32,
    )
    part_codes, part_scales = encode(partial_value)
    tp_count = lax.axis_size("tp")
    batch_count = lax.axis_size("batch")
    row_count = hidden.shape[0]
    local_cols = partial_value.shape[1]
    local_blocks = part_scales.shape[1]
    row_share = row_count // tp_count
    got_codes, got_scales = (
        lax.all_to_all(
            part_codes.reshape(batch_count, tp_count, row_share, local_cols),
            "tp",
            split_axis=1,
            concat_axis=1,
            tiled=True,
        ),
        lax.all_to_all(
            part_scales.reshape(batch_count, tp_count, row_share, local_blocks),
            "tp",
            split_axis=1,
            concat_axis=1,
            tiled=True,
        ),
    )
    summed = jnp.sum(decode(got_codes, got_scales), axis=1)
    new_codes, new_scales = encode(summed)
    home_codes, home_scales = (
        lax.all_to_all(new_codes, "batch", split_axis=0, concat_axis=2, tiled=True),
        lax.all_to_all(new_scales, "batch", split_axis=0, concat_axis=2, tiled=True),
    )
    out_codes, out_scales = (
        lax.all_gather(home_codes, "tp", axis=1, tiled=True),
        lax.all_gather(home_scales, "tp", axis=1, tiled=True),
    )
    return (out_codes.reshape(row_count, -1), out_scales.reshape(row_count, -1))


ANY = pl.BlockSpec(memory_space=pl.ANY)
COST = pl.CostEstimate(flops=10**10, bytes_accessed=10**7, transcendentals=0)


TOKEN = (8, 128)


def large(value):
    return value.size * value.dtype.itemsize > 3 * 2**20


class Chain:
    def __init__(self):
        self.tokens = []

    def call(self, body, operands, in_specs, out_specs, out_shape, name, grid=(), scratch=(), aliases=None):
        count, n_tokens, n_outs = len(operands), len(self.tokens), len(out_shape)

        def with_tokens(*refs):
            outs = count + n_tokens
            body(*refs[:count], *refs[outs : outs + n_outs], *refs[outs + n_outs + 1 :])

        operands = [
            pltpu.with_memory_space_constraint(value, pltpu.HBM) if large(value) else value
            for value in operands
        ]
        outs = pl.pallas_call(
            with_tokens,
            grid=grid,
            in_specs=list(in_specs) + [ANY] * n_tokens,
            out_specs=list(out_specs) + [ANY],
            out_shape=list(out_shape) + [jax.ShapeDtypeStruct(TOKEN, jnp.float32)],
            scratch_shapes=scratch,
            input_output_aliases=aliases or {},
            compiler_params=pltpu.CompilerParams(vmem_limit_bytes=VMEM),
            cost_estimate=COST,
            name=name,
        )(*operands, *self.tokens)
        self.tokens = [outs[-1]]
        return list(outs[:-1])

    def pin(self, value):
        pinned = self.call(
            lambda *refs: None,
            [value],
            [ANY],
            [ANY],
            [jax.ShapeDtypeStruct(value.shape, value.dtype)],
            "pin",
            aliases={0: 0},
        )
        return pinned[0]


def activate(chain, gate, up, first, steps, parts):
    rows = gate.shape[0]

    def body(gate_ref, up_ref, *refs):
        outs, (gates, ups, hidden, in_sems, out_sems) = refs[: len(parts)], refs[len(parts) :]

        def fetch(k, source, target, side):
            at = pl.ds((first + k) * STEP, STEP)
            return pltpu.make_async_copy(source.at[:, at], target.at[k], in_sems.at[side, k])

        for k in range(steps):
            fetch(k, gate_ref, gates, 0).start()
            fetch(k, up_ref, ups, 1).start()
        sent = []
        for k in range(steps):
            fetch(k, gate_ref, gates, 0).wait()
            fetch(k, up_ref, ups, 1).wait()
            value = gates[k].astype(jnp.float32)
            value = value / (1.0 + jnp.exp(-value)) * ups[k].astype(jnp.float32)
            hidden[k] = value.astype(jnp.bfloat16)
            for p, (a, b, s, e) in enumerate(parts):
                if s <= first + k < e:
                    copy = pltpu.make_async_copy(
                        hidden.at[k, pl.ds(a, b - a)],
                        outs[p].at[:, pl.ds((first + k - s) * STEP, STEP)],
                        out_sems.at[p, k],
                    )
                    copy.start()
                    sent.append(copy)
        for copy in sent:
            copy.wait()

    buffer = pltpu.VMEM((steps, rows, STEP), jnp.bfloat16)
    return chain.call(
        body,
        [gate, up],
        [ANY] * 2,
        [ANY] * len(parts),
        [jax.ShapeDtypeStruct((b - a, (e - s) * STEP), jnp.bfloat16) for a, b, s, e in parts],
        "activate",
        scratch=[buffer] * 3
        + [pltpu.SemaphoreType.DMA((2, steps)), pltpu.SemaphoreType.DMA((len(parts), steps))],
    )


def multiply(chain, chunks, weight, first, total, split):
    counts = [piece.shape[0] for piece in chunks[0]]
    rows, cols = sum(counts), weight.shape[1]
    width = sum(pieces[0].shape[1] for pieces in chunks)
    steps, part = width // DEPTH, cols // sum(map(len, split or [(0,)]))
    flat, col = [], 0
    for pieces in chunks:
        row = 0
        for piece in pieces:
            flat.append((piece, row, col))
            row += piece.shape[0]
        col += pieces[0].shape[1]
    n_total = 0 if total is None else 1
    n_in = len(flat) + 1 + n_total
    shapes = [jax.ShapeDtypeStruct((len(flips), rows, part), jnp.bfloat16) for flips in split]
    if not split:
        shapes = [jax.ShapeDtypeStruct((rows, cols), jnp.float32)]

    def body(*refs):
        piece_refs, weight_ref = refs[: len(flat)], refs[len(flat)]
        total_refs, refs = refs[len(flat) + 1 : n_in], refs[n_in:]
        outs, (left, slots, *sums, sems, piece_sems) = refs[: len(shapes)], refs[len(shapes) :]
        sums = sums[0] if sums else outs[0]

        def fetch(k, slot):
            return pltpu.make_async_copy(
                weight_ref.at[pl.ds(first * STEP + k * DEPTH, DEPTH)], slots.at[slot], sems.at[slot]
            )

        for k in range(min(SLOTS, steps)):
            fetch(k, k).start()
        copies = [
            pltpu.make_async_copy(
                ref,
                left.at[pl.ds(row, piece.shape[0]), pl.ds(col, piece.shape[1])],
                piece_sems.at[n],
            )
            for n, (ref, (piece, row, col)) in enumerate(zip(piece_refs, flat))
        ]
        if n_total:
            copies.append(pltpu.make_async_copy(total_refs[0], sums, piece_sems.at[len(flat)]))
        for copy in copies:
            copy.start()
        if not n_total:
            sums[...] = jnp.zeros(sums.shape, sums.dtype)
        for copy in copies:
            copy.wait()

        def step(k, carry):
            slot = lax.rem(k, SLOTS)
            fetch(k, slot).wait()
            piece = left[:, pl.ds(pl.multiple_of(k * DEPTH, DEPTH), DEPTH)]
            for n in range(cols // TILE):
                at = pl.ds(n * TILE, TILE)
                sums[:, at] += jnp.dot(piece, slots[slot, :, at], preferred_element_type=jnp.float32)

            @pl.when(k + SLOTS < steps)
            def _():
                fetch(k + SLOTS, slot).start()

            return carry

        lax.fori_loop(0, steps, step, 0)
        for out, flips in zip(outs, split):
            for n, flip in enumerate(flips):
                at = pl.ds(pl.multiple_of((lax.axis_index("tp") ^ flip) * part, part), part)
                out[n] = sums[:, at].astype(jnp.bfloat16)

    return chain.call(
        body,
        [piece for piece, _, _ in flat] + [weight] + ([total] if n_total else []),
        [ANY] * n_in,
        [pl.BlockSpec(memory_space=pltpu.VMEM)] * len(shapes),
        shapes,
        "multiply",
        scratch=[pltpu.VMEM((rows, width), jnp.bfloat16), pltpu.VMEM((SLOTS, DEPTH, cols), jnp.bfloat16)]
        + ([pltpu.VMEM((rows, cols), jnp.float32)] if split else [])
        + [pltpu.SemaphoreType.DMA((SLOTS,)), pltpu.SemaphoreType.DMA((len(flat) + 1,))],
    )


def add(chain, parts, outs):
    count = len(parts)

    def body(*refs):
        value = sum(ref[...].astype(jnp.float32) for ref in refs[:count]).astype(jnp.bfloat16)
        for ref, (n, a, b) in zip(refs[count:], outs):
            ref[0] = value[n, a:b]

    vmem = pl.BlockSpec(memory_space=pltpu.VMEM)
    shapes = [jax.ShapeDtypeStruct((1, b - a, parts[0].shape[2]), jnp.bfloat16) for _, a, b in outs]
    return chain.call(body, parts, [vmem] * count, [vmem] * len(outs), shapes, "add")


def join(chain, first, second):
    n = first.shape[0]

    def body(first_ref, second_ref, out_ref):
        out_ref[:n] = first_ref[...]
        out_ref[n:] = second_ref[...]

    vmem = pl.BlockSpec(memory_space=pltpu.VMEM)
    shape = jax.ShapeDtypeStruct((n + second.shape[0],) + first.shape[1:], first.dtype)
    return chain.call(body, [first, second], [vmem] * 2, [vmem], [shape], "join")[0]


def encode_blocks(value, store, scales, first):
    lanes = lax.broadcasted_iota(jnp.int32, scales.shape, 1)
    for n in range(value.shape[1] // BLOCK):
        block = value[:, n * BLOCK : (n + 1) * BLOCK].astype(jnp.float32)
        scale = (jnp.max(jnp.abs(block), axis=1, keepdims=True) + EPSILON).astype(jnp.bfloat16)
        scale = scale.astype(jnp.float32)
        store(n, (block / scale).astype(jnp.bfloat16))
        scales = jnp.where(lanes == first + n, scale, scales)
    return scales


def encode_columns(chain, codes, scales, shares, away, start, width):
    rows, part = shares[0][0].shape[1:]
    tp = len(shares)
    blocks = part // BLOCK
    at = slice(start, start + rows)
    height = start + rows if codes is None else codes.shape[0]
    given = [] if codes is None else [codes, scales]

    def body(*refs):
        share_refs = refs[len(given) : len(given) + tp]
        code_ref, scale_ref = refs[len(given) + tp :]
        j = pl.program_id(0)

        @pl.when(j == 0)
        def _():
            scale_ref[...] = refs[1][...] if given else jnp.zeros(scale_ref.shape, scale_ref.dtype)

        if given:
            code_ref[...] = refs[0][...]
        total = scale_ref[at].astype(jnp.float32)
        for flip in range(tp):
            t = lax.axis_index("tp") ^ flip

            def store(n, value, t=t):
                code_ref[at, pl.ds(pl.multiple_of((t * blocks + n) * BLOCK, BLOCK), BLOCK)] = value

            first = ((lax.axis_index("batch") ^ (j + away)) * tp + t) * blocks
            total = encode_blocks(share_refs[flip][...], store, total, first)
        scale_ref[at] = total.astype(jnp.bfloat16)

    whole = pl.BlockSpec((height, width // BLOCK), lambda j: (0, 0))
    columns = pl.BlockSpec((height, tp * part), lambda j: (0, lax.axis_index("batch") ^ (j + away)))

    def share_spec(n):
        return pl.BlockSpec((None, rows, part), lambda j: (n + j, 0, 0))

    return chain.call(
        body,
        given + [array for array, _ in shares],
        [columns, whole][: len(given)] + [share_spec(n) for _, n in shares],
        [columns, whole],
        [
            jax.ShapeDtypeStruct((height, width), jnp.bfloat16),
            jax.ShapeDtypeStruct((height, width // BLOCK), jnp.bfloat16),
        ],
        "encode",
        grid=(2,),
        aliases={0: 0, 1: 1} if given else {},
    )


DIRECT = [(0,), (1,), (2,), (3,)]
HALVES = [(0, 2), (1, 3)]


def paired_shards(gate_input, up_input, down_weight):
    rows, width = gate_input.shape
    tp, batch = lax.axis_size("tp"), lax.axis_size("batch")
    out_width = down_weight.shape[1] * batch
    cut = rows * EARLY // 8
    ends = [FIRST, FIRST + PIECE, FIRST + 2 * PIECE, FIRST + 3 * PIECE]
    spans = list(zip([0] + ends, ends))
    chain = Chain()

    def swap(value, flip):
        return lax.ppermute(value, "batch", [(b, b ^ flip) for b in range(batch)]) if flip else value

    def shift(value, flip):
        return lax.ppermute(value, "tp", [(t, t ^ flip) for t in range(tp)])

    def both_cores(piece):
        piece = chain.pin(piece)
        return [piece, swap(piece, 1)]

    def product(chunks, first, total, split=()):
        outs = multiply(chain, chunks, down_weight, first, total, split)
        return outs if split else outs[0]

    def sum_home(parts, away):
        half = parts[0].shape[1] // 2
        ahead, behind = add(chain, parts, [(0, 0, half), (0, half, 2 * half)])
        return swap(ahead, away), swap(behind, away + 1)

    def sum_pair(parts):
        keep, got = parts
        total = add(chain, [keep, got], [(0, 0, keep.shape[1]), (1, 0, keep.shape[1])])
        return [total[0], shift(total[1], 2)]

    near_0, send_0 = activate(
        chain, gate_input, up_input, 0, FIRST, [(0, rows, 0, FIRST), (0, cut, 0, FIRST)]
    )
    far_0 = swap(send_0, 2)
    pieces = activate(
        chain,
        gate_input,
        up_input,
        0,
        width // STEP,
        [(0, rows, a, b) for a, b in spans[1:]]
        + [(0, cut, a, b) for a, b in spans[1:]]
        + [(cut, rows, a, b) for a, b in [(0, ends[1])] + spans[2:]],
    )
    near, early, late = [near_0] + pieces[:3], pieces[3:6], pieces[6:]
    near = [[h, swap(h, 1)] for h in near]
    far_0 = both_cores(far_0)
    far_1, far_2 = swap(early[0], 2), swap(early[1], 2)

    total = product(near[:2], 0, None)
    near = product(near[2:], ends[1], total, HALVES)
    near = [near[0], shift(near[1], 1)]

    far_1 = both_cores(far_1)
    far_3 = swap(chain.pin(early[2]), 2)
    total = product([far_0, far_1], 0, None)
    far_2 = both_cores(far_2)
    late_0 = swap(chain.pin(late[0]), 2)
    near = sum_pair(near)
    total = product([far_2], ends[1], total)
    far_3 = both_cores(far_3)
    late_1 = swap(chain.pin(late[1]), 2)
    far = product([far_3], ends[2], total, HALVES)
    far = [far[0], shift(far[1], 1)]
    near = sum_home(near, 0)

    late_0 = both_cores(late_0)
    late_2 = swap(chain.pin(late[2]), 2)
    near = join(chain, *near)
    near = [near, shift(near, 2)]
    total = product([late_0], 0, None)
    far = sum_pair(far)
    late_1 = both_cores(late_1)
    total = product([late_1], ends[1], total)
    near.append(join(chain, *near))
    near[2] = shift(near[2], 1)
    far = sum_home(far, 2)
    late_2 = both_cores(late_2)
    parts = product([late_2], ends[2], total, DIRECT)
    parts = [parts[0]] + [shift(parts[flip], flip) for flip in range(1, tp)]
    far = join(chain, *far)
    far = [far] + [shift(far, flip) for flip in range(1, tp)]
    near = [(near[0], 0), (near[2], 0), (near[1], 0), (near[2], 2)]
    codes, scales = encode_columns(chain, None, None, near, 0, 0, out_width)
    last = sum_home(parts, 2)
    last = join(chain, *last)
    last = [last] + [shift(last, flip) for flip in range(1, tp)]
    far, last = [(array, 0) for array in far], [(array, 0) for array in last]
    codes, scales = encode_columns(chain, codes, scales, far, 2, 0, out_width)
    codes, scales = encode_columns(chain, codes, scales, last, 2, cut, out_width)
    return codes, scales


def solution(mesh):
    def shards(gate_input, up_input, down_weight):
        tp, batch = mesh.shape["tp"], mesh.shape["batch"]
        width, cols = down_weight.shape
        paired = batch == tp == 4 and cols % (tp * TILE) == 0 and width == (FIRST + 3 * PIECE) * STEP
        return (paired_shards if paired else general_shards)(gate_input, up_input, down_weight)

    in_specs = (P(("groups", "batch"), "tp"), P(("groups", "batch"), "tp"), P("tp", "batch"))
    out_specs = (P(("groups", "batch"), None), P(("groups", "batch"), None))
    return jax.shard_map(shards, mesh=mesh, in_specs=in_specs, out_specs=out_specs, check_vma=False)
```

```python
import functools

import jax
import jax.numpy as jnp
from jax import lax
from jax.experimental import pallas as pl
from jax.experimental.pallas import tpu as pltpu
from jax.sharding import PartitionSpec as P

BLOCK = 128
EPSILON = 1e-06

STEP = 1024
FIRST = 1
PIECE = 4
DEPTH = 512
SLOTS = 6
TILE = 512
EARLY = 5
VMEM = 32 * 2**20


def encode(values):
    leading = values.shape[:-1]
    blocks = values.reshape(leading + (values.shape[-1] // BLOCK, BLOCK))
    scales = (jnp.max(jnp.abs(blocks), axis=-1) + EPSILON).astype(jnp.bfloat16)
    widened = lax.optimization_barrier(scales).astype(jnp.float32)
    encoded = (blocks / widened[..., None]).astype(jnp.bfloat16)
    return (encoded.reshape(values.shape), scales)


def decode(encoded, scales):
    blocks = encoded.reshape(scales.shape + (BLOCK,)).astype(jnp.float32)
    return (blocks * scales.astype(jnp.float32)[..., None]).reshape(encoded.shape)


def general_shards(gate_input, up_input, down_weight):
    hidden = (jax.nn.silu(gate_input.astype(jnp.float32)) * up_input.astype(jnp.float32)).astype(
        jnp.bfloat16
    )
    partial_value = jnp.dot(
        lax.all_gather(hidden, "batch", axis=0, tiled=True),
        down_weight,
        preferred_element_type=jnp.float32,
    )
    part_codes, part_scales = encode(partial_value)
    tp_count = lax.axis_size("tp")
    batch_count = lax.axis_size("batch")
    row_count = hidden.shape[0]
    local_cols = partial_value.shape[1]
    local_blocks = part_scales.shape[1]
    row_share = row_count // tp_count
    got_codes, got_scales = (
        lax.all_to_all(
            part_codes.reshape(batch_count, tp_count, row_share, local_cols),
            "tp",
            split_axis=1,
            concat_axis=1,
            tiled=True,
        ),
        lax.all_to_all(
            part_scales.reshape(batch_count, tp_count, row_share, local_blocks),
            "tp",
            split_axis=1,
            concat_axis=1,
            tiled=True,
        ),
    )
    summed = jnp.sum(decode(got_codes, got_scales), axis=1)
    new_codes, new_scales = encode(summed)
    home_codes, home_scales = (
        lax.all_to_all(new_codes, "batch", split_axis=0, concat_axis=2, tiled=True),
        lax.all_to_all(new_scales, "batch", split_axis=0, concat_axis=2, tiled=True),
    )
    out_codes, out_scales = (
        lax.all_gather(home_codes, "tp", axis=1, tiled=True),
        lax.all_gather(home_scales, "tp", axis=1, tiled=True),
    )
    return (out_codes.reshape(row_count, -1), out_scales.reshape(row_count, -1))


ANY = pl.BlockSpec(memory_space=pl.ANY)
WEIGHTS = {"activate": 10**10, "multiply": 10**10, "pin": 10**10, "add": 0, "join": 0, "encode": 0}


TOKEN = (8, 128)


def large(value):
    return value.size * value.dtype.itemsize > 3 * 2**20


class Chain:
    def __init__(self):
        self.tokens = []

    def call(self, body, operands, in_specs, out_specs, out_shape, name, grid=(), scratch=(), aliases=None, cost=None):
        count, n_tokens, n_outs = len(operands), len(self.tokens), len(out_shape)

        def with_tokens(*refs):
            outs = count + n_tokens
            body(*refs[:count], *refs[outs : outs + n_outs], *refs[outs + n_outs + 1 :])

        operands = [
            pltpu.with_memory_space_constraint(value, pltpu.HBM) if large(value) else value
            for value in operands
        ]
        outs = pl.pallas_call(
            with_tokens,
            grid=grid,
            in_specs=list(in_specs) + [ANY] * n_tokens,
            out_specs=list(out_specs) + [ANY],
            out_shape=list(out_shape) + [jax.ShapeDtypeStruct(TOKEN, jnp.float32)],
            scratch_shapes=scratch,
            input_output_aliases=aliases or {},
            compiler_params=pltpu.CompilerParams(vmem_limit_bytes=VMEM),
            cost_estimate=pl.CostEstimate(
                flops=WEIGHTS[name] if cost is None else cost, bytes_accessed=1024, transcendentals=0
            ),
            name=name,
        )(*operands, *self.tokens)
        self.tokens = [outs[-1]]
        return list(outs[:-1])

    def pin(self, value):
        pinned = self.call(
            lambda *refs: None,
            [value],
            [ANY],
            [ANY],
            [jax.ShapeDtypeStruct(value.shape, value.dtype)],
            "pin",
            aliases={0: 0},
        )
        return pinned[0]


def activate(chain, gate, up, first, steps, parts):
    rows = gate.shape[0]

    def body(gate_ref, up_ref, *refs):
        outs, (gates, ups, hidden, in_sems, out_sems) = refs[: len(parts)], refs[len(parts) :]

        def fetch(k, source, target, side):
            at = pl.ds((first + k) * STEP, STEP)
            return pltpu.make_async_copy(source.at[:, at], target.at[k], in_sems.at[side, k])

        for k in range(steps):
            fetch(k, gate_ref, gates, 0).start()
            fetch(k, up_ref, ups, 1).start()
        sent = []
        for k in range(steps):
            fetch(k, gate_ref, gates, 0).wait()
            fetch(k, up_ref, ups, 1).wait()
            value = gates[k].astype(jnp.float32)
            value = value / (1.0 + jnp.exp(-value)) * ups[k].astype(jnp.float32)
            hidden[k] = value.astype(jnp.bfloat16)
            for p, (a, b, s, e) in enumerate(parts):
                if s <= first + k < e:
                    copy = pltpu.make_async_copy(
                        hidden.at[k, pl.ds(a, b - a)],
                        outs[p].at[:, pl.ds((first + k - s) * STEP, STEP)],
                        out_sems.at[p, k],
                    )
                    copy.start()
                    sent.append(copy)
        for copy in sent:
            copy.wait()

    buffer = pltpu.VMEM((steps, rows, STEP), jnp.bfloat16)
    return chain.call(
        body,
        [gate, up],
        [ANY] * 2,
        [ANY] * len(parts),
        [jax.ShapeDtypeStruct((b - a, (e - s) * STEP), jnp.bfloat16) for a, b, s, e in parts],
        "activate",
        scratch=[buffer] * 3
        + [pltpu.SemaphoreType.DMA((2, steps)), pltpu.SemaphoreType.DMA((len(parts), steps))],
    )


def multiply(chain, chunks, weight, first, total, split, cost):
    counts = [piece.shape[0] for piece in chunks[0]]
    rows, cols = sum(counts), weight.shape[1]
    width = sum(pieces[0].shape[1] for pieces in chunks)
    steps, part = width // DEPTH, cols // sum(map(len, split or [(0,)]))
    flat, col = [], 0
    for pieces in chunks:
        row = 0
        for piece in pieces:
            flat.append((piece, row, col))
            row += piece.shape[0]
        col += pieces[0].shape[1]
    n_total = 0 if total is None else 1
    n_in = len(flat) + 1 + n_total
    shapes = [jax.ShapeDtypeStruct((len(flips), rows, part), jnp.bfloat16) for flips in split]
    if not split:
        shapes = [jax.ShapeDtypeStruct((rows, cols), jnp.float32)]

    def body(*refs):
        piece_refs, weight_ref = refs[: len(flat)], refs[len(flat)]
        total_refs, refs = refs[len(flat) + 1 : n_in], refs[n_in:]
        outs, (left, slots, *sums, sems, piece_sems) = refs[: len(shapes)], refs[len(shapes) :]
        sums = sums[0] if sums else outs[0]

        def fetch(k, slot):
            return pltpu.make_async_copy(
                weight_ref.at[pl.ds(first * STEP + k * DEPTH, DEPTH)], slots.at[slot], sems.at[slot]
            )

        for k in range(min(SLOTS, steps)):
            fetch(k, k).start()
        copies = [
            pltpu.make_async_copy(
                ref,
                left.at[pl.ds(row, piece.shape[0]), pl.ds(col, piece.shape[1])],
                piece_sems.at[n],
            )
            for n, (ref, (piece, row, col)) in enumerate(zip(piece_refs, flat))
        ]
        if n_total:
            copies.append(pltpu.make_async_copy(total_refs[0], sums, piece_sems.at[len(flat)]))
        for copy in copies:
            copy.start()
        if not n_total:
            sums[...] = jnp.zeros(sums.shape, sums.dtype)
        for copy in copies:
            copy.wait()

        def step(k, carry):
            slot = lax.rem(k, SLOTS)
            fetch(k, slot).wait()
            piece = left[:, pl.ds(pl.multiple_of(k * DEPTH, DEPTH), DEPTH)]
            for n in range(cols // TILE):
                at = pl.ds(n * TILE, TILE)
                sums[:, at] += jnp.dot(piece, slots[slot, :, at], preferred_element_type=jnp.float32)

            @pl.when(k + SLOTS < steps)
            def _():
                fetch(k + SLOTS, slot).start()

            return carry

        lax.fori_loop(0, steps, step, 0)
        for out, flips in zip(outs, split):
            for n, flip in enumerate(flips):
                at = pl.ds(pl.multiple_of((lax.axis_index("tp") ^ flip) * part, part), part)
                out[n] = sums[:, at].astype(jnp.bfloat16)

    return chain.call(
        body,
        [piece for piece, _, _ in flat] + [weight] + ([total] if n_total else []),
        [ANY] * n_in,
        [pl.BlockSpec(memory_space=pltpu.VMEM)] * len(shapes),
        shapes,
        "multiply",
        cost=cost,
        scratch=[pltpu.VMEM((rows, width), jnp.bfloat16), pltpu.VMEM((SLOTS, DEPTH, cols), jnp.bfloat16)]
        + ([pltpu.VMEM((rows, cols), jnp.float32)] if split else [])
        + [pltpu.SemaphoreType.DMA((SLOTS,)), pltpu.SemaphoreType.DMA((len(flat) + 1,))],
    )


def add(chain, parts, outs):
    count = len(parts)

    def body(*refs):
        value = sum(ref[...].astype(jnp.float32) for ref in refs[:count]).astype(jnp.bfloat16)
        for ref, (n, a, b) in zip(refs[count:], outs):
            ref[0] = value[n, a:b]

    vmem = pl.BlockSpec(memory_space=pltpu.VMEM)
    shapes = [jax.ShapeDtypeStruct((1, b - a, parts[0].shape[2]), jnp.bfloat16) for _, a, b in outs]
    return chain.call(body, parts, [vmem] * count, [vmem] * len(outs), shapes, "add")


def join(chain, first, second):
    n = first.shape[0]

    def body(first_ref, second_ref, out_ref):
        out_ref[:n] = first_ref[...]
        out_ref[n:] = second_ref[...]

    vmem = pl.BlockSpec(memory_space=pltpu.VMEM)
    shape = jax.ShapeDtypeStruct((n + second.shape[0],) + first.shape[1:], first.dtype)
    return chain.call(body, [first, second], [vmem] * 2, [vmem], [shape], "join")[0]


def encode_blocks(value, store, scales, first):
    lanes = lax.broadcasted_iota(jnp.int32, scales.shape, 1)
    for n in range(value.shape[1] // BLOCK):
        block = value[:, n * BLOCK : (n + 1) * BLOCK].astype(jnp.float32)
        scale = (jnp.max(jnp.abs(block), axis=1, keepdims=True) + EPSILON).astype(jnp.bfloat16)
        scale = scale.astype(jnp.float32)
        store(n, (block / scale).astype(jnp.bfloat16))
        scales = jnp.where(lanes == first + n, scale, scales)
    return scales


def encode_columns(chain, codes, scales, shares, away, start, width):
    rows, part = shares[0][0].shape[1:]
    tp = len(shares)
    blocks = part // BLOCK
    at = slice(start, start + rows)
    height = start + rows if codes is None else codes.shape[0]
    given = [] if codes is None else [codes, scales]

    def body(*refs):
        share_refs = refs[len(given) : len(given) + tp]
        code_ref, scale_ref = refs[len(given) + tp :]
        j = pl.program_id(0)

        @pl.when(j == 0)
        def _():
            scale_ref[...] = refs[1][...] if given else jnp.zeros(scale_ref.shape, scale_ref.dtype)

        if given:
            code_ref[...] = refs[0][...]
        total = scale_ref[at].astype(jnp.float32)
        for flip in range(tp):
            t = lax.axis_index("tp") ^ flip

            def store(n, value, t=t):
                code_ref[at, pl.ds(pl.multiple_of((t * blocks + n) * BLOCK, BLOCK), BLOCK)] = value

            first = ((lax.axis_index("batch") ^ (j + away)) * tp + t) * blocks
            total = encode_blocks(share_refs[flip][...], store, total, first)
        scale_ref[at] = total.astype(jnp.bfloat16)

    whole = pl.BlockSpec((height, width // BLOCK), lambda j: (0, 0))
    columns = pl.BlockSpec((height, tp * part), lambda j: (0, lax.axis_index("batch") ^ (j + away)))

    def share_spec(n):
        return pl.BlockSpec((None, rows, part), lambda j: (n + j, 0, 0))

    return chain.call(
        body,
        given + [array for array, _ in shares],
        [columns, whole][: len(given)] + [share_spec(n) for _, n in shares],
        [columns, whole],
        [
            jax.ShapeDtypeStruct((height, width), jnp.bfloat16),
            jax.ShapeDtypeStruct((height, width // BLOCK), jnp.bfloat16),
        ],
        "encode",
        grid=(2,),
        aliases={0: 0, 1: 1} if given else {},
    )


DIRECT = [(0,), (1,), (2,), (3,)]
HALVES = [(0, 2), (1, 3)]


def paired_shards(gate_input, up_input, down_weight):
    rows, width = gate_input.shape
    tp, batch = lax.axis_size("tp"), lax.axis_size("batch")
    out_width = down_weight.shape[1] * batch
    cut = rows * EARLY // 8
    ends = [FIRST, FIRST + PIECE, FIRST + 2 * PIECE, FIRST + 3 * PIECE]
    spans = list(zip([0] + ends, ends))
    chain = Chain()

    def swap(value, flip):
        return lax.ppermute(value, "batch", [(b, b ^ flip) for b in range(batch)]) if flip else value

    def shift(value, flip):
        return lax.ppermute(value, "tp", [(t, t ^ flip) for t in range(tp)])

    def both_cores(piece):
        piece = chain.pin(piece)
        return [piece, swap(piece, 1)]

    def product(chunks, first, total, split=(), cost=None):
        outs = multiply(chain, chunks, down_weight, first, total, split, cost)
        return outs if split else outs[0]

    def sum_home(parts, away):
        half = parts[0].shape[1] // 2
        ahead, behind = add(chain, parts, [(0, 0, half), (0, half, 2 * half)])
        return swap(ahead, away), swap(behind, away + 1)

    def sum_pair(parts):
        keep, got = parts
        total = add(chain, [keep, got], [(0, 0, keep.shape[1]), (1, 0, keep.shape[1])])
        return [total[0], shift(total[1], 2)]

    near_0, send_0 = activate(
        chain, gate_input, up_input, 0, FIRST, [(0, rows, 0, FIRST), (0, cut, 0, FIRST)]
    )
    far_0 = swap(send_0, 2)
    pieces = activate(
        chain,
        gate_input,
        up_input,
        0,
        width // STEP,
        [(0, rows, a, b) for a, b in spans[1:]]
        + [(0, cut, a, b) for a, b in spans[1:]]
        + [(cut, rows, a, b) for a, b in [(0, ends[1])] + spans[2:]],
    )
    near, early, late = [near_0] + pieces[:3], pieces[3:6], pieces[6:]
    near = [[h, swap(h, 1)] for h in near]
    far_0 = both_cores(far_0)
    far_1, far_2 = swap(early[0], 2), swap(early[1], 2)

    total = product(near[:3], 0, None)
    far_1 = both_cores(far_1)
    far_3 = swap(chain.pin(early[2]), 2)
    near = product(near[3:], ends[2], total, HALVES)
    near = [near[0], shift(near[1], 1)]

    total = product([far_0, far_1], 0, None)
    far_2 = both_cores(far_2)
    late_0 = swap(chain.pin(late[0]), 2)
    near = sum_pair(near)
    total = product([far_2], ends[1], total)
    far_3 = both_cores(far_3)
    late_1, late_2 = swap(chain.pin(late[1]), 2), swap(chain.pin(late[2]), 2)
    near = sum_home(near, 0)
    far = product([far_3], ends[2], total, HALVES)
    far = [far[0], shift(far[1], 1)]

    late_0 = both_cores(late_0)
    near = join(chain, *near)
    near = [near, shift(near, 2)]
    total = product([late_0], 0, None)
    near.append(join(chain, *near))
    near[2] = shift(near[2], 1)
    far = sum_pair(far)
    late_1 = both_cores(late_1)
    total = product([late_1], ends[1], total)
    near = [(near[0], 0), (near[2], 0), (near[1], 0), (near[2], 2)]
    codes, scales = encode_columns(chain, None, None, near, 0, 0, out_width)
    far = sum_home(far, 2)
    late_2 = both_cores(late_2)
    far = join(chain, *far)
    far = [far, shift(far, 2)]
    last = product([late_2], ends[2], total, HALVES)
    last = [last[0], shift(last[1], 1)]
    far.append(join(chain, *far))
    far[2] = shift(far[2], 1)
    last = sum_home(sum_pair(last), 2)
    far = [(far[0], 0), (far[2], 0), (far[1], 0), (far[2], 2)]
    codes, scales = encode_columns(chain, codes, scales, far, 2, 0, out_width)
    last = join(chain, *last)
    last = [last] + [shift(last, flip) for flip in range(1, tp)]
    last = [(array, 0) for array in last]
    codes, scales = encode_columns(chain, codes, scales, last, 2, cut, out_width)
    return codes, scales


def solution(mesh):
    def shards(gate_input, up_input, down_weight):
        tp, batch = mesh.shape["tp"], mesh.shape["batch"]
        width, cols = down_weight.shape
        paired = batch == tp == 4 and cols % (tp * TILE) == 0 and width == (FIRST + 3 * PIECE) * STEP
        return (paired_shards if paired else general_shards)(gate_input, up_input, down_weight)

    in_specs = (P(("groups", "batch"), "tp"), P(("groups", "batch"), "tp"), P("tp", "batch"))
    out_specs = (P(("groups", "batch"), None), P(("groups", "batch"), None))
    return jax.shard_map(shards, mesh=mesh, in_specs=in_specs, out_specs=out_specs, check_vma=False)
```

```python
import functools

import jax
import jax.numpy as jnp
from jax import lax
from jax.experimental import pallas as pl
from jax.experimental.pallas import tpu as pltpu
from jax.sharding import PartitionSpec as P

BLOCK = 128
EPSILON = 1e-06

STEP = 1024
FIRST = 1
PIECE = 4
DEPTH = 512
SLOTS = 6
TILE = 512
EARLY = 5
VMEM = 32 * 2**20


def encode(values):
    leading = values.shape[:-1]
    blocks = values.reshape(leading + (values.shape[-1] // BLOCK, BLOCK))
    scales = (jnp.max(jnp.abs(blocks), axis=-1) + EPSILON).astype(jnp.bfloat16)
    widened = lax.optimization_barrier(scales).astype(jnp.float32)
    encoded = (blocks / widened[..., None]).astype(jnp.bfloat16)
    return (encoded.reshape(values.shape), scales)


def decode(encoded, scales):
    blocks = encoded.reshape(scales.shape + (BLOCK,)).astype(jnp.float32)
    return (blocks * scales.astype(jnp.float32)[..., None]).reshape(encoded.shape)


def general_shards(gate_input, up_input, down_weight):
    hidden = (jax.nn.silu(gate_input.astype(jnp.float32)) * up_input.astype(jnp.float32)).astype(
        jnp.bfloat16
    )
    partial_value = jnp.dot(
        lax.all_gather(hidden, "batch", axis=0, tiled=True),
        down_weight,
        preferred_element_type=jnp.float32,
    )
    part_codes, part_scales = encode(partial_value)
    tp_count = lax.axis_size("tp")
    batch_count = lax.axis_size("batch")
    row_count = hidden.shape[0]
    local_cols = partial_value.shape[1]
    local_blocks = part_scales.shape[1]
    row_share = row_count // tp_count
    got_codes, got_scales = (
        lax.all_to_all(
            part_codes.reshape(batch_count, tp_count, row_share, local_cols),
            "tp",
            split_axis=1,
            concat_axis=1,
            tiled=True,
        ),
        lax.all_to_all(
            part_scales.reshape(batch_count, tp_count, row_share, local_blocks),
            "tp",
            split_axis=1,
            concat_axis=1,
            tiled=True,
        ),
    )
    summed = jnp.sum(decode(got_codes, got_scales), axis=1)
    new_codes, new_scales = encode(summed)
    home_codes, home_scales = (
        lax.all_to_all(new_codes, "batch", split_axis=0, concat_axis=2, tiled=True),
        lax.all_to_all(new_scales, "batch", split_axis=0, concat_axis=2, tiled=True),
    )
    out_codes, out_scales = (
        lax.all_gather(home_codes, "tp", axis=1, tiled=True),
        lax.all_gather(home_scales, "tp", axis=1, tiled=True),
    )
    return (out_codes.reshape(row_count, -1), out_scales.reshape(row_count, -1))


ANY = pl.BlockSpec(memory_space=pl.ANY)
WEIGHTS = {"activate": 10**10, "multiply": 10**10, "pin": 10**10, "add": 0, "join": 0, "encode": 0, "encode_near": 0}


TOKEN = (8, 128)


def large(value):
    return value.size * value.dtype.itemsize > 3 * 2**20


class Chain:
    def __init__(self):
        self.tokens = []

    def call(self, body, operands, in_specs, out_specs, out_shape, name, grid=(), scratch=(), aliases=None, cost=None):
        count, n_tokens, n_outs = len(operands), len(self.tokens), len(out_shape)

        def with_tokens(*refs):
            outs = count + n_tokens
            body(*refs[:count], *refs[outs : outs + n_outs], *refs[outs + n_outs + 1 :])

        operands = [
            pltpu.with_memory_space_constraint(value, pltpu.HBM) if large(value) else value
            for value in operands
        ]
        outs = pl.pallas_call(
            with_tokens,
            grid=grid,
            in_specs=list(in_specs) + [ANY] * n_tokens,
            out_specs=list(out_specs) + [ANY],
            out_shape=list(out_shape) + [jax.ShapeDtypeStruct(TOKEN, jnp.float32)],
            scratch_shapes=scratch,
            input_output_aliases=aliases or {},
            compiler_params=pltpu.CompilerParams(vmem_limit_bytes=VMEM),
            cost_estimate=pl.CostEstimate(
                flops=WEIGHTS[name] if cost is None else cost, bytes_accessed=1024, transcendentals=0
            ),
            name=name,
        )(*operands, *self.tokens)
        self.tokens = [outs[-1]]
        return list(outs[:-1])

    def pin(self, value):
        pinned = self.call(
            lambda *refs: None,
            [value],
            [ANY],
            [ANY],
            [jax.ShapeDtypeStruct(value.shape, value.dtype)],
            "pin",
            aliases={0: 0},
        )
        return pinned[0]


def activate(chain, gate, up, first, steps, parts):
    rows = gate.shape[0]

    def body(gate_ref, up_ref, *refs):
        outs, (gates, ups, hidden, in_sems, out_sems) = refs[: len(parts)], refs[len(parts) :]

        def fetch(k, source, target, side):
            at = pl.ds((first + k) * STEP, STEP)
            return pltpu.make_async_copy(source.at[:, at], target.at[k], in_sems.at[side, k])

        for k in range(steps):
            fetch(k, gate_ref, gates, 0).start()
            fetch(k, up_ref, ups, 1).start()
        sent = []
        for k in range(steps):
            fetch(k, gate_ref, gates, 0).wait()
            fetch(k, up_ref, ups, 1).wait()
            value = gates[k].astype(jnp.float32)
            value = value / (1.0 + jnp.exp(-value)) * ups[k].astype(jnp.float32)
            hidden[k] = value.astype(jnp.bfloat16)
            for p, (a, b, s, e) in enumerate(parts):
                if s <= first + k < e:
                    copy = pltpu.make_async_copy(
                        hidden.at[k, pl.ds(a, b - a)],
                        outs[p].at[:, pl.ds((first + k - s) * STEP, STEP)],
                        out_sems.at[p, k],
                    )
                    copy.start()
                    sent.append(copy)
        for copy in sent:
            copy.wait()

    buffer = pltpu.VMEM((steps, rows, STEP), jnp.bfloat16)
    return chain.call(
        body,
        [gate, up],
        [ANY] * 2,
        [ANY] * len(parts),
        [jax.ShapeDtypeStruct((b - a, (e - s) * STEP), jnp.bfloat16) for a, b, s, e in parts],
        "activate",
        scratch=[buffer] * 3
        + [pltpu.SemaphoreType.DMA((2, steps)), pltpu.SemaphoreType.DMA((len(parts), steps))],
    )


def multiply(chain, chunks, weight, first, total, last, split):
    counts = [piece.shape[0] for piece in chunks[0]]
    rows, cols = sum(counts), weight.shape[1]
    width = sum(pieces[0].shape[1] for pieces in chunks)
    steps, part = width // DEPTH, cols // max(1, sum(map(len, split)))
    flat, col = [], 0
    for pieces in chunks:
        row = 0
        for piece in pieces:
            flat.append((piece, row, col))
            row += piece.shape[0]
        col += pieces[0].shape[1]
    n_total = 0 if total is None else 1
    n_in = len(flat) + 1 + n_total
    shapes = [jax.ShapeDtypeStruct((len(flips), rows, part), jnp.bfloat16) for flips in split]
    if not split:
        shapes = [jax.ShapeDtypeStruct((rows, cols), jnp.float32)]
    if last and not split:
        part = cols // lax.axis_size("tp")
        shapes = [jax.ShapeDtypeStruct((cols // part, rows, part), jnp.bfloat16)]

    def body(*refs):
        piece_refs, weight_ref = refs[: len(flat)], refs[len(flat)]
        total_refs, refs = refs[len(flat) + 1 : n_in], refs[n_in:]
        outs, (left, slots, *sums, sems, piece_sems) = refs[: len(shapes)], refs[len(shapes) :]
        sums = sums[0] if sums else outs[0]

        def fetch(k, slot):
            return pltpu.make_async_copy(
                weight_ref.at[pl.ds(first * STEP + k * DEPTH, DEPTH)], slots.at[slot], sems.at[slot]
            )

        for k in range(min(SLOTS, steps)):
            fetch(k, k).start()
        copies = [
            pltpu.make_async_copy(
                ref,
                left.at[pl.ds(row, piece.shape[0]), pl.ds(col, piece.shape[1])],
                piece_sems.at[n],
            )
            for n, (ref, (piece, row, col)) in enumerate(zip(piece_refs, flat))
        ]
        if n_total:
            copies.append(pltpu.make_async_copy(total_refs[0], sums, piece_sems.at[len(flat)]))
        for copy in copies:
            copy.start()
        if not n_total:
            sums[...] = jnp.zeros(sums.shape, sums.dtype)
        for copy in copies:
            copy.wait()

        def step(k, carry):
            slot = lax.rem(k, SLOTS)
            fetch(k, slot).wait()
            piece = left[:, pl.ds(pl.multiple_of(k * DEPTH, DEPTH), DEPTH)]
            for n in range(cols // TILE):
                at = pl.ds(n * TILE, TILE)
                sums[:, at] += jnp.dot(piece, slots[slot, :, at], preferred_element_type=jnp.float32)

            @pl.when(k + SLOTS < steps)
            def _():
                fetch(k + SLOTS, slot).start()

            return carry

        lax.fori_loop(0, steps, step, 0)
        if last and not split:
            for t in range(cols // part):
                outs[0][t] = sums[:, t * part : (t + 1) * part].astype(jnp.bfloat16)
        for out, flips in zip(outs, split):
            for n, flip in enumerate(flips):
                at = pl.ds(pl.multiple_of((lax.axis_index("tp") ^ flip) * part, part), part)
                out[n] = sums[:, at].astype(jnp.bfloat16)

    return chain.call(
        body,
        [piece for piece, _, _ in flat] + [weight] + ([total] if n_total else []),
        [ANY] * n_in,
        [pl.BlockSpec(memory_space=pltpu.VMEM)] * len(shapes),
        shapes,
        "multiply",
        scratch=[pltpu.VMEM((rows, width), jnp.bfloat16), pltpu.VMEM((SLOTS, DEPTH, cols), jnp.bfloat16)]
        + ([pltpu.VMEM((rows, cols), jnp.float32)] if last else [])
        + [pltpu.SemaphoreType.DMA((SLOTS,)), pltpu.SemaphoreType.DMA((len(flat) + 1,))],
    )


def add(chain, parts, outs, spec=None):
    count = len(parts)

    def body(*refs):
        value = sum(ref[...].astype(jnp.float32) for ref in refs[:count]).astype(jnp.bfloat16)
        for ref, (n, a, b) in zip(refs[count:], outs):
            ref[0] = value[n, a:b]

    vmem = pl.BlockSpec(memory_space=pltpu.VMEM)
    shapes = [jax.ShapeDtypeStruct((1, b - a, parts[0].shape[2]), jnp.bfloat16) for _, a, b in outs]
    specs = [spec or vmem] * count
    return chain.call(body, parts, specs, [vmem] * len(outs), shapes, "add", grid=(1,) if spec else ())


def join(chain, first, second):
    n = first.shape[0]

    def body(first_ref, second_ref, out_ref):
        out_ref[:n] = first_ref[...]
        out_ref[n:] = second_ref[...]

    vmem = pl.BlockSpec(memory_space=pltpu.VMEM)
    shape = jax.ShapeDtypeStruct((n + second.shape[0],) + first.shape[1:], first.dtype)
    return chain.call(body, [first, second], [vmem] * 2, [vmem], [shape], "join")[0]


def encode_blocks(value, store, scales, first):
    lanes = lax.broadcasted_iota(jnp.int32, scales.shape, 1)
    for n in range(value.shape[1] // BLOCK):
        block = value[:, n * BLOCK : (n + 1) * BLOCK].astype(jnp.float32)
        scale = (jnp.max(jnp.abs(block), axis=1, keepdims=True) + EPSILON).astype(jnp.bfloat16)
        scale = scale.astype(jnp.float32)
        store(n, (block / scale).astype(jnp.bfloat16))
        scales = jnp.where(lanes == first + n, scale, scales)
    return scales


def encode_columns(chain, codes, scales, shares, away, start, width):
    rows, part = shares[0][0].shape[1:]
    tp = len(shares)
    blocks = part // BLOCK
    at = slice(start, start + rows)
    height = start + rows if codes is None else codes.shape[0]
    given = [] if codes is None else [codes, scales]

    def body(*refs):
        share_refs = refs[len(given) : len(given) + tp]
        code_ref, scale_ref = refs[len(given) + tp :]
        j = pl.program_id(0)

        @pl.when(j == 0)
        def _():
            scale_ref[...] = refs[1][...] if given else jnp.zeros(scale_ref.shape, scale_ref.dtype)

        if given:
            code_ref[...] = refs[0][...]
        total = scale_ref[at].astype(jnp.float32)
        for flip in range(tp):
            t = lax.axis_index("tp") ^ flip

            def store(n, value, t=t):
                code_ref[at, pl.ds(pl.multiple_of((t * blocks + n) * BLOCK, BLOCK), BLOCK)] = value

            first = ((lax.axis_index("batch") ^ (j + away)) * tp + t) * blocks
            total = encode_blocks(share_refs[flip][...], store, total, first)
        scale_ref[at] = total.astype(jnp.bfloat16)

    whole = pl.BlockSpec((height, width // BLOCK), lambda j: (0, 0))
    columns = pl.BlockSpec((height, tp * part), lambda j: (0, lax.axis_index("batch") ^ (j + away)))

    def share_spec(n):
        return pl.BlockSpec((None, rows, part), lambda j: (n + j, 0, 0))

    return chain.call(
        body,
        given + [array for array, _ in shares],
        [columns, whole][: len(given)] + [share_spec(n) for _, n in shares],
        [columns, whole],
        [
            jax.ShapeDtypeStruct((height, width), jnp.bfloat16),
            jax.ShapeDtypeStruct((height, width // BLOCK), jnp.bfloat16),
        ],
        "encode",
        grid=(2,),
        aliases={0: 0, 1: 1} if given else {},
    )


DIRECT = [(0,), (1,), (2,), (3,)]
HALVES = [(0, 2), (1, 3)]


def paired_shards(gate_input, up_input, down_weight):
    rows, width = gate_input.shape
    tp, batch = lax.axis_size("tp"), lax.axis_size("batch")
    out_width = down_weight.shape[1] * batch
    cut = rows * EARLY // 8
    ends = [FIRST, FIRST + PIECE, FIRST + 2 * PIECE, FIRST + 3 * PIECE]
    spans = list(zip([0] + ends, ends))
    chain = Chain()

    def swap(value, flip):
        return lax.ppermute(value, "batch", [(b, b ^ flip) for b in range(batch)]) if flip else value

    def shift(value, flip):
        return lax.ppermute(value, "tp", [(t, t ^ flip) for t in range(tp)])

    def both_cores(piece):
        piece = chain.pin(piece)
        return [piece, swap(piece, 1)]

    def product(chunks, first, total, last=False, split=()):
        outs = multiply(chain, chunks, down_weight, first, total, last, split)
        return outs if split else outs[0]

    def sum_home(parts, away):
        half = parts[0].shape[1] // 2
        ahead, behind = add(chain, parts, [(0, 0, half), (0, half, 2 * half)])
        return swap(ahead, away), swap(behind, away + 1)

    def sum_pair(parts):
        keep, got = parts
        total = add(chain, [keep, got], [(0, 0, keep.shape[1]), (1, 0, keep.shape[1])])
        return [total[0], shift(total[1], 2)]

    near_0, send_0 = activate(
        chain, gate_input, up_input, 0, FIRST, [(0, rows, 0, FIRST), (0, cut, 0, FIRST)]
    )
    far_0 = swap(send_0, 2)
    near_1, early_1, late_0 = activate(
        chain, gate_input, up_input, 0, ends[1], [(0, rows, *spans[1]), (0, cut, *spans[1]), (cut, rows, 0, ends[1])]
    )
    far_1 = swap(early_1, 2)
    near = [[h, swap(h, 1)] for h in (near_0, near_1)]
    far_0 = both_cores(far_0)
    near_2, near_3, early_2, early_3, late_1, late_2 = activate(
        chain,
        gate_input,
        up_input,
        ends[1],
        ends[3] - ends[1],
        [(a, b, *span) for a, b in ((0, rows), (0, cut), (cut, rows)) for span in spans[2:]],
    )
    far_2 = swap(early_2, 2)
    near = near + [[h, swap(h, 1)] for h in (near_2, near_3)]

    total = product(near[:3], 0, None)
    far_1 = both_cores(far_1)
    far_3 = swap(chain.pin(early_3), 2)
    near = product(near[3:], ends[2], total, True)
    near = lax.psum_scatter(near, "tp", scatter_dimension=0, tiled=True)

    total = product([far_0, far_1], 0, None)
    far_2 = both_cores(far_2)
    late_0 = swap(chain.pin(late_0), 2)
    total = product([far_2], ends[1], total)
    far_3 = both_cores(far_3)
    late_1 = swap(chain.pin(late_1), 2)
    far = product([far_3], ends[2], total, True, HALVES)
    far = [far[0], shift(far[1], 1)]

    block = pl.BlockSpec(near.shape, lambda k: (0, 0, 0))
    near, beside = add(chain, [near], [(0, 0, rows), (0, rows, 2 * rows)], block)
    beside = swap(beside, 1)

    late_0 = both_cores(late_0)
    late_2 = swap(chain.pin(late_2), 2)
    total = product([late_0], 0, None)
    near = join(chain, near, beside)
    near = [near, shift(near, 2)]
    far = sum_pair(far)
    late_1 = both_cores(late_1)
    total = product([late_1], ends[1], total)
    near.append(join(chain, *near))
    near[2] = shift(near[2], 1)
    far = sum_home(far, 2)
    late_2 = both_cores(late_2)
    far = join(chain, *far)
    far = [far, shift(far, 2)]
    last = product([late_2], ends[2], total, True, HALVES)
    last = [last[0], shift(last[1], 1)]
    far.append(join(chain, *far))
    far[2] = shift(far[2], 1)
    near = [(near[0], 0), (near[2], 0), (near[1], 0), (near[2], 2)]
    codes, scales = encode_columns(chain, None, None, near, 0, 0, out_width)
    last = sum_pair(last)
    last = sum_home(last, 2)
    far = [(far[0], 0), (far[2], 0), (far[1], 0), (far[2], 2)]
    codes, scales = encode_columns(chain, codes, scales, far, 2, 0, out_width)
    last = join(chain, *last)
    last = [last] + [shift(last, flip) for flip in range(1, tp)]
    last = [(array, 0) for array in last]
    codes, scales = encode_columns(chain, codes, scales, last, 2, cut, out_width)
    return codes, scales


def solution(mesh):
    def shards(gate_input, up_input, down_weight):
        tp, batch = mesh.shape["tp"], mesh.shape["batch"]
        width, cols = down_weight.shape
        paired = batch == tp == 4 and cols % (tp * TILE) == 0 and width == (FIRST + 3 * PIECE) * STEP
        return (paired_shards if paired else general_shards)(gate_input, up_input, down_weight)

    in_specs = (P(("groups", "batch"), "tp"), P(("groups", "batch"), "tp"), P("tp", "batch"))
    out_specs = (P(("groups", "batch"), None), P(("groups", "batch"), None))
    return jax.shard_map(shards, mesh=mesh, in_specs=in_specs, out_specs=out_specs, check_vma=False)
```

```python
import functools

import jax
import jax.numpy as jnp
from jax import lax
from jax.experimental import pallas as pl
from jax.experimental.pallas import tpu as pltpu
from jax.sharding import PartitionSpec as P

BLOCK = 128
EPSILON = 1e-06

STEP = 1024
FIRST = 1
PIECE = 4
DEPTH = 512
SLOTS = 6
TILE = 512
EARLY = 5
LANES = 128
VMEM = 32 * 2**20


def encode(values):
    leading = values.shape[:-1]
    blocks = values.reshape(leading + (values.shape[-1] // BLOCK, BLOCK))
    scales = (jnp.max(jnp.abs(blocks), axis=-1) + EPSILON).astype(jnp.bfloat16)
    widened = lax.optimization_barrier(scales).astype(jnp.float32)
    encoded = (blocks / widened[..., None]).astype(jnp.bfloat16)
    return (encoded.reshape(values.shape), scales)


def decode(encoded, scales):
    blocks = encoded.reshape(scales.shape + (BLOCK,)).astype(jnp.float32)
    return (blocks * scales.astype(jnp.float32)[..., None]).reshape(encoded.shape)


def general_shards(gate_input, up_input, down_weight):
    hidden = (jax.nn.silu(gate_input.astype(jnp.float32)) * up_input.astype(jnp.float32)).astype(
        jnp.bfloat16
    )
    partial_value = jnp.dot(
        lax.all_gather(hidden, "batch", axis=0, tiled=True),
        down_weight,
        preferred_element_type=jnp.float32,
    )
    part_codes, part_scales = encode(partial_value)
    tp_count = lax.axis_size("tp")
    batch_count = lax.axis_size("batch")
    row_count = hidden.shape[0]
    local_cols = partial_value.shape[1]
    local_blocks = part_scales.shape[1]
    row_share = row_count // tp_count
    got_codes, got_scales = (
        lax.all_to_all(
            part_codes.reshape(batch_count, tp_count, row_share, local_cols),
            "tp",
            split_axis=1,
            concat_axis=1,
            tiled=True,
        ),
        lax.all_to_all(
            part_scales.reshape(batch_count, tp_count, row_share, local_blocks),
            "tp",
            split_axis=1,
            concat_axis=1,
            tiled=True,
        ),
    )
    summed = jnp.sum(decode(got_codes, got_scales), axis=1)
    new_codes, new_scales = encode(summed)
    home_codes, home_scales = (
        lax.all_to_all(new_codes, "batch", split_axis=0, concat_axis=2, tiled=True),
        lax.all_to_all(new_scales, "batch", split_axis=0, concat_axis=2, tiled=True),
    )
    out_codes, out_scales = (
        lax.all_gather(home_codes, "tp", axis=1, tiled=True),
        lax.all_gather(home_scales, "tp", axis=1, tiled=True),
    )
    return (out_codes.reshape(row_count, -1), out_scales.reshape(row_count, -1))


ANY = pl.BlockSpec(memory_space=pl.ANY)
WEIGHTS = {"activate": 10**10, "multiply": 10**10, "pin": 10**10, "add": 0, "join": 0, "encode": 0}


TOKEN = (8, 128)


def large(value):
    return value.size * value.dtype.itemsize > 3 * 2**20


class Chain:
    def __init__(self):
        self.tokens = []

    def call(self, body, operands, in_specs, out_specs, out_shape, name, grid=(), scratch=(), aliases=None, cost=None):
        count, n_tokens, n_outs = len(operands), len(self.tokens), len(out_shape)

        def with_tokens(*refs):
            outs = count + n_tokens
            body(*refs[:count], *refs[outs : outs + n_outs], *refs[outs + n_outs + 1 :])

        operands = [
            pltpu.with_memory_space_constraint(value, pltpu.HBM) if large(value) else value
            for value in operands
        ]
        outs = pl.pallas_call(
            with_tokens,
            grid=grid,
            in_specs=list(in_specs) + [ANY] * n_tokens,
            out_specs=list(out_specs) + [ANY],
            out_shape=list(out_shape) + [jax.ShapeDtypeStruct(TOKEN, jnp.float32)],
            scratch_shapes=scratch,
            input_output_aliases=aliases or {},
            compiler_params=pltpu.CompilerParams(vmem_limit_bytes=VMEM),
            cost_estimate=pl.CostEstimate(
                flops=WEIGHTS[name] if cost is None else cost, bytes_accessed=1024, transcendentals=0
            ),
            name=name,
        )(*operands, *self.tokens)
        self.tokens = [outs[-1]]
        return list(outs[:-1])

    def pin(self, value, cost=None):
        pinned = self.call(
            lambda *refs: None,
            [value],
            [ANY],
            [ANY],
            [jax.ShapeDtypeStruct(value.shape, value.dtype)],
            "pin",
            aliases={0: 0},
            cost=cost,
        )
        return pinned[0]


def activate(chain, gate, up, first, steps, parts):
    rows = gate.shape[0]

    def body(gate_ref, up_ref, *refs):
        outs, (gates, ups, hidden, in_sems, out_sems) = refs[: len(parts)], refs[len(parts) :]

        def fetch(k, source, target, side):
            at = pl.ds((first + k) * STEP, STEP)
            return pltpu.make_async_copy(source.at[:, at], target.at[k], in_sems.at[side, k])

        for k in range(steps):
            fetch(k, gate_ref, gates, 0).start()
            fetch(k, up_ref, ups, 1).start()
        sent = []
        for k in range(steps):
            fetch(k, gate_ref, gates, 0).wait()
            fetch(k, up_ref, ups, 1).wait()
            value = gates[k].astype(jnp.float32)
            value = value / (1.0 + jnp.exp(-value)) * ups[k].astype(jnp.float32)
            hidden[k] = value.astype(jnp.bfloat16)
            for p, (a, b, s, e) in enumerate(parts):
                if s <= first + k < e:
                    copy = pltpu.make_async_copy(
                        hidden.at[k, pl.ds(a, b - a)],
                        outs[p].at[:, pl.ds((first + k - s) * STEP, STEP)],
                        out_sems.at[p, k],
                    )
                    copy.start()
                    sent.append(copy)
        for copy in sent:
            copy.wait()

    buffer = pltpu.VMEM((steps, rows, STEP), jnp.bfloat16)
    return chain.call(
        body,
        [gate, up],
        [ANY] * 2,
        [ANY] * len(parts),
        [jax.ShapeDtypeStruct((b - a, (e - s) * STEP), jnp.bfloat16) for a, b, s, e in parts],
        "activate",
        scratch=[buffer] * 3
        + [pltpu.SemaphoreType.DMA((2, steps)), pltpu.SemaphoreType.DMA((len(parts), steps))],
    )


def multiply(chain, chunks, weight, first, total, split, cost):
    counts = [piece.shape[0] for piece in chunks[0]]
    rows, cols = sum(counts), weight.shape[1]
    width = sum(pieces[0].shape[1] for pieces in chunks)
    steps, part = width // DEPTH, cols // sum(map(len, split or [(0,)]))
    flat, col = [], 0
    for pieces in chunks:
        row = 0
        for piece in pieces:
            flat.append((piece, row, col))
            row += piece.shape[0]
        col += pieces[0].shape[1]
    n_total = 0 if total is None else 1
    n_in = len(flat) + 1 + n_total
    shapes = [jax.ShapeDtypeStruct((len(flips), rows, part), jnp.bfloat16) for flips in split]
    if not split:
        shapes = [jax.ShapeDtypeStruct((rows, cols), jnp.float32)]

    def body(*refs):
        piece_refs, weight_ref = refs[: len(flat)], refs[len(flat)]
        total_refs, refs = refs[len(flat) + 1 : n_in], refs[n_in:]
        outs, (left, slots, *sums, sems, piece_sems) = refs[: len(shapes)], refs[len(shapes) :]
        sums = sums[0] if sums else outs[0]

        def fetch(k, slot):
            return pltpu.make_async_copy(
                weight_ref.at[pl.ds(first * STEP + k * DEPTH, DEPTH)], slots.at[slot], sems.at[slot]
            )

        for k in range(min(SLOTS, steps)):
            fetch(k, k).start()
        copies = [
            pltpu.make_async_copy(
                ref,
                left.at[pl.ds(row, piece.shape[0]), pl.ds(col, piece.shape[1])],
                piece_sems.at[n],
            )
            for n, (ref, (piece, row, col)) in enumerate(zip(piece_refs, flat))
        ]
        if n_total:
            copies.append(pltpu.make_async_copy(total_refs[0], sums, piece_sems.at[len(flat)]))
        for copy in copies:
            copy.start()
        if not n_total:
            sums[...] = jnp.zeros(sums.shape, sums.dtype)
        for copy in copies:
            copy.wait()

        def step(k, carry):
            slot = lax.rem(k, SLOTS)
            fetch(k, slot).wait()
            piece = left[:, pl.ds(pl.multiple_of(k * DEPTH, DEPTH), DEPTH)]
            for n in range(cols // TILE):
                at = pl.ds(n * TILE, TILE)
                sums[:, at] += jnp.dot(piece, slots[slot, :, at], preferred_element_type=jnp.float32)

            @pl.when(k + SLOTS < steps)
            def _():
                fetch(k + SLOTS, slot).start()

            return carry

        lax.fori_loop(0, steps, step, 0)
        for out, flips in zip(outs, split):
            for n, flip in enumerate(flips):
                at = pl.ds(pl.multiple_of((lax.axis_index("tp") ^ flip) * part, part), part)
                out[n] = sums[:, at].astype(jnp.bfloat16)

    return chain.call(
        body,
        [piece for piece, _, _ in flat] + [weight] + ([total] if n_total else []),
        [ANY] * n_in,
        [pl.BlockSpec(memory_space=pltpu.VMEM)] * len(shapes),
        shapes,
        "multiply",
        cost=cost,
        scratch=[pltpu.VMEM((rows, width), jnp.bfloat16), pltpu.VMEM((SLOTS, DEPTH, cols), jnp.bfloat16)]
        + ([pltpu.VMEM((rows, cols), jnp.float32)] if split else [])
        + [pltpu.SemaphoreType.DMA((SLOTS,)), pltpu.SemaphoreType.DMA((len(flat) + 1,))],
    )


def add(chain, parts, outs):
    count = len(parts)

    def body(*refs):
        value = sum(ref[...].astype(jnp.float32) for ref in refs[:count]).astype(jnp.bfloat16)
        for ref, (n, a, b) in zip(refs[count:], outs):
            ref[0] = value[n, a:b]

    vmem = pl.BlockSpec(memory_space=pltpu.VMEM)
    shapes = [jax.ShapeDtypeStruct((1, b - a, parts[0].shape[2]), jnp.bfloat16) for _, a, b in outs]
    return chain.call(body, parts, [vmem] * count, [vmem] * len(outs), shapes, "add")


def join(chain, first, second):
    n = first.shape[0]

    def body(first_ref, second_ref, out_ref):
        out_ref[:n] = first_ref[...]
        out_ref[n:] = second_ref[...]

    vmem = pl.BlockSpec(memory_space=pltpu.VMEM)
    shape = jax.ShapeDtypeStruct((n + second.shape[0],) + first.shape[1:], first.dtype)
    return chain.call(body, [first, second], [vmem] * 2, [vmem], [shape], "join")[0]


def encode_blocks(value, store, scales, first):
    lanes = lax.broadcasted_iota(jnp.int32, scales.shape, 1)
    for n in range(value.shape[1] // BLOCK):
        block = value[:, n * BLOCK : (n + 1) * BLOCK].astype(jnp.float32)
        scale = (jnp.max(jnp.abs(block), axis=1, keepdims=True) + EPSILON).astype(jnp.bfloat16)
        scale = scale.astype(jnp.float32)
        store(n, (block / scale).astype(jnp.bfloat16))
        scales = jnp.where(lanes == first + n, scale, scales)
    return scales


def encode_columns(chain, codes, scales, shares, away, start, height, width, last=False):
    rows, part = shares[0][0].shape[1:]
    tp = len(shares)
    blocks, spread = part // BLOCK, tp * part
    given = [] if codes is None else [codes, scales]

    def body(*refs):
        share_refs = refs[len(given) : len(given) + tp]
        code_ref, scale_ref, buffer, table, sems = refs[len(given) + tp :]
        table[...] = refs[1][...] if given else jnp.zeros(table.shape, table.dtype)
        total = table[start : start + rows]
        copies = []
        for j in range(2):
            place = lax.axis_index("batch") ^ (j + away)
            for flip, (ref, (_, n)) in enumerate(zip(share_refs, shares)):
                t = lax.axis_index("tp") ^ flip

                def store(m, value):
                    at = pl.ds(pl.multiple_of((t * blocks + m) * BLOCK, BLOCK), BLOCK)
                    buffer[j, :, at] = value

                total = encode_blocks(ref[n + j], store, total, (place * tp + t) * blocks)
            columns = pl.ds(pl.multiple_of(place * spread, spread), spread)
            copy = pltpu.make_async_copy(
                buffer.at[j], code_ref.at[pl.ds(start, rows), columns], sems.at[j]
            )
            copy.start()
            copies.append(copy)
        table[start : start + rows] = total
        if last:
            scale_ref[...] = table[...].T[: width // BLOCK].astype(jnp.bfloat16)
        else:
            scale_ref[...] = table[...]
        for copy in copies:
            copy.wait()

    vmem = pl.BlockSpec(memory_space=pltpu.VMEM)
    kept = jax.ShapeDtypeStruct((height, LANES), jnp.float32)
    return chain.call(
        body,
        given + [array for array, _ in shares],
        [ANY, vmem][: len(given)] + [vmem] * tp,
        [ANY, vmem],
        [
            jax.ShapeDtypeStruct((height, width), jnp.bfloat16),
            jax.ShapeDtypeStruct((width // BLOCK, height), jnp.bfloat16) if last else kept,
        ],
        "encode",
        scratch=[
            pltpu.VMEM((2, rows, spread), jnp.bfloat16),
            pltpu.VMEM((height, LANES), jnp.float32),
            pltpu.SemaphoreType.DMA((2,)),
        ],
        aliases={0: 0} if given else {},
    )


DIRECT = [(0,), (1,), (2,), (3,)]
HALVES = [(0, 2), (1, 3)]


def paired_shards(gate_input, up_input, down_weight):
    rows, width = gate_input.shape
    tp, batch = lax.axis_size("tp"), lax.axis_size("batch")
    out_width = down_weight.shape[1] * batch
    cut = rows * EARLY // 8
    ends = [FIRST, FIRST + PIECE, FIRST + 2 * PIECE, FIRST + 3 * PIECE]
    spans = list(zip([0] + ends, ends))
    chain = Chain()

    def swap(value, flip):
        return lax.ppermute(value, "batch", [(b, b ^ flip) for b in range(batch)]) if flip else value

    def shift(value, flip):
        return lax.ppermute(value, "tp", [(t, t ^ flip) for t in range(tp)])

    def both_cores(piece, cost=None):
        piece = chain.pin(piece, cost)
        return [piece, swap(piece, 1)]

    def product(chunks, first, total, split=(), cost=None):
        outs = multiply(chain, chunks, down_weight, first, total, split, cost)
        return outs if split else outs[0]

    def sum_home(parts, away):
        half = parts[0].shape[1] // 2
        ahead, behind = add(chain, parts, [(0, 0, half), (0, half, 2 * half)])
        return swap(ahead, away), swap(behind, away + 1)

    def sum_pair(parts):
        keep, got = parts
        total = add(chain, [keep, got], [(0, 0, keep.shape[1]), (1, 0, keep.shape[1])])
        return [total[0], shift(total[1], 2)]

    near_0, send_0 = activate(
        chain, gate_input, up_input, 0, FIRST, [(0, rows, 0, FIRST), (0, cut, 0, FIRST)]
    )
    far_0 = swap(send_0, 2)
    pieces = activate(
        chain,
        gate_input,
        up_input,
        0,
        width // STEP,
        [(0, rows, a, b) for a, b in spans[1:]]
        + [(0, cut, a, b) for a, b in spans[1:]]
        + [(cut, rows, a, b) for a, b in [(0, ends[1])] + spans[2:]],
    )
    near, early, late = [near_0] + pieces[:3], pieces[3:6], pieces[6:]
    near = [[h, swap(h, 1)] for h in near]
    far_0 = both_cores(far_0)
    far_1, far_2 = swap(early[0], 2), swap(early[1], 2)

    total = product(near[:2], 0, None)
    near = product(near[2:], ends[1], total, HALVES)
    near = [near[0], shift(near[1], 1)]

    far_1 = both_cores(far_1)
    far_3 = swap(chain.pin(early[2]), 2)
    total = product([far_0, far_1], 0, None)
    far_2 = both_cores(far_2)
    late_0 = swap(chain.pin(late[0]), 2)
    near = sum_pair(near)
    total = product([far_2], ends[1], total)
    far_3 = both_cores(far_3)
    late_1, late_2 = swap(chain.pin(late[1]), 2), swap(chain.pin(late[2]), 2)
    far = product([far_3], ends[2], total, HALVES)
    far = [far[0], shift(far[1], 1)]
    near = sum_home(near, 0)

    late_0 = both_cores(late_0)
    near = join(chain, *near)
    near = [near, shift(near, 2)]
    total = product([late_0], 0, None)
    near.append(join(chain, *near))
    near[2] = shift(near[2], 1)
    far = sum_pair(far)
    late_1 = both_cores(late_1)
    total = product([late_1], ends[1], total)
    late_2 = both_cores(late_2, 0)
    last = product([late_2], ends[2], total, HALVES, cost=0)
    last = [last[0], shift(last[1], 1)]
    far = sum_home(far, 2)
    near = [(near[0], 0), (near[2], 0), (near[1], 0), (near[2], 2)]
    codes, scales = encode_columns(chain, None, None, near, 0, 0, rows, out_width)
    last = sum_pair(last)
    far = join(chain, *far)
    far = [far, shift(far, 2)]
    last = sum_home(last, 2)
    far.append(join(chain, *far))
    far[2] = shift(far[2], 1)
    last = join(chain, *last)
    last = [last] + [shift(last, flip) for flip in range(1, tp)]
    far = [(far[0], 0), (far[2], 0), (far[1], 0), (far[2], 2)]
    codes, scales = encode_columns(chain, codes, scales, far, 2, 0, rows, out_width)
    last = [(array, 0) for array in last]
    codes, scales = encode_columns(chain, codes, scales, last, 2, cut, rows, out_width, True)
    return codes, scales.T


def solution(mesh):
    def shards(gate_input, up_input, down_weight):
        tp, batch = mesh.shape["tp"], mesh.shape["batch"]
        width, cols = down_weight.shape
        paired = batch == tp == 4 and batch * cols <= LANES * BLOCK and cols % (tp * TILE) == 0 and width == (FIRST + 3 * PIECE) * STEP
        return (paired_shards if paired else general_shards)(gate_input, up_input, down_weight)

    in_specs = (P(("groups", "batch"), "tp"), P(("groups", "batch"), "tp"), P("tp", "batch"))
    out_specs = (P(("groups", "batch"), None), P(("groups", "batch"), None))
    return jax.shard_map(shards, mesh=mesh, in_specs=in_specs, out_specs=out_specs, check_vma=False)
```

```python
import functools

import jax
import jax.numpy as jnp
from jax import lax
from jax.experimental import pallas as pl
from jax.experimental.pallas import tpu as pltpu
from jax.sharding import PartitionSpec as P

BLOCK = 128
EPSILON = 1e-06

STEP = 1024
FIRST = 1
PIECE = 4
DEPTH = 512
SLOTS = 6
TILE = 512
EARLY = 5
LANES = 128
VMEM = 32 * 2**20


def encode(values):
    leading = values.shape[:-1]
    blocks = values.reshape(leading + (values.shape[-1] // BLOCK, BLOCK))
    scales = (jnp.max(jnp.abs(blocks), axis=-1) + EPSILON).astype(jnp.bfloat16)
    widened = lax.optimization_barrier(scales).astype(jnp.float32)
    encoded = (blocks / widened[..., None]).astype(jnp.bfloat16)
    return (encoded.reshape(values.shape), scales)


def decode(encoded, scales):
    blocks = encoded.reshape(scales.shape + (BLOCK,)).astype(jnp.float32)
    return (blocks * scales.astype(jnp.float32)[..., None]).reshape(encoded.shape)


def general_shards(gate_input, up_input, down_weight):
    hidden = (jax.nn.silu(gate_input.astype(jnp.float32)) * up_input.astype(jnp.float32)).astype(
        jnp.bfloat16
    )
    partial_value = jnp.dot(
        lax.all_gather(hidden, "batch", axis=0, tiled=True),
        down_weight,
        preferred_element_type=jnp.float32,
    )
    part_codes, part_scales = encode(partial_value)
    tp_count = lax.axis_size("tp")
    batch_count = lax.axis_size("batch")
    row_count = hidden.shape[0]
    local_cols = partial_value.shape[1]
    local_blocks = part_scales.shape[1]
    row_share = row_count // tp_count
    got_codes, got_scales = (
        lax.all_to_all(
            part_codes.reshape(batch_count, tp_count, row_share, local_cols),
            "tp",
            split_axis=1,
            concat_axis=1,
            tiled=True,
        ),
        lax.all_to_all(
            part_scales.reshape(batch_count, tp_count, row_share, local_blocks),
            "tp",
            split_axis=1,
            concat_axis=1,
            tiled=True,
        ),
    )
    summed = jnp.sum(decode(got_codes, got_scales), axis=1)
    new_codes, new_scales = encode(summed)
    home_codes, home_scales = (
        lax.all_to_all(new_codes, "batch", split_axis=0, concat_axis=2, tiled=True),
        lax.all_to_all(new_scales, "batch", split_axis=0, concat_axis=2, tiled=True),
    )
    out_codes, out_scales = (
        lax.all_gather(home_codes, "tp", axis=1, tiled=True),
        lax.all_gather(home_scales, "tp", axis=1, tiled=True),
    )
    return (out_codes.reshape(row_count, -1), out_scales.reshape(row_count, -1))


ANY = pl.BlockSpec(memory_space=pl.ANY)
WEIGHTS = {"activate": 10**10, "multiply": 10**10, "pin": 10**10, "add": 0, "join": 0, "encode": 0}


TOKEN = (8, 128)


def large(value):
    return value.size * value.dtype.itemsize > 3 * 2**20


class Chain:
    def __init__(self):
        self.tokens = []

    def call(self, body, operands, in_specs, out_specs, out_shape, name, grid=(), scratch=(), aliases=None, cost=None):
        count, n_tokens, n_outs = len(operands), len(self.tokens), len(out_shape)

        def with_tokens(*refs):
            outs = count + n_tokens
            body(*refs[:count], *refs[outs : outs + n_outs], *refs[outs + n_outs + 1 :])

        operands = [
            pltpu.with_memory_space_constraint(value, pltpu.HBM) if large(value) else value
            for value in operands
        ]
        outs = pl.pallas_call(
            with_tokens,
            grid=grid,
            in_specs=list(in_specs) + [ANY] * n_tokens,
            out_specs=list(out_specs) + [ANY],
            out_shape=list(out_shape) + [jax.ShapeDtypeStruct(TOKEN, jnp.float32)],
            scratch_shapes=scratch,
            input_output_aliases=aliases or {},
            compiler_params=pltpu.CompilerParams(vmem_limit_bytes=VMEM),
            cost_estimate=pl.CostEstimate(
                flops=WEIGHTS[name] if cost is None else cost, bytes_accessed=1024, transcendentals=0
            ),
            name=name,
        )(*operands, *self.tokens)
        self.tokens = [outs[-1]]
        return list(outs[:-1])

    def pin(self, value, cost=None):
        pinned = self.call(
            lambda *refs: None,
            [value],
            [ANY],
            [ANY],
            [jax.ShapeDtypeStruct(value.shape, value.dtype)],
            "pin",
            aliases={0: 0},
            cost=cost,
        )
        return pinned[0]


def activate(chain, gate, up, first, steps, parts):
    rows = gate.shape[0]

    def body(gate_ref, up_ref, *refs):
        outs, (gates, ups, hidden, in_sems, out_sems) = refs[: len(parts)], refs[len(parts) :]

        def fetch(k, source, target, side):
            at = pl.ds((first + k) * STEP, STEP)
            return pltpu.make_async_copy(source.at[:, at], target.at[k], in_sems.at[side, k])

        for k in range(steps):
            fetch(k, gate_ref, gates, 0).start()
            fetch(k, up_ref, ups, 1).start()
        sent = []
        for k in range(steps):
            fetch(k, gate_ref, gates, 0).wait()
            fetch(k, up_ref, ups, 1).wait()
            value = gates[k].astype(jnp.float32)
            value = value / (1.0 + jnp.exp(-value)) * ups[k].astype(jnp.float32)
            hidden[k] = value.astype(jnp.bfloat16)
            for p, (a, b, s, e) in enumerate(parts):
                if s <= first + k < e:
                    copy = pltpu.make_async_copy(
                        hidden.at[k, pl.ds(a, b - a)],
                        outs[p].at[:, pl.ds((first + k - s) * STEP, STEP)],
                        out_sems.at[p, k],
                    )
                    copy.start()
                    sent.append(copy)
        for copy in sent:
            copy.wait()

    buffer = pltpu.VMEM((steps, rows, STEP), jnp.bfloat16)
    return chain.call(
        body,
        [gate, up],
        [ANY] * 2,
        [ANY] * len(parts),
        [jax.ShapeDtypeStruct((b - a, (e - s) * STEP), jnp.bfloat16) for a, b, s, e in parts],
        "activate",
        scratch=[buffer] * 3
        + [pltpu.SemaphoreType.DMA((2, steps)), pltpu.SemaphoreType.DMA((len(parts), steps))],
    )


def multiply(chain, chunks, weight, first, total, split, cost):
    counts = [piece.shape[0] for piece in chunks[0]]
    rows, cols = sum(counts), weight.shape[1]
    width = sum(pieces[0].shape[1] for pieces in chunks)
    steps, part = width // DEPTH, cols // sum(map(len, split or [(0,)]))
    flat, col = [], 0
    for pieces in chunks:
        row = 0
        for piece in pieces:
            flat.append((piece, row, col))
            row += piece.shape[0]
        col += pieces[0].shape[1]
    n_total = 0 if total is None else 1
    n_in = len(flat) + 1 + n_total
    shapes = [jax.ShapeDtypeStruct((len(flips), rows, part), jnp.bfloat16) for flips in split]
    if not split:
        shapes = [jax.ShapeDtypeStruct((rows, cols), jnp.float32)]

    def body(*refs):
        piece_refs, weight_ref = refs[: len(flat)], refs[len(flat)]
        total_refs, refs = refs[len(flat) + 1 : n_in], refs[n_in:]
        outs, (left, slots, *sums, sems, piece_sems) = refs[: len(shapes)], refs[len(shapes) :]
        sums = sums[0] if sums else outs[0]

        def fetch(k, slot):
            return pltpu.make_async_copy(
                weight_ref.at[pl.ds(first * STEP + k * DEPTH, DEPTH)], slots.at[slot], sems.at[slot]
            )

        for k in range(min(SLOTS, steps)):
            fetch(k, k).start()
        copies = [
            pltpu.make_async_copy(
                ref,
                left.at[pl.ds(row, piece.shape[0]), pl.ds(col, piece.shape[1])],
                piece_sems.at[n],
            )
            for n, (ref, (piece, row, col)) in enumerate(zip(piece_refs, flat))
        ]
        if n_total:
            copies.append(pltpu.make_async_copy(total_refs[0], sums, piece_sems.at[len(flat)]))
        for copy in copies:
            copy.start()
        if not n_total:
            sums[...] = jnp.zeros(sums.shape, sums.dtype)
        for copy in copies:
            copy.wait()

        def step(k, carry):
            slot = lax.rem(k, SLOTS)
            fetch(k, slot).wait()
            piece = left[:, pl.ds(pl.multiple_of(k * DEPTH, DEPTH), DEPTH)]
            for n in range(cols // TILE):
                at = pl.ds(n * TILE, TILE)
                sums[:, at] += jnp.dot(piece, slots[slot, :, at], preferred_element_type=jnp.float32)

            @pl.when(k + SLOTS < steps)
            def _():
                fetch(k + SLOTS, slot).start()

            return carry

        lax.fori_loop(0, steps, step, 0)
        for out, flips in zip(outs, split):
            for n, flip in enumerate(flips):
                at = pl.ds(pl.multiple_of((lax.axis_index("tp") ^ flip) * part, part), part)
                out[n] = sums[:, at].astype(jnp.bfloat16)

    return chain.call(
        body,
        [piece for piece, _, _ in flat] + [weight] + ([total] if n_total else []),
        [ANY] * n_in,
        [pl.BlockSpec(memory_space=pltpu.VMEM)] * len(shapes),
        shapes,
        "multiply",
        cost=cost,
        scratch=[pltpu.VMEM((rows, width), jnp.bfloat16), pltpu.VMEM((SLOTS, DEPTH, cols), jnp.bfloat16)]
        + ([pltpu.VMEM((rows, cols), jnp.float32)] if split else [])
        + [pltpu.SemaphoreType.DMA((SLOTS,)), pltpu.SemaphoreType.DMA((len(flat) + 1,))],
    )


def add(chain, parts, outs, cost=None):
    count = len(parts)

    def body(*refs):
        value = sum(ref[...].astype(jnp.float32) for ref in refs[:count]).astype(jnp.bfloat16)
        for ref, (n, a, b) in zip(refs[count:], outs):
            ref[0] = value[n, a:b]

    vmem = pl.BlockSpec(memory_space=pltpu.VMEM)
    shapes = [jax.ShapeDtypeStruct((1, b - a, parts[0].shape[2]), jnp.bfloat16) for _, a, b in outs]
    return chain.call(body, parts, [vmem] * count, [vmem] * len(outs), shapes, "add", cost=cost)


def join(chain, first, second, cost=None):
    n = first.shape[0]

    def body(first_ref, second_ref, out_ref):
        out_ref[:n] = first_ref[...]
        out_ref[n:] = second_ref[...]

    vmem = pl.BlockSpec(memory_space=pltpu.VMEM)
    shape = jax.ShapeDtypeStruct((n + second.shape[0],) + first.shape[1:], first.dtype)
    return chain.call(body, [first, second], [vmem] * 2, [vmem], [shape], "join", cost=cost)[0]


def encode_blocks(value, store, scales, first):
    lanes = lax.broadcasted_iota(jnp.int32, scales.shape, 1)
    for n in range(value.shape[1] // BLOCK):
        block = value[:, n * BLOCK : (n + 1) * BLOCK].astype(jnp.float32)
        scale = (jnp.max(jnp.abs(block), axis=1, keepdims=True) + EPSILON).astype(jnp.bfloat16)
        scale = scale.astype(jnp.float32)
        store(n, (block / scale).astype(jnp.bfloat16))
        scales = jnp.where(lanes == first + n, scale, scales)
    return scales


def encode_columns(chain, codes, scales, shares, away, start, height, width, last=False, cost=None):
    rows, part = shares[0][0].shape[1:]
    tp = len(shares)
    blocks, spread = part // BLOCK, tp * part
    given = [] if codes is None else [codes, scales]

    def body(*refs):
        share_refs = refs[len(given) : len(given) + tp]
        code_ref, scale_ref, buffer, table, sems = refs[len(given) + tp :]
        table[...] = refs[1][...] if given else jnp.zeros(table.shape, table.dtype)
        total = table[start : start + rows]
        copies = []
        for j in range(2):
            place = lax.axis_index("batch") ^ (j + away)
            for flip, (ref, (_, n)) in enumerate(zip(share_refs, shares)):
                t = lax.axis_index("tp") ^ flip

                def store(m, value):
                    at = pl.ds(pl.multiple_of((t * blocks + m) * BLOCK, BLOCK), BLOCK)
                    buffer[j, :, at] = value

                total = encode_blocks(ref[n + j], store, total, (place * tp + t) * blocks)
            columns = pl.ds(pl.multiple_of(place * spread, spread), spread)
            copy = pltpu.make_async_copy(
                buffer.at[j], code_ref.at[pl.ds(start, rows), columns], sems.at[j]
            )
            copy.start()
            copies.append(copy)
        table[start : start + rows] = total
        if last:
            scale_ref[...] = table[...].T[: width // BLOCK].astype(jnp.bfloat16)
        else:
            scale_ref[...] = table[...]
        for copy in copies:
            copy.wait()

    vmem = pl.BlockSpec(memory_space=pltpu.VMEM)
    kept = jax.ShapeDtypeStruct((height, LANES), jnp.float32)
    return chain.call(
        body,
        given + [array for array, _ in shares],
        [ANY, vmem][: len(given)] + [vmem] * tp,
        [ANY, vmem],
        [
            jax.ShapeDtypeStruct((height, width), jnp.bfloat16),
            jax.ShapeDtypeStruct((width // BLOCK, height), jnp.bfloat16) if last else kept,
        ],
        "encode",
        cost=cost,
        scratch=[
            pltpu.VMEM((2, rows, spread), jnp.bfloat16),
            pltpu.VMEM((height, LANES), jnp.float32),
            pltpu.SemaphoreType.DMA((2,)),
        ],
        aliases={0: 0} if given else {},
    )


DIRECT = [(0,), (1,), (2,), (3,)]
HALVES = [(0, 2), (1, 3)]


def paired_shards(gate_input, up_input, down_weight):
    rows, width = gate_input.shape
    tp, batch = lax.axis_size("tp"), lax.axis_size("batch")
    out_width = down_weight.shape[1] * batch
    cut = rows * EARLY // 8
    ends = [FIRST, FIRST + PIECE, FIRST + 2 * PIECE, FIRST + 3 * PIECE]
    spans = list(zip([0] + ends, ends))
    chain = Chain()

    def swap(value, flip):
        return lax.ppermute(value, "batch", [(b, b ^ flip) for b in range(batch)]) if flip else value

    def shift(value, flip):
        return lax.ppermute(value, "tp", [(t, t ^ flip) for t in range(tp)])

    def both_cores(piece, cost=None):
        piece = chain.pin(piece, cost)
        return [piece, swap(piece, 1)]

    def product(chunks, first, total, split=(), cost=None):
        outs = multiply(chain, chunks, down_weight, first, total, split, cost)
        return outs if split else outs[0]

    def sum_home(parts, away, cost=None):
        half = parts[0].shape[1] // 2
        ahead, behind = add(chain, parts, [(0, 0, half), (0, half, 2 * half)], cost)
        return swap(ahead, away), swap(behind, away + 1)

    def sum_pair(parts):
        keep, got = parts
        total = add(chain, [keep, got], [(0, 0, keep.shape[1]), (1, 0, keep.shape[1])])
        return [total[0], shift(total[1], 2)]

    near_0, send_0 = activate(
        chain, gate_input, up_input, 0, FIRST, [(0, rows, 0, FIRST), (0, cut, 0, FIRST)]
    )
    far_0 = swap(send_0, 2)
    pieces = activate(
        chain,
        gate_input,
        up_input,
        0,
        width // STEP,
        [(0, rows, a, b) for a, b in spans[1:]]
        + [(0, cut, a, b) for a, b in spans[1:]]
        + [(cut, rows, a, b) for a, b in [(0, ends[1]), (ends[1], ends[3])]],
    )
    near, early, late = [near_0] + pieces[:3], pieces[3:6], pieces[6:]
    near = [[h, swap(h, 1)] for h in near]
    far_0 = both_cores(far_0)
    far_1, far_2 = swap(early[0], 2), swap(early[1], 2)

    total = product(near[:2], 0, None)
    near = product(near[2:], ends[1], total, HALVES)
    near = [near[0], shift(near[1], 1)]

    far_1 = both_cores(far_1)
    far_3 = swap(chain.pin(early[2]), 2)
    total = product([far_0, far_1], 0, None)
    far_2 = both_cores(far_2)
    late_0 = swap(chain.pin(late[0]), 2)
    near = sum_pair(near)
    total = product([far_2], ends[1], total)
    far_3 = both_cores(far_3)
    late_1 = swap(chain.pin(late[1]), 2)
    far = product([far_3], ends[2], total, HALVES)
    far = [far[0], shift(far[1], 1)]
    near = sum_home(near, 0)

    late_0 = both_cores(late_0)
    near = join(chain, *near)
    near = [near, shift(near, 2)]
    total = product([late_0], 0, None)
    far = sum_pair(far)
    near.append(join(chain, *near))
    near[2] = shift(near[2], 1)
    late_1 = both_cores(late_1)
    last = product([late_1], ends[1], total, HALVES)
    last = [last[0], shift(last[1], 1)]
    far = sum_home(far, 2, 10**10)
    last = sum_pair(last)
    near = [(near[0], 0), (near[2], 0), (near[1], 0), (near[2], 2)]
    codes, scales = encode_columns(chain, None, None, near, 0, 0, rows, out_width, cost=10**10)
    last = sum_home(last, 2)
    far = join(chain, *far)
    far = [far, shift(far, 2)]
    last = join(chain, *last)
    last = [last] + [shift(last, flip) for flip in range(1, tp)]
    far.append(join(chain, *far))
    far[2] = shift(far[2], 1)
    far = [(far[0], 0), (far[2], 0), (far[1], 0), (far[2], 2)]
    codes, scales = encode_columns(chain, codes, scales, far, 2, 0, rows, out_width)
    last = [(array, 0) for array in last]
    codes, scales = encode_columns(chain, codes, scales, last, 2, cut, rows, out_width, True)
    return codes, scales.T


def solution(mesh):
    def shards(gate_input, up_input, down_weight):
        tp, batch = mesh.shape["tp"], mesh.shape["batch"]
        width, cols = down_weight.shape
        paired = batch == tp == 4 and batch * cols <= LANES * BLOCK and cols % (tp * TILE) == 0 and width == (FIRST + 3 * PIECE) * STEP
        return (paired_shards if paired else general_shards)(gate_input, up_input, down_weight)

    in_specs = (P(("groups", "batch"), "tp"), P(("groups", "batch"), "tp"), P("tp", "batch"))
    out_specs = (P(("groups", "batch"), None), P(("groups", "batch"), None))
    return jax.shard_map(shards, mesh=mesh, in_specs=in_specs, out_specs=out_specs, check_vma=False)
```

```python
import functools

import jax
import jax.numpy as jnp
from jax import lax
from jax.experimental import pallas as pl
from jax.experimental.pallas import tpu as pltpu
from jax.sharding import PartitionSpec as P

BLOCK = 128
EPSILON = 1e-06

STEP = 1024
PIECE = 4
DEPTH = 512
SLOTS = 6
TILE = 512
EARLY = 5
LANES = 128
VMEM = 32 * 2**20


def encode(values):
    leading = values.shape[:-1]
    blocks = values.reshape(leading + (values.shape[-1] // BLOCK, BLOCK))
    scales = (jnp.max(jnp.abs(blocks), axis=-1) + EPSILON).astype(jnp.bfloat16)
    widened = lax.optimization_barrier(scales).astype(jnp.float32)
    encoded = (blocks / widened[..., None]).astype(jnp.bfloat16)
    return (encoded.reshape(values.shape), scales)


def decode(encoded, scales):
    blocks = encoded.reshape(scales.shape + (BLOCK,)).astype(jnp.float32)
    return (blocks * scales.astype(jnp.float32)[..., None]).reshape(encoded.shape)


def general_shards(gate_input, up_input, down_weight):
    hidden = (jax.nn.silu(gate_input.astype(jnp.float32)) * up_input.astype(jnp.float32)).astype(
        jnp.bfloat16
    )
    partial_value = jnp.dot(
        lax.all_gather(hidden, "batch", axis=0, tiled=True),
        down_weight,
        preferred_element_type=jnp.float32,
    )
    part_codes, part_scales = encode(partial_value)
    tp_count = lax.axis_size("tp")
    batch_count = lax.axis_size("batch")
    row_count = hidden.shape[0]
    local_cols = partial_value.shape[1]
    local_blocks = part_scales.shape[1]
    row_share = row_count // tp_count
    got_codes, got_scales = (
        lax.all_to_all(
            part_codes.reshape(batch_count, tp_count, row_share, local_cols),
            "tp",
            split_axis=1,
            concat_axis=1,
            tiled=True,
        ),
        lax.all_to_all(
            part_scales.reshape(batch_count, tp_count, row_share, local_blocks),
            "tp",
            split_axis=1,
            concat_axis=1,
            tiled=True,
        ),
    )
    summed = jnp.sum(decode(got_codes, got_scales), axis=1)
    new_codes, new_scales = encode(summed)
    home_codes, home_scales = (
        lax.all_to_all(new_codes, "batch", split_axis=0, concat_axis=2, tiled=True),
        lax.all_to_all(new_scales, "batch", split_axis=0, concat_axis=2, tiled=True),
    )
    out_codes, out_scales = (
        lax.all_gather(home_codes, "tp", axis=1, tiled=True),
        lax.all_gather(home_scales, "tp", axis=1, tiled=True),
    )
    return (out_codes.reshape(row_count, -1), out_scales.reshape(row_count, -1))


ANY = pl.BlockSpec(memory_space=pl.ANY)
WEIGHTS = {"activate": 10**10, "multiply": 10**10, "pin": 10**10, "add": 0, "join": 0, "encode": 0}


TOKEN = (8, 128)


def large(value):
    return value.size * value.dtype.itemsize > 3 * 2**20


class Chain:
    def __init__(self):
        self.tokens = []

    def call(self, body, operands, in_specs, out_specs, out_shape, name, grid=(), scratch=(), aliases=None, cost=None):
        count, n_tokens, n_outs = len(operands), len(self.tokens), len(out_shape)

        def with_tokens(*refs):
            outs = count + n_tokens
            body(*refs[:count], *refs[outs : outs + n_outs], *refs[outs + n_outs + 1 :])

        operands = [
            pltpu.with_memory_space_constraint(value, pltpu.HBM) if large(value) else value
            for value in operands
        ]
        outs = pl.pallas_call(
            with_tokens,
            grid=grid,
            in_specs=list(in_specs) + [ANY] * n_tokens,
            out_specs=list(out_specs) + [ANY],
            out_shape=list(out_shape) + [jax.ShapeDtypeStruct(TOKEN, jnp.float32)],
            scratch_shapes=scratch,
            input_output_aliases=aliases or {},
            compiler_params=pltpu.CompilerParams(vmem_limit_bytes=VMEM),
            cost_estimate=pl.CostEstimate(
                flops=WEIGHTS[name] if cost is None else cost, bytes_accessed=1024, transcendentals=0
            ),
            name=name,
        )(*operands, *self.tokens)
        self.tokens = [outs[-1]]
        return list(outs[:-1])

    def pin(self, value, cost=None):
        pinned = self.call(
            lambda *refs: None,
            [value],
            [ANY],
            [ANY],
            [jax.ShapeDtypeStruct(value.shape, value.dtype)],
            "pin",
            aliases={0: 0},
            cost=cost,
        )
        return pinned[0]


def activate(chain, gate, up, first, steps, parts):
    rows = gate.shape[0]

    def body(gate_ref, up_ref, *refs):
        outs, (gates, ups, hidden, in_sems, out_sems) = refs[: len(parts)], refs[len(parts) :]

        def fetch(k, source, target, side):
            at = pl.ds((first + k) * STEP, STEP)
            return pltpu.make_async_copy(source.at[:, at], target.at[k], in_sems.at[side, k])

        for k in range(steps):
            fetch(k, gate_ref, gates, 0).start()
            fetch(k, up_ref, ups, 1).start()
        sent = []
        for k in range(steps):
            fetch(k, gate_ref, gates, 0).wait()
            fetch(k, up_ref, ups, 1).wait()
            value = gates[k].astype(jnp.float32)
            value = value / (1.0 + jnp.exp(-value)) * ups[k].astype(jnp.float32)
            hidden[k] = value.astype(jnp.bfloat16)
            for p, (a, b, s, e) in enumerate(parts):
                if s <= first + k < e:
                    copy = pltpu.make_async_copy(
                        hidden.at[k, pl.ds(a, b - a)],
                        outs[p].at[:, pl.ds((first + k - s) * STEP, STEP)],
                        out_sems.at[p, k],
                    )
                    copy.start()
                    sent.append(copy)
        for copy in sent:
            copy.wait()

    buffer = pltpu.VMEM((steps, rows, STEP), jnp.bfloat16)
    return chain.call(
        body,
        [gate, up],
        [ANY] * 2,
        [ANY] * len(parts),
        [jax.ShapeDtypeStruct((b - a, (e - s) * STEP), jnp.bfloat16) for a, b, s, e in parts],
        "activate",
        scratch=[buffer] * 3
        + [pltpu.SemaphoreType.DMA((2, steps)), pltpu.SemaphoreType.DMA((len(parts), steps))],
    )


def multiply(chain, chunks, weight, first, total, split, cost):
    counts = [piece.shape[0] for piece in chunks[0]]
    rows, cols = sum(counts), weight.shape[1]
    width = sum(pieces[0].shape[1] for pieces in chunks)
    steps, part = width // DEPTH, cols // sum(map(len, split or [(0,)]))
    flat, col = [], 0
    for pieces in chunks:
        row = 0
        for piece in pieces:
            flat.append((piece, row, col))
            row += piece.shape[0]
        col += pieces[0].shape[1]
    n_total = 0 if total is None else 1
    n_in = len(flat) + 1 + n_total
    shapes = [jax.ShapeDtypeStruct((len(flips), rows, part), jnp.bfloat16) for flips in split]
    if not split:
        shapes = [jax.ShapeDtypeStruct((rows, cols), jnp.float32)]

    def body(*refs):
        piece_refs, weight_ref = refs[: len(flat)], refs[len(flat)]
        total_refs, refs = refs[len(flat) + 1 : n_in], refs[n_in:]
        outs, (left, slots, *sums, sems, piece_sems) = refs[: len(shapes)], refs[len(shapes) :]
        sums = sums[0] if sums else outs[0]

        def fetch(k, slot):
            return pltpu.make_async_copy(
                weight_ref.at[pl.ds(first * STEP + k * DEPTH, DEPTH)], slots.at[slot], sems.at[slot]
            )

        for k in range(min(SLOTS, steps)):
            fetch(k, k).start()
        copies = [
            pltpu.make_async_copy(
                ref,
                left.at[pl.ds(row, piece.shape[0]), pl.ds(col, piece.shape[1])],
                piece_sems.at[n],
            )
            for n, (ref, (piece, row, col)) in enumerate(zip(piece_refs, flat))
        ]
        if n_total:
            copies.append(pltpu.make_async_copy(total_refs[0], sums, piece_sems.at[len(flat)]))
        for copy in copies:
            copy.start()
        if not n_total:
            sums[...] = jnp.zeros(sums.shape, sums.dtype)
        for copy in copies:
            copy.wait()

        def step(k, carry):
            slot = lax.rem(k, SLOTS)
            fetch(k, slot).wait()
            piece = left[:, pl.ds(pl.multiple_of(k * DEPTH, DEPTH), DEPTH)]
            for n in range(cols // TILE):
                at = pl.ds(n * TILE, TILE)
                sums[:, at] += jnp.dot(piece, slots[slot, :, at], preferred_element_type=jnp.float32)

            @pl.when(k + SLOTS < steps)
            def _():
                fetch(k + SLOTS, slot).start()

            return carry

        lax.fori_loop(0, steps, step, 0)
        for out, flips in zip(outs, split):
            for n, flip in enumerate(flips):
                at = pl.ds(pl.multiple_of((lax.axis_index("tp") ^ flip) * part, part), part)
                out[n] = sums[:, at].astype(jnp.bfloat16)

    return chain.call(
        body,
        [piece for piece, _, _ in flat] + [weight] + ([total] if n_total else []),
        [ANY] * n_in,
        [pl.BlockSpec(memory_space=pltpu.VMEM)] * len(shapes),
        shapes,
        "multiply",
        cost=cost,
        scratch=[pltpu.VMEM((rows, width), jnp.bfloat16), pltpu.VMEM((SLOTS, DEPTH, cols), jnp.bfloat16)]
        + ([pltpu.VMEM((rows, cols), jnp.float32)] if split else [])
        + [pltpu.SemaphoreType.DMA((SLOTS,)), pltpu.SemaphoreType.DMA((len(flat) + 1,))],
    )


def add(chain, parts, outs, cost=None):
    count = len(parts)

    def body(*refs):
        value = sum(ref[...].astype(jnp.float32) for ref in refs[:count]).astype(jnp.bfloat16)
        for ref, (n, a, b) in zip(refs[count:], outs):
            ref[0] = value[n, a:b]

    vmem = pl.BlockSpec(memory_space=pltpu.VMEM)
    shapes = [jax.ShapeDtypeStruct((1, b - a, parts[0].shape[2]), jnp.bfloat16) for _, a, b in outs]
    return chain.call(body, parts, [vmem] * count, [vmem] * len(outs), shapes, "add", cost=cost)


def join(chain, first, second, cost=None):
    n = first.shape[0]

    def body(first_ref, second_ref, out_ref):
        out_ref[:n] = first_ref[...]
        out_ref[n:] = second_ref[...]

    vmem = pl.BlockSpec(memory_space=pltpu.VMEM)
    shape = jax.ShapeDtypeStruct((n + second.shape[0],) + first.shape[1:], first.dtype)
    return chain.call(body, [first, second], [vmem] * 2, [vmem], [shape], "join", cost=cost)[0]


def encode_blocks(value, store, scales, first):
    lanes = lax.broadcasted_iota(jnp.int32, scales.shape, 1)
    for n in range(value.shape[1] // BLOCK):
        block = value[:, n * BLOCK : (n + 1) * BLOCK].astype(jnp.float32)
        scale = (jnp.max(jnp.abs(block), axis=1, keepdims=True) + EPSILON).astype(jnp.bfloat16)
        scale = scale.astype(jnp.float32)
        store(n, (block / scale).astype(jnp.bfloat16))
        scales = jnp.where(lanes == first + n, scale, scales)
    return scales


def encode_columns(chain, codes, scales, shares, away, start, height, width, last=False, cost=None):
    rows, part = shares[0][0].shape[1:]
    tp = len(shares)
    blocks, spread = part // BLOCK, tp * part
    given = [] if codes is None else [codes, scales]

    def body(*refs):
        share_refs = refs[len(given) : len(given) + tp]
        code_ref, scale_ref, buffer, table, sems = refs[len(given) + tp :]
        table[...] = refs[1][...] if given else jnp.zeros(table.shape, table.dtype)
        total = table[start : start + rows]
        copies = []
        for j in range(2):
            place = lax.axis_index("batch") ^ (j + away)
            for flip, (ref, (_, n)) in enumerate(zip(share_refs, shares)):
                t = lax.axis_index("tp") ^ flip

                def store(m, value):
                    at = pl.ds(pl.multiple_of((t * blocks + m) * BLOCK, BLOCK), BLOCK)
                    buffer[j, :, at] = value

                total = encode_blocks(ref[n + j], store, total, (place * tp + t) * blocks)
            columns = pl.ds(pl.multiple_of(place * spread, spread), spread)
            copy = pltpu.make_async_copy(
                buffer.at[j], code_ref.at[pl.ds(start, rows), columns], sems.at[j]
            )
            copy.start()
            copies.append(copy)
        table[start : start + rows] = total
        if last:
            scale_ref[...] = table[...].T[: width // BLOCK].astype(jnp.bfloat16)
        else:
            scale_ref[...] = table[...]
        for copy in copies:
            copy.wait()

    vmem = pl.BlockSpec(memory_space=pltpu.VMEM)
    kept = jax.ShapeDtypeStruct((height, LANES), jnp.float32)
    return chain.call(
        body,
        given + [array for array, _ in shares],
        [ANY, vmem][: len(given)] + [vmem] * tp,
        [ANY, vmem],
        [
            jax.ShapeDtypeStruct((height, width), jnp.bfloat16),
            jax.ShapeDtypeStruct((width // BLOCK, height), jnp.bfloat16) if last else kept,
        ],
        "encode",
        cost=cost,
        scratch=[
            pltpu.VMEM((2, rows, spread), jnp.bfloat16),
            pltpu.VMEM((height, LANES), jnp.float32),
            pltpu.SemaphoreType.DMA((2,)),
        ],
        aliases={0: 0} if given else {},
    )


DIRECT = [(0,), (1,), (2,), (3,)]
HALVES = [(0, 2), (1, 3)]


def paired_shards(gate_input, up_input, down_weight):
    rows, width = gate_input.shape
    tp, batch = lax.axis_size("tp"), lax.axis_size("batch")
    out_width = down_weight.shape[1] * batch
    cut = rows * EARLY // 8
    steps = width // STEP
    first, middle = steps - 2 * PIECE, steps - PIECE
    half = steps // 2
    chain = Chain()

    def swap(value, flip):
        return lax.ppermute(value, "batch", [(b, b ^ flip) for b in range(batch)]) if flip else value

    def shift(value, flip):
        return lax.ppermute(value, "tp", [(t, t ^ flip) for t in range(tp)])

    def both_cores(piece, cost=None):
        piece = chain.pin(piece, cost)
        return [piece, swap(piece, 1)]

    def product(chunks, first, total, split=(), cost=None):
        outs = multiply(chain, chunks, down_weight, first, total, split, cost)
        return outs if split else outs[0]

    def sum_home(parts, away, cost=None):
        half = parts[0].shape[1] // 2
        ahead, behind = add(chain, parts, [(0, 0, half), (0, half, 2 * half)], cost)
        return swap(ahead, away), swap(behind, away + 1)

    def sum_pair(parts):
        keep, got = parts
        total = add(chain, [keep, got], [(0, 0, keep.shape[1]), (1, 0, keep.shape[1])])
        return [total[0], shift(total[1], 2)]

    near_0, near_1, far_0, far_1, far_2, late_0, late_1 = activate(
        chain,
        gate_input,
        up_input,
        0,
        steps,
        [(0, rows, 0, first), (0, rows, first, steps)]
        + [(0, cut, 0, first), (0, cut, first, middle), (0, cut, middle, steps)]
        + [(cut, rows, 0, half), (cut, rows, half, steps)],
    )
    far_0 = swap(far_0, 2)
    near_0, near_1 = [near_0, swap(near_0, 1)], [near_1, swap(near_1, 1)]

    total = product([near_0], 0, None)
    far_1 = swap(chain.pin(far_1), 2)
    near = product([near_1], first, total, HALVES)
    near = [near[0], shift(near[1], 1)]

    far_0 = both_cores(far_0)
    far_2 = swap(chain.pin(far_2), 2)
    total = product([far_0], 0, None)
    far_1 = both_cores(far_1)
    late_0 = swap(chain.pin(late_0), 2)
    near = sum_pair(near)
    total = product([far_1], first, total)
    far_2 = both_cores(far_2)
    late_1 = swap(chain.pin(late_1), 2)
    far = product([far_2], middle, total, HALVES)
    far = [far[0], shift(far[1], 1)]
    near = sum_home(near, 0)

    late_0 = both_cores(late_0)
    near = join(chain, *near)
    near = [near, shift(near, 2)]
    total = product([late_0], 0, None)
    far = sum_pair(far)
    near.append(join(chain, *near))
    near[2] = shift(near[2], 1)
    late_1 = both_cores(late_1)
    last = product([late_1], half, total, HALVES)
    last = [last[0], shift(last[1], 1)]
    far = sum_home(far, 2, 10**10)
    last = sum_pair(last)
    near = [(near[0], 0), (near[2], 0), (near[1], 0), (near[2], 2)]
    codes, scales = encode_columns(chain, None, None, near, 0, 0, rows, out_width, cost=10**10)
    far = join(chain, *far)
    far = [far, shift(far, 2)]
    last = sum_home(last, 2)
    far.append(join(chain, *far))
    far[2] = shift(far[2], 1)
    last = join(chain, *last)
    last = [last] + [shift(last, flip) for flip in range(1, tp)]
    far = [(far[0], 0), (far[2], 0), (far[1], 0), (far[2], 2)]
    codes, scales = encode_columns(chain, codes, scales, far, 2, 0, rows, out_width)
    last = [(array, 0) for array in last]
    codes, scales = encode_columns(chain, codes, scales, last, 2, cut, rows, out_width, True)
    return codes, scales.T


def solution(mesh):
    def shards(gate_input, up_input, down_weight):
        tp, batch = mesh.shape["tp"], mesh.shape["batch"]
        width, cols = down_weight.shape
        paired = batch == tp == 4 and batch * cols <= LANES * BLOCK and cols % (tp * TILE) == 0 and width % STEP == 0 and width > 2 * PIECE * STEP
        return (paired_shards if paired else general_shards)(gate_input, up_input, down_weight)

    in_specs = (P(("groups", "batch"), "tp"), P(("groups", "batch"), "tp"), P("tp", "batch"))
    out_specs = (P(("groups", "batch"), None), P(("groups", "batch"), None))
    return jax.shard_map(shards, mesh=mesh, in_specs=in_specs, out_specs=out_specs, check_vma=False)
```

```python
import functools

import jax
import jax.numpy as jnp
from jax import lax
from jax.experimental import pallas as pl
from jax.experimental.pallas import tpu as pltpu
from jax.sharding import PartitionSpec as P

BLOCK = 128
EPSILON = 1e-06

STEP = 1024
PIECE = 4
DEPTH = 512
SLOTS = 6
TILE = 512
EARLY = 5
LANES = 128
VMEM = 32 * 2**20


def encode(values):
    leading = values.shape[:-1]
    blocks = values.reshape(leading + (values.shape[-1] // BLOCK, BLOCK))
    scales = (jnp.max(jnp.abs(blocks), axis=-1) + EPSILON).astype(jnp.bfloat16)
    widened = lax.optimization_barrier(scales).astype(jnp.float32)
    encoded = (blocks / widened[..., None]).astype(jnp.bfloat16)
    return (encoded.reshape(values.shape), scales)


def decode(encoded, scales):
    blocks = encoded.reshape(scales.shape + (BLOCK,)).astype(jnp.float32)
    return (blocks * scales.astype(jnp.float32)[..., None]).reshape(encoded.shape)


def general_shards(gate_input, up_input, down_weight):
    hidden = (jax.nn.silu(gate_input.astype(jnp.float32)) * up_input.astype(jnp.float32)).astype(
        jnp.bfloat16
    )
    partial_value = jnp.dot(
        lax.all_gather(hidden, "batch", axis=0, tiled=True),
        down_weight,
        preferred_element_type=jnp.float32,
    )
    part_codes, part_scales = encode(partial_value)
    tp_count = lax.axis_size("tp")
    batch_count = lax.axis_size("batch")
    row_count = hidden.shape[0]
    local_cols = partial_value.shape[1]
    local_blocks = part_scales.shape[1]
    row_share = row_count // tp_count
    got_codes, got_scales = (
        lax.all_to_all(
            part_codes.reshape(batch_count, tp_count, row_share, local_cols),
            "tp",
            split_axis=1,
            concat_axis=1,
            tiled=True,
        ),
        lax.all_to_all(
            part_scales.reshape(batch_count, tp_count, row_share, local_blocks),
            "tp",
            split_axis=1,
            concat_axis=1,
            tiled=True,
        ),
    )
    summed = jnp.sum(decode(got_codes, got_scales), axis=1)
    new_codes, new_scales = encode(summed)
    home_codes, home_scales = (
        lax.all_to_all(new_codes, "batch", split_axis=0, concat_axis=2, tiled=True),
        lax.all_to_all(new_scales, "batch", split_axis=0, concat_axis=2, tiled=True),
    )
    out_codes, out_scales = (
        lax.all_gather(home_codes, "tp", axis=1, tiled=True),
        lax.all_gather(home_scales, "tp", axis=1, tiled=True),
    )
    return (out_codes.reshape(row_count, -1), out_scales.reshape(row_count, -1))


ANY = pl.BlockSpec(memory_space=pl.ANY)
WEIGHTS = {"activate": 10**10, "multiply": 10**10, "pin": 10**10, "add": 0, "join": 0, "encode": 0}


TOKEN = (8, 128)


def large(value):
    return value.size * value.dtype.itemsize > 3 * 2**20


class Chain:
    def __init__(self):
        self.tokens = []

    def call(self, body, operands, in_specs, out_specs, out_shape, name, grid=(), scratch=(), aliases=None, cost=None):
        count, n_tokens, n_outs = len(operands), len(self.tokens), len(out_shape)

        def with_tokens(*refs):
            outs = count + n_tokens
            body(*refs[:count], *refs[outs : outs + n_outs], *refs[outs + n_outs + 1 :])

        operands = [
            pltpu.with_memory_space_constraint(value, pltpu.HBM) if large(value) else value
            for value in operands
        ]
        outs = pl.pallas_call(
            with_tokens,
            grid=grid,
            in_specs=list(in_specs) + [ANY] * n_tokens,
            out_specs=list(out_specs) + [ANY],
            out_shape=list(out_shape) + [jax.ShapeDtypeStruct(TOKEN, jnp.float32)],
            scratch_shapes=scratch,
            input_output_aliases=aliases or {},
            compiler_params=pltpu.CompilerParams(vmem_limit_bytes=VMEM),
            cost_estimate=pl.CostEstimate(
                flops=WEIGHTS[name] if cost is None else cost, bytes_accessed=1024, transcendentals=0
            ),
            name=name,
        )(*operands, *self.tokens)
        self.tokens = [outs[-1]]
        return list(outs[:-1])

    def pin(self, value, cost=None):
        pinned = self.call(
            lambda *refs: None,
            [value],
            [ANY],
            [ANY],
            [jax.ShapeDtypeStruct(value.shape, value.dtype)],
            "pin",
            aliases={0: 0},
            cost=cost,
        )
        return pinned[0]


def activate(chain, gate, up, first, steps, parts):
    rows = gate.shape[0]

    def body(gate_ref, up_ref, *refs):
        outs, (gates, ups, hidden, in_sems, out_sems) = refs[: len(parts)], refs[len(parts) :]

        def fetch(k, source, target, side):
            at = pl.ds((first + k) * STEP, STEP)
            return pltpu.make_async_copy(source.at[:, at], target.at[k], in_sems.at[side, k])

        for k in range(steps):
            fetch(k, gate_ref, gates, 0).start()
            fetch(k, up_ref, ups, 1).start()
        sent = []
        for k in range(steps):
            fetch(k, gate_ref, gates, 0).wait()
            fetch(k, up_ref, ups, 1).wait()
            value = gates[k].astype(jnp.float32)
            value = value / (1.0 + jnp.exp(-value)) * ups[k].astype(jnp.float32)
            hidden[k] = value.astype(jnp.bfloat16)
            for p, (a, b, s, e) in enumerate(parts):
                if s <= first + k < e:
                    copy = pltpu.make_async_copy(
                        hidden.at[k, pl.ds(a, b - a)],
                        outs[p].at[:, pl.ds((first + k - s) * STEP, STEP)],
                        out_sems.at[p, k],
                    )
                    copy.start()
                    sent.append(copy)
        for copy in sent:
            copy.wait()

    buffer = pltpu.VMEM((steps, rows, STEP), jnp.bfloat16)
    return chain.call(
        body,
        [gate, up],
        [ANY] * 2,
        [ANY] * len(parts),
        [jax.ShapeDtypeStruct((b - a, (e - s) * STEP), jnp.bfloat16) for a, b, s, e in parts],
        "activate",
        scratch=[buffer] * 3
        + [pltpu.SemaphoreType.DMA((2, steps)), pltpu.SemaphoreType.DMA((len(parts), steps))],
    )


def multiply(chain, chunks, weight, first, total, split, cost):
    counts = [piece.shape[0] for piece in chunks[0]]
    rows, cols = sum(counts), weight.shape[1]
    width = sum(pieces[0].shape[1] for pieces in chunks)
    steps, part = width // DEPTH, cols // sum(map(len, split or [(0,)]))
    flat, col = [], 0
    for pieces in chunks:
        row = 0
        for piece in pieces:
            flat.append((piece, row, col))
            row += piece.shape[0]
        col += pieces[0].shape[1]
    n_total = 0 if total is None else 1
    n_in = len(flat) + 1 + n_total
    shapes = [jax.ShapeDtypeStruct((len(flips), rows, part), jnp.bfloat16) for flips in split]
    if not split:
        shapes = [jax.ShapeDtypeStruct((rows, cols), jnp.float32)]

    def body(*refs):
        piece_refs, weight_ref = refs[: len(flat)], refs[len(flat)]
        total_refs, refs = refs[len(flat) + 1 : n_in], refs[n_in:]
        outs, (left, slots, *sums, sems, piece_sems) = refs[: len(shapes)], refs[len(shapes) :]
        sums = sums[0] if sums else outs[0]

        def fetch(k, slot):
            return pltpu.make_async_copy(
                weight_ref.at[pl.ds(first * STEP + k * DEPTH, DEPTH)], slots.at[slot], sems.at[slot]
            )

        for k in range(min(SLOTS, steps)):
            fetch(k, k).start()
        copies = [
            pltpu.make_async_copy(
                ref,
                left.at[pl.ds(row, piece.shape[0]), pl.ds(col, piece.shape[1])],
                piece_sems.at[n],
            )
            for n, (ref, (piece, row, col)) in enumerate(zip(piece_refs, flat))
        ]
        if n_total:
            copies.append(pltpu.make_async_copy(total_refs[0], sums, piece_sems.at[len(flat)]))
        for copy in copies:
            copy.start()
        if not n_total:
            sums[...] = jnp.zeros(sums.shape, sums.dtype)
        for copy in copies:
            copy.wait()

        def step(k, carry):
            slot = lax.rem(k, SLOTS)
            fetch(k, slot).wait()
            piece = left[:, pl.ds(pl.multiple_of(k * DEPTH, DEPTH), DEPTH)]
            for n in range(cols // TILE):
                at = pl.ds(n * TILE, TILE)
                sums[:, at] += jnp.dot(piece, slots[slot, :, at], preferred_element_type=jnp.float32)

            @pl.when(k + SLOTS < steps)
            def _():
                fetch(k + SLOTS, slot).start()

            return carry

        lax.fori_loop(0, steps, step, 0)
        for out, flips in zip(outs, split):
            for n, flip in enumerate(flips):
                at = pl.ds(pl.multiple_of((lax.axis_index("tp") ^ flip) * part, part), part)
                out[n] = sums[:, at].astype(jnp.bfloat16)

    return chain.call(
        body,
        [piece for piece, _, _ in flat] + [weight] + ([total] if n_total else []),
        [ANY] * n_in,
        [pl.BlockSpec(memory_space=pltpu.VMEM)] * len(shapes),
        shapes,
        "multiply",
        cost=cost,
        scratch=[pltpu.VMEM((rows, width), jnp.bfloat16), pltpu.VMEM((SLOTS, DEPTH, cols), jnp.bfloat16)]
        + ([pltpu.VMEM((rows, cols), jnp.float32)] if split else [])
        + [pltpu.SemaphoreType.DMA((SLOTS,)), pltpu.SemaphoreType.DMA((len(flat) + 1,))],
    )


def add(chain, parts, outs, cost=None):
    count = len(parts)

    def body(*refs):
        value = sum(ref[...].astype(jnp.float32) for ref in refs[:count]).astype(jnp.bfloat16)
        for ref, (n, a, b) in zip(refs[count:], outs):
            ref[0] = value[n, a:b]

    vmem = pl.BlockSpec(memory_space=pltpu.VMEM)
    shapes = [jax.ShapeDtypeStruct((1, b - a, parts[0].shape[2]), jnp.bfloat16) for _, a, b in outs]
    return chain.call(body, parts, [vmem] * count, [vmem] * len(outs), shapes, "add", cost=cost)


def join(chain, first, second, cost=None):
    n = first.shape[0]

    def body(first_ref, second_ref, out_ref):
        out_ref[:n] = first_ref[...]
        out_ref[n:] = second_ref[...]

    vmem = pl.BlockSpec(memory_space=pltpu.VMEM)
    shape = jax.ShapeDtypeStruct((n + second.shape[0],) + first.shape[1:], first.dtype)
    return chain.call(body, [first, second], [vmem] * 2, [vmem], [shape], "join", cost=cost)[0]


def encode_blocks(value, store, scales, first):
    lanes = lax.broadcasted_iota(jnp.int32, scales.shape, 1)
    for n in range(value.shape[1] // BLOCK):
        block = value[:, n * BLOCK : (n + 1) * BLOCK].astype(jnp.float32)
        scale = (jnp.max(jnp.abs(block), axis=1, keepdims=True) + EPSILON).astype(jnp.bfloat16)
        scale = scale.astype(jnp.float32)
        store(n, (block / scale).astype(jnp.bfloat16))
        scales = jnp.where(lanes == first + n, scale, scales)
    return scales


def encode_columns(chain, codes, scales, shares, away, start, height, width, last=False, cost=None):
    rows, part = shares[0][0].shape[1:]
    tp = len(shares)
    blocks, spread = part // BLOCK, tp * part
    given = [] if codes is None else [codes, scales]

    def body(*refs):
        share_refs = refs[len(given) : len(given) + tp]
        code_ref, scale_ref, buffer, table, sems = refs[len(given) + tp :]
        table[...] = refs[1][...] if given else jnp.zeros(table.shape, table.dtype)
        total = table[start : start + rows]
        copies = []
        for j in range(2):
            place = lax.axis_index("batch") ^ (j + away)
            for flip, (ref, (_, n)) in enumerate(zip(share_refs, shares)):
                t = lax.axis_index("tp") ^ flip

                def store(m, value):
                    at = pl.ds(pl.multiple_of((t * blocks + m) * BLOCK, BLOCK), BLOCK)
                    buffer[j, :, at] = value

                total = encode_blocks(ref[n + j], store, total, (place * tp + t) * blocks)
            columns = pl.ds(pl.multiple_of(place * spread, spread), spread)
            copy = pltpu.make_async_copy(
                buffer.at[j], code_ref.at[pl.ds(start, rows), columns], sems.at[j]
            )
            copy.start()
            copies.append(copy)
        table[start : start + rows] = total
        if last:
            scale_ref[...] = table[...].T[: width // BLOCK].astype(jnp.bfloat16)
        else:
            scale_ref[...] = table[...]
        for copy in copies:
            copy.wait()

    vmem = pl.BlockSpec(memory_space=pltpu.VMEM)
    kept = jax.ShapeDtypeStruct((height, LANES), jnp.float32)
    return chain.call(
        body,
        given + [array for array, _ in shares],
        [ANY, vmem][: len(given)] + [vmem] * tp,
        [ANY, vmem],
        [
            jax.ShapeDtypeStruct((height, width), jnp.bfloat16),
            jax.ShapeDtypeStruct((width // BLOCK, height), jnp.bfloat16) if last else kept,
        ],
        "encode",
        cost=cost,
        scratch=[
            pltpu.VMEM((2, rows, spread), jnp.bfloat16),
            pltpu.VMEM((height, LANES), jnp.float32),
            pltpu.SemaphoreType.DMA((2,)),
        ],
        aliases={0: 0} if given else {},
    )


DIRECT = [(0,), (1,), (2,), (3,)]
HALVES = [(0, 2), (1, 3)]


def paired_shards(gate_input, up_input, down_weight):
    rows, width = gate_input.shape
    tp, batch = lax.axis_size("tp"), lax.axis_size("batch")
    out_width = down_weight.shape[1] * batch
    cut = rows * EARLY // 8
    steps = width // STEP
    first, middle = steps - 2 * PIECE, steps - PIECE
    half = steps // 2
    chain = Chain()

    def swap(value, flip):
        return lax.ppermute(value, "batch", [(b, b ^ flip) for b in range(batch)]) if flip else value

    def shift(value, flip):
        return lax.ppermute(value, "tp", [(t, t ^ flip) for t in range(tp)])

    def both_cores(piece, cost=None):
        piece = chain.pin(piece, cost)
        return [piece, swap(piece, 1)]

    def product(chunks, first, total, split=(), cost=None):
        outs = multiply(chain, chunks, down_weight, first, total, split, cost)
        return outs if split else outs[0]

    def sum_home(parts, away, cost=None):
        half = parts[0].shape[1] // 2
        ahead, behind = add(chain, parts, [(0, 0, half), (0, half, 2 * half)], cost)
        return swap(ahead, away), swap(behind, away + 1)

    def sum_pair(parts):
        keep, got = parts
        total = add(chain, [keep, got], [(0, 0, keep.shape[1]), (1, 0, keep.shape[1])])
        return [total[0], shift(total[1], 2)]

    near_0, near_1, far_0, far_1, far_2, late_0, late_1 = activate(
        chain,
        gate_input,
        up_input,
        0,
        steps,
        [(0, rows, 0, first), (0, rows, first, steps)]
        + [(0, cut, 0, first), (0, cut, first, middle), (0, cut, middle, steps)]
        + [(cut, rows, 0, half), (cut, rows, half, steps)],
    )
    far_0 = swap(far_0, 2)
    near_0, near_1 = [near_0, swap(near_0, 1)], [near_1, swap(near_1, 1)]

    total = product([near_0], 0, None)
    far_1 = swap(chain.pin(far_1), 2)
    near = product([near_1], first, total, HALVES)
    near = [near[0], shift(near[1], 1)]

    far_0 = both_cores(far_0)
    far_2 = swap(chain.pin(far_2), 2)
    total = product([far_0], 0, None)
    far_1 = both_cores(far_1)
    late_0 = swap(chain.pin(late_0), 2)
    near = sum_pair(near)
    total = product([far_1], first, total)
    far_2 = both_cores(far_2)
    late_1 = swap(chain.pin(late_1), 2)
    far = product([far_2], middle, total, HALVES)
    far = [far[0], shift(far[1], 1)]
    near = sum_home(near, 0)

    late_0 = both_cores(late_0)
    near = join(chain, *near)
    near = [near, shift(near, 2)]
    total = product([late_0], 0, None)
    far = sum_pair(far)
    near.append(join(chain, *near))
    near[2] = shift(near[2], 1)
    late_1 = both_cores(late_1)
    last = product([late_1], half, total, HALVES)
    last = [last[0], shift(last[1], 1)]
    far = sum_home(far, 2, 10**10)
    far = join(chain, *far)
    far = [far, shift(far, 2)]
    last = sum_pair(last)
    near = [(near[0], 0), (near[2], 0), (near[1], 0), (near[2], 2)]
    codes, scales = encode_columns(chain, None, None, near, 0, 0, rows, out_width, cost=10**10)
    last = sum_home(last, 2)
    far.append(join(chain, *far))
    far[2] = shift(far[2], 1)
    last = join(chain, *last)
    last = [last] + [shift(last, flip) for flip in range(1, tp)]
    far = [(far[0], 0), (far[2], 0), (far[1], 0), (far[2], 2)]
    codes, scales = encode_columns(chain, codes, scales, far, 2, 0, rows, out_width)
    last = [(array, 0) for array in last]
    codes, scales = encode_columns(chain, codes, scales, last, 2, cut, rows, out_width, True)
    return codes, scales.T


def solution(mesh):
    def shards(gate_input, up_input, down_weight):
        tp, batch = mesh.shape["tp"], mesh.shape["batch"]
        width, cols = down_weight.shape
        paired = batch == tp == 4 and batch * cols <= LANES * BLOCK and cols % (tp * TILE) == 0 and width % STEP == 0 and width > 2 * PIECE * STEP
        return (paired_shards if paired else general_shards)(gate_input, up_input, down_weight)

    in_specs = (P(("groups", "batch"), "tp"), P(("groups", "batch"), "tp"), P("tp", "batch"))
    out_specs = (P(("groups", "batch"), None), P(("groups", "batch"), None))
    return jax.shard_map(shards, mesh=mesh, in_specs=in_specs, out_specs=out_specs, check_vma=False)
```

```python
import functools

import jax
import jax.numpy as jnp
from jax import lax
from jax.experimental import pallas as pl
from jax.experimental.pallas import tpu as pltpu
from jax.sharding import PartitionSpec as P

BLOCK = 128
EPSILON = 1e-06

STEP = 1024
PIECE = 4
DEPTH = 512
SLOTS = 6
TILE = 512
EARLY = 5
LANES = 128
VMEM = 32 * 2**20


def encode(values):
    leading = values.shape[:-1]
    blocks = values.reshape(leading + (values.shape[-1] // BLOCK, BLOCK))
    scales = (jnp.max(jnp.abs(blocks), axis=-1) + EPSILON).astype(jnp.bfloat16)
    widened = lax.optimization_barrier(scales).astype(jnp.float32)
    encoded = (blocks / widened[..., None]).astype(jnp.bfloat16)
    return (encoded.reshape(values.shape), scales)


def decode(encoded, scales):
    blocks = encoded.reshape(scales.shape + (BLOCK,)).astype(jnp.float32)
    return (blocks * scales.astype(jnp.float32)[..., None]).reshape(encoded.shape)


def general_shards(gate_input, up_input, down_weight):
    hidden = (jax.nn.silu(gate_input.astype(jnp.float32)) * up_input.astype(jnp.float32)).astype(
        jnp.bfloat16
    )
    partial_value = jnp.dot(
        lax.all_gather(hidden, "batch", axis=0, tiled=True),
        down_weight,
        preferred_element_type=jnp.float32,
    )
    part_codes, part_scales = encode(partial_value)
    tp_count = lax.axis_size("tp")
    batch_count = lax.axis_size("batch")
    row_count = hidden.shape[0]
    local_cols = partial_value.shape[1]
    local_blocks = part_scales.shape[1]
    row_share = row_count // tp_count
    got_codes, got_scales = (
        lax.all_to_all(
            part_codes.reshape(batch_count, tp_count, row_share, local_cols),
            "tp",
            split_axis=1,
            concat_axis=1,
            tiled=True,
        ),
        lax.all_to_all(
            part_scales.reshape(batch_count, tp_count, row_share, local_blocks),
            "tp",
            split_axis=1,
            concat_axis=1,
            tiled=True,
        ),
    )
    summed = jnp.sum(decode(got_codes, got_scales), axis=1)
    new_codes, new_scales = encode(summed)
    home_codes, home_scales = (
        lax.all_to_all(new_codes, "batch", split_axis=0, concat_axis=2, tiled=True),
        lax.all_to_all(new_scales, "batch", split_axis=0, concat_axis=2, tiled=True),
    )
    out_codes, out_scales = (
        lax.all_gather(home_codes, "tp", axis=1, tiled=True),
        lax.all_gather(home_scales, "tp", axis=1, tiled=True),
    )
    return (out_codes.reshape(row_count, -1), out_scales.reshape(row_count, -1))


ANY = pl.BlockSpec(memory_space=pl.ANY)
WEIGHTS = {"activate": 10**10, "multiply": 10**10, "pin": 10**10, "add": 0, "join": 0, "encode": 0}


TOKEN = (8, 128)


def large(value):
    return value.size * value.dtype.itemsize > 3 * 2**20


class Chain:
    def __init__(self):
        self.tokens = []

    def call(self, body, operands, in_specs, out_specs, out_shape, name, grid=(), scratch=(), aliases=None, cost=None):
        count, n_tokens, n_outs = len(operands), len(self.tokens), len(out_shape)

        def with_tokens(*refs):
            outs = count + n_tokens
            body(*refs[:count], *refs[outs : outs + n_outs], *refs[outs + n_outs + 1 :])

        operands = [
            pltpu.with_memory_space_constraint(value, pltpu.HBM) if large(value) else value
            for value in operands
        ]
        outs = pl.pallas_call(
            with_tokens,
            grid=grid,
            in_specs=list(in_specs) + [ANY] * n_tokens,
            out_specs=list(out_specs) + [ANY],
            out_shape=list(out_shape) + [jax.ShapeDtypeStruct(TOKEN, jnp.float32)],
            scratch_shapes=scratch,
            input_output_aliases=aliases or {},
            compiler_params=pltpu.CompilerParams(vmem_limit_bytes=VMEM),
            cost_estimate=pl.CostEstimate(
                flops=WEIGHTS[name] if cost is None else cost, bytes_accessed=1024, transcendentals=0
            ),
            name=name,
        )(*operands, *self.tokens)
        self.tokens = [outs[-1]]
        return list(outs[:-1])

    def pin(self, value, cost=None):
        pinned = self.call(
            lambda *refs: None,
            [value],
            [ANY],
            [ANY],
            [jax.ShapeDtypeStruct(value.shape, value.dtype)],
            "pin",
            aliases={0: 0},
            cost=cost,
        )
        return pinned[0]


def activate(chain, gate, up, first, steps, parts):
    rows = gate.shape[0]

    def body(gate_ref, up_ref, *refs):
        outs, (gates, ups, hidden, in_sems, out_sems) = refs[: len(parts)], refs[len(parts) :]

        def fetch(k, source, target, side):
            at = pl.ds((first + k) * STEP, STEP)
            return pltpu.make_async_copy(source.at[:, at], target.at[k], in_sems.at[side, k])

        for k in range(steps):
            fetch(k, gate_ref, gates, 0).start()
            fetch(k, up_ref, ups, 1).start()
        sent = []
        for k in range(steps):
            fetch(k, gate_ref, gates, 0).wait()
            fetch(k, up_ref, ups, 1).wait()
            value = gates[k].astype(jnp.float32)
            value = value / (1.0 + jnp.exp(-value)) * ups[k].astype(jnp.float32)
            hidden[k] = value.astype(jnp.bfloat16)
            for p, (a, b, s, e) in enumerate(parts):
                if s <= first + k < e:
                    copy = pltpu.make_async_copy(
                        hidden.at[k, pl.ds(a, b - a)],
                        outs[p].at[:, pl.ds((first + k - s) * STEP, STEP)],
                        out_sems.at[p, k],
                    )
                    copy.start()
                    sent.append(copy)
        for copy in sent:
            copy.wait()

    buffer = pltpu.VMEM((steps, rows, STEP), jnp.bfloat16)
    return chain.call(
        body,
        [gate, up],
        [ANY] * 2,
        [ANY] * len(parts),
        [jax.ShapeDtypeStruct((b - a, (e - s) * STEP), jnp.bfloat16) for a, b, s, e in parts],
        "activate",
        scratch=[buffer] * 3
        + [pltpu.SemaphoreType.DMA((2, steps)), pltpu.SemaphoreType.DMA((len(parts), steps))],
    )


def multiply(chain, chunks, weight, first, total, split, cost):
    counts = [piece.shape[0] for piece in chunks[0]]
    rows, cols = sum(counts), weight.shape[1]
    width = sum(pieces[0].shape[1] for pieces in chunks)
    steps, part = width // DEPTH, cols // sum(map(len, split or [(0,)]))
    flat, col = [], 0
    for pieces in chunks:
        row = 0
        for piece in pieces:
            flat.append((piece, row, col))
            row += piece.shape[0]
        col += pieces[0].shape[1]
    n_total = 0 if total is None else 1
    n_in = len(flat) + 1 + n_total
    shapes = [jax.ShapeDtypeStruct((len(flips), rows, part), jnp.bfloat16) for flips in split]
    if not split:
        shapes = [jax.ShapeDtypeStruct((rows, cols), jnp.float32)]

    def body(*refs):
        piece_refs, weight_ref = refs[: len(flat)], refs[len(flat)]
        total_refs, refs = refs[len(flat) + 1 : n_in], refs[n_in:]
        outs, (left, slots, *sums, sems, piece_sems) = refs[: len(shapes)], refs[len(shapes) :]
        sums = sums[0] if sums else outs[0]

        def fetch(k, slot):
            return pltpu.make_async_copy(
                weight_ref.at[pl.ds(first * STEP + k * DEPTH, DEPTH)], slots.at[slot], sems.at[slot]
            )

        for k in range(min(SLOTS, steps)):
            fetch(k, k).start()
        copies = [
            pltpu.make_async_copy(
                ref,
                left.at[pl.ds(row, piece.shape[0]), pl.ds(col, piece.shape[1])],
                piece_sems.at[n],
            )
            for n, (ref, (piece, row, col)) in enumerate(zip(piece_refs, flat))
        ]
        if n_total:
            copies.append(pltpu.make_async_copy(total_refs[0], sums, piece_sems.at[len(flat)]))
        for copy in copies:
            copy.start()
        if not n_total:
            sums[...] = jnp.zeros(sums.shape, sums.dtype)
        for copy in copies:
            copy.wait()

        def step(k, carry):
            slot = lax.rem(k, SLOTS)
            fetch(k, slot).wait()
            piece = left[:, pl.ds(pl.multiple_of(k * DEPTH, DEPTH), DEPTH)]
            for n in range(cols // TILE):
                at = pl.ds(n * TILE, TILE)
                sums[:, at] += jnp.dot(piece, slots[slot, :, at], preferred_element_type=jnp.float32)

            @pl.when(k + SLOTS < steps)
            def _():
                fetch(k + SLOTS, slot).start()

            return carry

        lax.fori_loop(0, steps, step, 0)
        for out, flips in zip(outs, split):
            for n, flip in enumerate(flips):
                at = pl.ds(pl.multiple_of((lax.axis_index("tp") ^ flip) * part, part), part)
                out[n] = sums[:, at].astype(jnp.bfloat16)

    return chain.call(
        body,
        [piece for piece, _, _ in flat] + [weight] + ([total] if n_total else []),
        [ANY] * n_in,
        [pl.BlockSpec(memory_space=pltpu.VMEM)] * len(shapes),
        shapes,
        "multiply",
        cost=cost,
        scratch=[pltpu.VMEM((rows, width), jnp.bfloat16), pltpu.VMEM((SLOTS, DEPTH, cols), jnp.bfloat16)]
        + ([pltpu.VMEM((rows, cols), jnp.float32)] if split else [])
        + [pltpu.SemaphoreType.DMA((SLOTS,)), pltpu.SemaphoreType.DMA((len(flat) + 1,))],
    )


def add(chain, parts, outs, cost=None):
    count = len(parts)

    def body(*refs):
        value = sum(ref[...].astype(jnp.float32) for ref in refs[:count]).astype(jnp.bfloat16)
        for ref, (n, a, b) in zip(refs[count:], outs):
            ref[0] = value[n, a:b]

    vmem = pl.BlockSpec(memory_space=pltpu.VMEM)
    shapes = [jax.ShapeDtypeStruct((1, b - a, parts[0].shape[2]), jnp.bfloat16) for _, a, b in outs]
    return chain.call(body, parts, [vmem] * count, [vmem] * len(outs), shapes, "add", cost=cost)


def join(chain, first, second, cost=None):
    n = first.shape[0]

    def body(first_ref, second_ref, out_ref):
        out_ref[:n] = first_ref[...]
        out_ref[n:] = second_ref[...]

    vmem = pl.BlockSpec(memory_space=pltpu.VMEM)
    shape = jax.ShapeDtypeStruct((n + second.shape[0],) + first.shape[1:], first.dtype)
    return chain.call(body, [first, second], [vmem] * 2, [vmem], [shape], "join", cost=cost)[0]


def encode_blocks(value, store, scales, first):
    lanes = lax.broadcasted_iota(jnp.int32, scales.shape, 1)
    for n in range(value.shape[1] // BLOCK):
        block = value[:, n * BLOCK : (n + 1) * BLOCK].astype(jnp.float32)
        scale = (jnp.max(jnp.abs(block), axis=1, keepdims=True) + EPSILON).astype(jnp.bfloat16)
        scale = scale.astype(jnp.float32)
        store(n, (block / scale).astype(jnp.bfloat16))
        scales = jnp.where(lanes == first + n, scale, scales)
    return scales


def encode_columns(chain, codes, scales, shares, away, start, height, width, last=False, cost=None):
    rows, part = shares[0][0].shape[1:]
    tp = len(shares)
    blocks, spread = part // BLOCK, tp * part
    given = [] if codes is None else [codes, scales]

    def body(*refs):
        share_refs = refs[len(given) : len(given) + tp]
        code_ref, scale_ref, buffer, table, sems = refs[len(given) + tp :]
        table[...] = refs[1][...] if given else jnp.zeros(table.shape, table.dtype)
        total = table[start : start + rows]
        copies = []
        for j in range(2):
            place = lax.axis_index("batch") ^ (j + away)
            for flip, (ref, (_, n)) in enumerate(zip(share_refs, shares)):
                t = lax.axis_index("tp") ^ flip

                def store(m, value):
                    at = pl.ds(pl.multiple_of((t * blocks + m) * BLOCK, BLOCK), BLOCK)
                    buffer[j, :, at] = value

                total = encode_blocks(ref[n + j], store, total, (place * tp + t) * blocks)
            columns = pl.ds(pl.multiple_of(place * spread, spread), spread)
            copy = pltpu.make_async_copy(
                buffer.at[j], code_ref.at[pl.ds(start, rows), columns], sems.at[j]
            )
            copy.start()
            copies.append(copy)
        table[start : start + rows] = total
        if last:
            scale_ref[...] = table[...].T[: width // BLOCK].astype(jnp.bfloat16)
        else:
            scale_ref[...] = table[...]
        for copy in copies:
            copy.wait()

    vmem = pl.BlockSpec(memory_space=pltpu.VMEM)
    kept = jax.ShapeDtypeStruct((height, LANES), jnp.float32)
    return chain.call(
        body,
        given + [array for array, _ in shares],
        [ANY, vmem][: len(given)] + [vmem] * tp,
        [ANY, vmem],
        [
            jax.ShapeDtypeStruct((height, width), jnp.bfloat16),
            jax.ShapeDtypeStruct((width // BLOCK, height), jnp.bfloat16) if last else kept,
        ],
        "encode",
        cost=cost,
        scratch=[
            pltpu.VMEM((2, rows, spread), jnp.bfloat16),
            pltpu.VMEM((height, LANES), jnp.float32),
            pltpu.SemaphoreType.DMA((2,)),
        ],
        aliases={0: 0} if given else {},
    )


DIRECT = [(0,), (1,), (2,), (3,)]
HALVES = [(0, 2), (1, 3)]


def paired_shards(gate_input, up_input, down_weight):
    rows, width = gate_input.shape
    tp, batch = lax.axis_size("tp"), lax.axis_size("batch")
    out_width = down_weight.shape[1] * batch
    cut = rows * EARLY // 8
    steps = width // STEP
    first, middle = steps - 2 * PIECE, steps - PIECE
    half = steps // 2
    chain = Chain()

    def swap(value, flip):
        return lax.ppermute(value, "batch", [(b, b ^ flip) for b in range(batch)]) if flip else value

    def shift(value, flip):
        return lax.ppermute(value, "tp", [(t, t ^ flip) for t in range(tp)])

    def both_cores(piece, cost=None):
        piece = chain.pin(piece, cost)
        return [piece, swap(piece, 1)]

    def product(chunks, first, total, split=(), cost=None):
        outs = multiply(chain, chunks, down_weight, first, total, split, cost)
        return outs if split else outs[0]

    def sum_home(parts, away, cost=None):
        half = parts[0].shape[1] // 2
        ahead, behind = add(chain, parts, [(0, 0, half), (0, half, 2 * half)], cost)
        return swap(ahead, away), swap(behind, away + 1)

    def sum_pair(parts):
        keep, got = parts
        total = add(chain, [keep, got], [(0, 0, keep.shape[1]), (1, 0, keep.shape[1])])
        return [total[0], shift(total[1], 2)]

    near_0, near_1, far_0, far_1, far_2, late_0, late_1 = activate(
        chain,
        gate_input,
        up_input,
        0,
        steps,
        [(0, rows, 0, first), (0, rows, first, steps)]
        + [(0, cut, 0, first), (0, cut, first, middle), (0, cut, middle, steps)]
        + [(cut, rows, 0, half), (cut, rows, half, steps)],
    )
    far_0 = swap(far_0, 2)
    near_0, near_1 = [near_0, swap(near_0, 1)], [near_1, swap(near_1, 1)]

    total = product([near_0], 0, None)
    far_1 = swap(chain.pin(far_1), 2)
    near = product([near_1], first, total, HALVES)
    near = [near[0], shift(near[1], 1)]

    far_0 = both_cores(far_0)
    far_2 = swap(chain.pin(far_2), 2)
    total = product([far_0], 0, None)
    far_1 = both_cores(far_1)
    late_0 = swap(chain.pin(late_0), 2)
    near = sum_pair(near)
    total = product([far_1], first, total)
    far_2 = both_cores(far_2)
    late_1 = swap(chain.pin(late_1), 2)
    far = product([far_2], middle, total, HALVES)
    far = [far[0], shift(far[1], 1)]
    near = sum_home(near, 0)

    late_0 = both_cores(late_0)
    near = join(chain, *near)
    near = [near, shift(near, 2)]
    total = product([late_0], 0, None)
    far = sum_pair(far)
    near.append(join(chain, *near))
    near[2] = shift(near[2], 1)
    late_1 = both_cores(late_1)
    last = product([late_1], half, total, HALVES)
    last = [last[0], shift(last[1], 1)]
    far = sum_home(far, 2, 10**10)
    last = sum_pair(last)
    near = [(near[0], 0), (near[2], 0), (near[1], 0), (near[2], 2)]
    codes, scales = encode_columns(chain, None, None, near, 0, 0, rows, out_width, cost=10**10)
    last = sum_home(last, 2)
    far = join(chain, *far)
    far = [far, shift(far, 2)]
    last = join(chain, *last)
    last = [last] + [shift(last, flip) for flip in range(1, tp)]
    far.append(join(chain, *far))
    far[2] = shift(far[2], 1)
    far = [(far[0], 0), (far[2], 0), (far[1], 0), (far[2], 2)]
    codes, scales = encode_columns(chain, codes, scales, far, 2, 0, rows, out_width)
    last = [(array, 0) for array in last]
    codes, scales = encode_columns(chain, codes, scales, last, 2, cut, rows, out_width, True)
    return codes, scales.T


def solution(mesh):
    def shards(gate_input, up_input, down_weight):
        tp, batch = mesh.shape["tp"], mesh.shape["batch"]
        width, cols = down_weight.shape
        paired = batch == tp == 4 and batch * cols <= LANES * BLOCK and cols % (tp * TILE) == 0 and width % STEP == 0 and width > 2 * PIECE * STEP
        return (paired_shards if paired else general_shards)(gate_input, up_input, down_weight)

    in_specs = (P(("groups", "batch"), "tp"), P(("groups", "batch"), "tp"), P("tp", "batch"))
    out_specs = (P(("groups", "batch"), None), P(("groups", "batch"), None))
    return jax.shard_map(shards, mesh=mesh, in_specs=in_specs, out_specs=out_specs, check_vma=False)
```

```python
import functools

import jax
import jax.numpy as jnp
from jax import lax
from jax.experimental import pallas as pl
from jax.experimental.pallas import tpu as pltpu
from jax.sharding import PartitionSpec as P

BLOCK = 128
EPSILON = 1e-06

STEP = 1024
PIECE = 4
DEPTH = 512
SLOTS = 6
TILE = 512
EARLY = 5
LANES = 128
VMEM = 32 * 2**20


def encode(values):
    leading = values.shape[:-1]
    blocks = values.reshape(leading + (values.shape[-1] // BLOCK, BLOCK))
    scales = (jnp.max(jnp.abs(blocks), axis=-1) + EPSILON).astype(jnp.bfloat16)
    widened = lax.optimization_barrier(scales).astype(jnp.float32)
    encoded = (blocks / widened[..., None]).astype(jnp.bfloat16)
    return (encoded.reshape(values.shape), scales)


def decode(encoded, scales):
    blocks = encoded.reshape(scales.shape + (BLOCK,)).astype(jnp.float32)
    return (blocks * scales.astype(jnp.float32)[..., None]).reshape(encoded.shape)


def general_shards(gate_input, up_input, down_weight):
    hidden = (jax.nn.silu(gate_input.astype(jnp.float32)) * up_input.astype(jnp.float32)).astype(
        jnp.bfloat16
    )
    partial_value = jnp.dot(
        lax.all_gather(hidden, "batch", axis=0, tiled=True),
        down_weight,
        preferred_element_type=jnp.float32,
    )
    part_codes, part_scales = encode(partial_value)
    tp_count = lax.axis_size("tp")
    batch_count = lax.axis_size("batch")
    row_count = hidden.shape[0]
    local_cols = partial_value.shape[1]
    local_blocks = part_scales.shape[1]
    row_share = row_count // tp_count
    got_codes, got_scales = (
        lax.all_to_all(
            part_codes.reshape(batch_count, tp_count, row_share, local_cols),
            "tp",
            split_axis=1,
            concat_axis=1,
            tiled=True,
        ),
        lax.all_to_all(
            part_scales.reshape(batch_count, tp_count, row_share, local_blocks),
            "tp",
            split_axis=1,
            concat_axis=1,
            tiled=True,
        ),
    )
    summed = jnp.sum(decode(got_codes, got_scales), axis=1)
    new_codes, new_scales = encode(summed)
    home_codes, home_scales = (
        lax.all_to_all(new_codes, "batch", split_axis=0, concat_axis=2, tiled=True),
        lax.all_to_all(new_scales, "batch", split_axis=0, concat_axis=2, tiled=True),
    )
    out_codes, out_scales = (
        lax.all_gather(home_codes, "tp", axis=1, tiled=True),
        lax.all_gather(home_scales, "tp", axis=1, tiled=True),
    )
    return (out_codes.reshape(row_count, -1), out_scales.reshape(row_count, -1))


ANY = pl.BlockSpec(memory_space=pl.ANY)
WEIGHTS = {"activate": 10**10, "multiply": 10**10, "pin": 10**10, "add": 0, "join": 0, "encode": 0}


TOKEN = (8, 128)


def large(value):
    return value.size * value.dtype.itemsize > 3 * 2**20


class Chain:
    def __init__(self):
        self.tokens = []

    def call(self, body, operands, in_specs, out_specs, out_shape, name, grid=(), scratch=(), aliases=None, cost=None):
        count, n_tokens, n_outs = len(operands), len(self.tokens), len(out_shape)

        def with_tokens(*refs):
            outs = count + n_tokens
            body(*refs[:count], *refs[outs : outs + n_outs], *refs[outs + n_outs + 1 :])

        operands = [
            pltpu.with_memory_space_constraint(value, pltpu.HBM) if large(value) else value
            for value in operands
        ]
        outs = pl.pallas_call(
            with_tokens,
            grid=grid,
            in_specs=list(in_specs) + [ANY] * n_tokens,
            out_specs=list(out_specs) + [ANY],
            out_shape=list(out_shape) + [jax.ShapeDtypeStruct(TOKEN, jnp.float32)],
            scratch_shapes=scratch,
            input_output_aliases=aliases or {},
            compiler_params=pltpu.CompilerParams(vmem_limit_bytes=VMEM),
            cost_estimate=pl.CostEstimate(
                flops=WEIGHTS[name] if cost is None else cost, bytes_accessed=1024, transcendentals=0
            ),
            name=name,
        )(*operands, *self.tokens)
        self.tokens = [outs[-1]]
        return list(outs[:-1])

    def pin(self, value, cost=None):
        pinned = self.call(
            lambda *refs: None,
            [value],
            [ANY],
            [ANY],
            [jax.ShapeDtypeStruct(value.shape, value.dtype)],
            "pin",
            aliases={0: 0},
            cost=cost,
        )
        return pinned[0]


def activate(chain, gate, up, first, steps, parts):
    rows = gate.shape[0]

    def body(gate_ref, up_ref, *refs):
        outs, (gates, ups, hidden, in_sems, out_sems) = refs[: len(parts)], refs[len(parts) :]

        def fetch(k, source, target, side):
            at = pl.ds((first + k) * STEP, STEP)
            return pltpu.make_async_copy(source.at[:, at], target.at[k], in_sems.at[side, k])

        for k in range(steps):
            fetch(k, gate_ref, gates, 0).start()
            fetch(k, up_ref, ups, 1).start()
        sent = []
        for k in range(steps):
            fetch(k, gate_ref, gates, 0).wait()
            fetch(k, up_ref, ups, 1).wait()
            value = gates[k].astype(jnp.float32)
            value = value / (1.0 + jnp.exp(-value)) * ups[k].astype(jnp.float32)
            hidden[k] = value.astype(jnp.bfloat16)
            for p, (a, b, s, e) in enumerate(parts):
                if s <= first + k < e:
                    copy = pltpu.make_async_copy(
                        hidden.at[k, pl.ds(a, b - a)],
                        outs[p].at[:, pl.ds((first + k - s) * STEP, STEP)],
                        out_sems.at[p, k],
                    )
                    copy.start()
                    sent.append(copy)
        for copy in sent:
            copy.wait()

    buffer = pltpu.VMEM((steps, rows, STEP), jnp.bfloat16)
    return chain.call(
        body,
        [gate, up],
        [ANY] * 2,
        [ANY] * len(parts),
        [jax.ShapeDtypeStruct((b - a, (e - s) * STEP), jnp.bfloat16) for a, b, s, e in parts],
        "activate",
        scratch=[buffer] * 3
        + [pltpu.SemaphoreType.DMA((2, steps)), pltpu.SemaphoreType.DMA((len(parts), steps))],
    )


def multiply(chain, chunks, weight, first, total, split, cost):
    counts = [piece.shape[0] for piece in chunks[0]]
    rows, cols = sum(counts), weight.shape[1]
    width = sum(pieces[0].shape[1] for pieces in chunks)
    steps, part = width // DEPTH, cols // sum(map(len, split or [(0,)]))
    flat, col = [], 0
    for pieces in chunks:
        row = 0
        for piece in pieces:
            flat.append((piece, row, col))
            row += piece.shape[0]
        col += pieces[0].shape[1]
    n_total = 0 if total is None else 1
    n_in = len(flat) + 1 + n_total
    shapes = [jax.ShapeDtypeStruct((len(flips), rows, part), jnp.bfloat16) for flips in split]
    if not split:
        shapes = [jax.ShapeDtypeStruct((rows, cols), jnp.float32)]

    def body(*refs):
        piece_refs, weight_ref = refs[: len(flat)], refs[len(flat)]
        total_refs, refs = refs[len(flat) + 1 : n_in], refs[n_in:]
        outs, (left, slots, *sums, sems, piece_sems) = refs[: len(shapes)], refs[len(shapes) :]
        sums = sums[0] if sums else outs[0]

        def fetch(k, slot):
            return pltpu.make_async_copy(
                weight_ref.at[pl.ds(first * STEP + k * DEPTH, DEPTH)], slots.at[slot], sems.at[slot]
            )

        for k in range(min(SLOTS, steps)):
            fetch(k, k).start()
        copies = [
            pltpu.make_async_copy(
                ref,
                left.at[pl.ds(row, piece.shape[0]), pl.ds(col, piece.shape[1])],
                piece_sems.at[n],
            )
            for n, (ref, (piece, row, col)) in enumerate(zip(piece_refs, flat))
        ]
        if n_total:
            copies.append(pltpu.make_async_copy(total_refs[0], sums, piece_sems.at[len(flat)]))
        for copy in copies:
            copy.start()
        if not n_total:
            sums[...] = jnp.zeros(sums.shape, sums.dtype)
        for copy in copies:
            copy.wait()

        def step(k, carry):
            slot = lax.rem(k, SLOTS)
            fetch(k, slot).wait()
            piece = left[:, pl.ds(pl.multiple_of(k * DEPTH, DEPTH), DEPTH)]
            for n in range(cols // TILE):
                at = pl.ds(n * TILE, TILE)
                sums[:, at] += jnp.dot(piece, slots[slot, :, at], preferred_element_type=jnp.float32)

            @pl.when(k + SLOTS < steps)
            def _():
                fetch(k + SLOTS, slot).start()

            return carry

        lax.fori_loop(0, steps, step, 0)
        for out, flips in zip(outs, split):
            for n, flip in enumerate(flips):
                at = pl.ds(pl.multiple_of((lax.axis_index("tp") ^ flip) * part, part), part)
                out[n] = sums[:, at].astype(jnp.bfloat16)

    return chain.call(
        body,
        [piece for piece, _, _ in flat] + [weight] + ([total] if n_total else []),
        [ANY] * n_in,
        [pl.BlockSpec(memory_space=pltpu.VMEM)] * len(shapes),
        shapes,
        "multiply",
        cost=cost,
        scratch=[pltpu.VMEM((rows, width), jnp.bfloat16), pltpu.VMEM((SLOTS, DEPTH, cols), jnp.bfloat16)]
        + ([pltpu.VMEM((rows, cols), jnp.float32)] if split else [])
        + [pltpu.SemaphoreType.DMA((SLOTS,)), pltpu.SemaphoreType.DMA((len(flat) + 1,))],
    )


def add(chain, parts, outs, cost=None):
    count = len(parts)

    def body(*refs):
        value = sum(ref[...].astype(jnp.float32) for ref in refs[:count]).astype(jnp.bfloat16)
        for ref, (n, a, b) in zip(refs[count:], outs):
            ref[0] = value[n, a:b]

    vmem = pl.BlockSpec(memory_space=pltpu.VMEM)
    shapes = [jax.ShapeDtypeStruct((1, b - a, parts[0].shape[2]), jnp.bfloat16) for _, a, b in outs]
    return chain.call(body, parts, [vmem] * count, [vmem] * len(outs), shapes, "add", cost=cost)


def join(chain, first, second, cost=None):
    n = first.shape[0]

    def body(first_ref, second_ref, out_ref):
        out_ref[:n] = first_ref[...]
        out_ref[n:] = second_ref[...]

    vmem = pl.BlockSpec(memory_space=pltpu.VMEM)
    shape = jax.ShapeDtypeStruct((n + second.shape[0],) + first.shape[1:], first.dtype)
    return chain.call(body, [first, second], [vmem] * 2, [vmem], [shape], "join", cost=cost)[0]


def encode_blocks(value, store, scales, first):
    lanes = lax.broadcasted_iota(jnp.int32, scales.shape, 1)
    for n in range(value.shape[1] // BLOCK):
        block = value[:, n * BLOCK : (n + 1) * BLOCK].astype(jnp.float32)
        scale = (jnp.max(jnp.abs(block), axis=1, keepdims=True) + EPSILON).astype(jnp.bfloat16)
        scale = scale.astype(jnp.float32)
        store(n, (block / scale).astype(jnp.bfloat16))
        scales = jnp.where(lanes == first + n, scale, scales)
    return scales


def encode_columns(chain, codes, scales, shares, away, start, height, width, last=False, cost=None):
    rows, part = shares[0][0].shape[1:]
    tp = len(shares)
    blocks, spread = part // BLOCK, tp * part
    given = [] if codes is None else [codes, scales]

    def body(*refs):
        share_refs = refs[len(given) : len(given) + tp]
        code_ref, scale_ref, buffer, table, sems = refs[len(given) + tp :]
        table[...] = refs[1][...] if given else jnp.zeros(table.shape, table.dtype)
        total = table[start : start + rows]
        copies = []
        for j in range(2):
            place = lax.axis_index("batch") ^ (j + away)
            for flip, (ref, (_, n)) in enumerate(zip(share_refs, shares)):
                t = lax.axis_index("tp") ^ flip

                def store(m, value):
                    at = pl.ds(pl.multiple_of((t * blocks + m) * BLOCK, BLOCK), BLOCK)
                    buffer[j, :, at] = value

                total = encode_blocks(ref[n + j], store, total, (place * tp + t) * blocks)
            columns = pl.ds(pl.multiple_of(place * spread, spread), spread)
            copy = pltpu.make_async_copy(
                buffer.at[j], code_ref.at[pl.ds(start, rows), columns], sems.at[j]
            )
            copy.start()
            copies.append(copy)
        table[start : start + rows] = total
        if last:
            scale_ref[...] = table[...].T[: width // BLOCK].astype(jnp.bfloat16)
        else:
            scale_ref[...] = table[...]
        for copy in copies:
            copy.wait()

    vmem = pl.BlockSpec(memory_space=pltpu.VMEM)
    kept = jax.ShapeDtypeStruct((height, LANES), jnp.float32)
    return chain.call(
        body,
        given + [array for array, _ in shares],
        [ANY, vmem][: len(given)] + [vmem] * tp,
        [ANY, vmem],
        [
            jax.ShapeDtypeStruct((height, width), jnp.bfloat16),
            jax.ShapeDtypeStruct((width // BLOCK, height), jnp.bfloat16) if last else kept,
        ],
        "encode",
        cost=cost,
        scratch=[
            pltpu.VMEM((2, rows, spread), jnp.bfloat16),
            pltpu.VMEM((height, LANES), jnp.float32),
            pltpu.SemaphoreType.DMA((2,)),
        ],
        aliases={0: 0} if given else {},
    )


DIRECT = [(0,), (1,), (2,), (3,)]
HALVES = [(0, 2), (1, 3)]


def paired_shards(gate_input, up_input, down_weight):
    rows, width = gate_input.shape
    tp, batch = lax.axis_size("tp"), lax.axis_size("batch")
    out_width = down_weight.shape[1] * batch
    cut = rows * EARLY // 8
    steps = width // STEP
    first, middle = steps - 2 * PIECE, steps - PIECE
    half = steps - steps // 2
    chain = Chain()

    def swap(value, flip):
        return lax.ppermute(value, "batch", [(b, b ^ flip) for b in range(batch)]) if flip else value

    def shift(value, flip):
        return lax.ppermute(value, "tp", [(t, t ^ flip) for t in range(tp)])

    def both_cores(piece, cost=None):
        piece = chain.pin(piece, cost)
        return [piece, swap(piece, 1)]

    def product(chunks, first, total, split=(), cost=None):
        outs = multiply(chain, chunks, down_weight, first, total, split, cost)
        return outs if split else outs[0]

    def sum_home(parts, away, cost=None):
        half = parts[0].shape[1] // 2
        ahead, behind = add(chain, parts, [(0, 0, half), (0, half, 2 * half)], cost)
        return swap(ahead, away), swap(behind, away + 1)

    def sum_pair(parts):
        keep, got = parts
        total = add(chain, [keep, got], [(0, 0, keep.shape[1]), (1, 0, keep.shape[1])])
        return [total[0], shift(total[1], 2)]

    near_0, near_1, far_0, far_1, far_2, late_0, late_1 = activate(
        chain,
        gate_input,
        up_input,
        0,
        steps,
        [(0, rows, 0, first), (0, rows, first, steps)]
        + [(0, cut, 0, first), (0, cut, first, middle), (0, cut, middle, steps)]
        + [(cut, rows, 0, half), (cut, rows, half, steps)],
    )
    far_0 = swap(far_0, 2)
    near_0, near_1 = [near_0, swap(near_0, 1)], [near_1, swap(near_1, 1)]

    total = product([near_0], 0, None)
    far_1 = swap(chain.pin(far_1), 2)
    near = product([near_1], first, total, HALVES)
    near = [near[0], shift(near[1], 1)]

    far_0 = both_cores(far_0)
    far_2 = swap(chain.pin(far_2), 2)
    total = product([far_0], 0, None)
    far_1 = both_cores(far_1)
    late_0 = swap(chain.pin(late_0), 2)
    near = sum_pair(near)
    total = product([far_1], first, total)
    far_2 = both_cores(far_2)
    late_1 = swap(chain.pin(late_1), 2)
    far = product([far_2], middle, total, HALVES)
    far = [far[0], shift(far[1], 1)]
    near = sum_home(near, 0)

    late_0 = both_cores(late_0)
    near = join(chain, *near)
    near = [near, shift(near, 2)]
    total = product([late_0], 0, None)
    far = sum_pair(far)
    near.append(join(chain, *near))
    near[2] = shift(near[2], 1)
    late_1 = both_cores(late_1)
    last = product([late_1], half, total, HALVES)
    last = [last[0], shift(last[1], 1)]
    far = sum_home(far, 2, 10**10)
    last = sum_pair(last)
    near = [(near[0], 0), (near[2], 0), (near[1], 0), (near[2], 2)]
    codes, scales = encode_columns(chain, None, None, near, 0, 0, rows, out_width, cost=10**10)
    last = sum_home(last, 2)
    far = join(chain, *far)
    far = [far, shift(far, 2)]
    last = join(chain, *last)
    last = [last] + [shift(last, flip) for flip in range(1, tp)]
    far.append(join(chain, *far))
    far[2] = shift(far[2], 1)
    far = [(far[0], 0), (far[2], 0), (far[1], 0), (far[2], 2)]
    codes, scales = encode_columns(chain, codes, scales, far, 2, 0, rows, out_width)
    last = [(array, 0) for array in last]
    codes, scales = encode_columns(chain, codes, scales, last, 2, cut, rows, out_width, True)
    return codes, scales.T


def solution(mesh):
    def shards(gate_input, up_input, down_weight):
        tp, batch = mesh.shape["tp"], mesh.shape["batch"]
        width, cols = down_weight.shape
        paired = batch == tp == 4 and batch * cols <= LANES * BLOCK and cols % (tp * TILE) == 0 and width % STEP == 0 and width > 2 * PIECE * STEP
        return (paired_shards if paired else general_shards)(gate_input, up_input, down_weight)

    in_specs = (P(("groups", "batch"), "tp"), P(("groups", "batch"), "tp"), P("tp", "batch"))
    out_specs = (P(("groups", "batch"), None), P(("groups", "batch"), None))
    return jax.shard_map(shards, mesh=mesh, in_specs=in_specs, out_specs=out_specs, check_vma=False)
```
